32 devices in a mesh: dp: 2 (over core), cp: 8 (over z, x), hd: 2 (over y).
Axes of the slice: x: 2, y: 2, z: 4, core: 2. Of those that a mesh axis runs over, the one named last changes fastest.
Arguments:
- tokens: bfloat16 [2, 5120, 1024], P('dp', ('cp', 'hd')), may hold values from -6 to 6
- doc_ids: int32 [2, 5120], P('dp'), may hold values from 0 to 2, as said below
- cotangent: bfloat16 [2, 5120, 1024], P('dp', ('cp', 'hd')), may hold values from -6 to 6
- w_in: bfloat16 [1024, 4096], P(('dp', 'cp')), may hold values from -0.1875 to 0.1875
- w_dt: bfloat16 [1024, 24], P(('dp', 'cp')), may hold values from -0.1875 to 0.1875
- w_mo: bfloat16 [1536, 1024], P(('dp', 'cp')), may hold values from -0.15625 to 0.15625
- w_ao: bfloat16 [512, 1024], P(('dp', 'cp')), may hold values from -4 to 4
- w_gu: bfloat16 [1024, 4096], P(('dp', 'cp')), may hold values from -0.1875 to 0.1875
- w_down: bfloat16 [2048, 1024], P(('dp', 'cp')), may hold values from -0.125 to 0.125
- norm1: float32 [1024], replicated, may hold values from 0.5 to 1.5
- norm2: float32 [1024], replicated, may hold values from 0.5 to 1.5
- gate_norm: float32 [1536], replicated, may hold values from 0.5 to 1.5
- conv_w: float32 [4, 1792], replicated, may hold values from -3 to 3
- conv_b: float32 [1792], replicated, may hold values from -2 to 2
- dt_bias: float32 [24], replicated, may hold values from -3 to -1
- a_log: float32 [24], replicated
- d_skip: float32 [24], replicated, may hold values from 0.5 to 1.5
Outputs:
- out: bfloat16 [2, 5120, 1024], P('dp', ('cp', 'hd'))
- d_tokens: bfloat16 [2, 5120, 1024], P('dp', ('cp', 'hd'))
- g_w_in: float32 [1024, 4096], P(('dp', 'cp', 'hd'))
- g_w_dt: float32 [1024, 24], P(('dp', 'cp', 'hd'))
- g_w_mo: float32 [1536, 1024], P(('dp', 'cp', 'hd'))
- g_w_ao: float32 [512, 1024], P(('dp', 'cp', 'hd'))
- g_w_gu: float32 [1024, 4096], P(('dp', 'cp', 'hd'))
- g_w_down: float32 [2048, 1024], P(('dp', 'cp', 'hd'))
- g_norm1: float32 [1024], replicated
- g_norm2: float32 [1024], replicated
- g_gate_norm: float32 [1536], replicated
- g_conv_w: float32 [4, 1792], replicated
- g_conv_b: float32 [1792], replicated
- g_dt_bias: float32 [24], replicated
- g_a_log: float32 [24], replicated
- g_d_skip: float32 [24], replicated
The draws below stay inside these ranges and needn't reach their ends.
Inputs may be any that keep to these rules, and one draw needn't show every extreme that they name: `doc_ids`: in each sequence the document numbers are 0, 1, 2 in order and never fall; document 0 ends within the first 640 positions and document 2 begins within the last 640 positions.
All inputs are finite; a program needn't handle non-finite values.
Results may differ from the reference program's by a relative error of at most 0.015.
Values may be sent and summed in bfloat16 or wider, within the bound.
No kernel may reach another device: no remote copies, remote signals or barrier semaphores. Data moves between devices by JAX's collectives and lax.ppermute only.
A program may use at most 256 MiB of HBM per device.

```python
import math
import jax
import jax.numpy as jnp
from jax import lax

D = 1024
HM = 24
HDIM = 64
NST = 128
QH = 8
KVH = 2
FF = 2048
CONV = 4
TOK_DEV = 320
SEQS = 2
STRETCH = 640
LENGTH = 5120
COLS = 4096
CONV_CH = 1792
N_HD = 2


def draw_doc_ids(key, part):
    key = jax.random.fold_in(key, 11)
    early_key, late_key = jax.random.split(key)
    early_cut = jax.random.randint(early_key, (SEQS, 1), 1, STRETCH)
    late_cut = LENGTH - jax.random.randint(late_key, (SEQS, 1), 1, STRETCH)
    positions = jnp.arange(LENGTH, dtype=jnp.int32)[None, :]
    return (positions >= early_cut).astype(jnp.int32) + (positions >= late_cut).astype(jnp.int32)


def draw_a_log(key, part):
    key = jax.random.fold_in(key, 7)
    lowest = math.log(0.5 / LENGTH)
    highest_rate = math.log(1.0 / 30.0)
    log_rate = jax.random.uniform(key, (HM,), jnp.float32, lowest, highest_rate)
    return log_rate - math.log(0.15)


def shard_levels(key, extent, cuts, least, top_value):
    factor_of = 1.0
    for dim, shards_of in cuts:
        heights = jax.random.uniform(jax.random.fold_in(jax.random.fold_in(key, 6), dim), (shards_of,), jnp.float32, least / len(cuts), top_value / len(cuts))
        factor_of = factor_of * jnp.repeat(jnp.exp(heights), extent[dim] // shards_of).reshape((-1,) + (1,) * (len(extent) - 1 - dim))
    return factor_of


def scatter_about(own_key, shape, scale, most, cuts=(), kind=jnp.bfloat16):
    loudness = shard_levels(own_key, shape, cuts, -0.22, 0.18) if cuts else 1.0
    array = jax.random.normal(own_key, shape, jnp.float32) * scale * loudness
    return jnp.minimum(jnp.maximum(array, -most), most).astype(kind)


def setup_inputs(seed: int = 0) -> dict:
    seeds = jax.random.split(jax.random.key(seed), 18)
    tokens = scatter_about(seeds[0], (SEQS, LENGTH, D), 1.0, 6.0, ((0, 2), (1, 16)))
    doc_ids = draw_doc_ids(jax.random.fold_in(seeds[17], 71), 0)
    cotangent = scatter_about(seeds[2], (SEQS, LENGTH, D), 1.0, 6.0, ((0, 2), (1, 16)))
    w_in = scatter_about(seeds[3], (D, COLS), D ** -0.5, 0.1875, ((0, 16),))
    w_dt = scatter_about(seeds[4], (D, HM), D ** -0.5, 0.1875, ((0, 16),))
    w_mo = scatter_about(seeds[5], (HM * HDIM, D), (HM * HDIM) ** -0.5, 0.15625, ((0, 16),))
    w_ao = scatter_about(seeds[6], (QH * HDIM, D), 2 ** -0.5, 4.0, ((0, 16),))
    w_gu = scatter_about(seeds[7], (D, 2 * FF), D ** -0.5, 0.1875, ((0, 16),))
    w_down = scatter_about(seeds[8], (FF, D), FF ** -0.5, 0.125, ((0, 16),))
    norm1 = jnp.clip(1.0 + 0.1 * jax.random.normal(seeds[9], (D,), jnp.float32), 0.5, 1.5)
    norm2 = jnp.clip(1.0 + 0.1 * jax.random.normal(seeds[10], (D,), jnp.float32), 0.5, 1.5)
    gate_norm = jnp.clip(1.0 + 0.1 * jax.random.normal(seeds[11], (HM * HDIM,), jnp.float32), 0.5, 1.5)
    conv_w = scatter_about(seeds[12], (CONV, CONV_CH), 0.5, 3.0, (), jnp.float32)
    conv_b = scatter_about(seeds[13], (CONV_CH,), 0.3, 2.0, (), jnp.float32)
    dt_bias = jnp.clip(jax.random.uniform(seeds[14], (HM,), jnp.float32, -3.0, -1.0), -3.0, -1.0)
    a_log = draw_a_log(jax.random.fold_in(seeds[17], 71), 0)
    d_skip = jnp.clip(jax.random.uniform(seeds[16], (HM,), jnp.float32, 0.5, 1.5), 0.5, 1.5)
    return dict(tokens=tokens, doc_ids=doc_ids, cotangent=cotangent, w_in=w_in, w_dt=w_dt, w_mo=w_mo, w_ao=w_ao, w_gu=w_gu, w_down=w_down, norm1=norm1, norm2=norm2, gate_norm=gate_norm, conv_w=conv_w, conv_b=conv_b, dt_bias=dt_bias, a_log=a_log, d_skip=d_skip)


eps_norm = 1e-05
rope_base = 100000000000.0
masked = -1e+30
highest = lax.Precision.HIGHEST

@jax.custom_vjp
def low(v):
    return lax.optimization_barrier(v.astype(jnp.bfloat16)).astype(jnp.float32)

@jax.custom_vjp
def low_back(v):
    return v

def low_keep(v):
    return (low(v), None)

def low_pass(kept, grad):
    return (grad,)

def back_keep(v):
    return (v, None)

def back_low(kept, grad):
    return (low(grad),)
low.defvjp(low_keep, low_pass)
low_back.defvjp(back_keep, back_low)

def rms_norm(values, gain_vec):
    return values * lax.rsqrt(lax.optimization_barrier(jnp.mean(values * values, axis=-1, keepdims=True)) + eps_norm) * gain_vec

def rotate(values, positions):
    half_width = values.shape[-1] // 2
    frequency = rope_base ** (-2.0 * jnp.arange(half_width, dtype=jnp.float32) / values.shape[-1])
    angles = positions.astype(jnp.float32)[:, None] * frequency[None, :]
    cosines = jnp.cos(angles)[:, None, :]
    sines = jnp.sin(angles)[:, None, :]
    first_half = values[..., :half_width]
    second_half = values[..., half_width:]
    return jnp.concatenate([first_half * cosines - second_half * sines, second_half * cosines + first_half * sines], axis=-1)

def causal_conv(padded, conv_taps, conv_shift):
    tap_count = conv_taps.shape[0]
    out_rows = padded.shape[0] - tap_count + 1
    summed = conv_shift[None, :]
    for tap_index in range(tap_count):
        summed = summed + conv_taps[tap_index][None, :] * padded[tap_index:tap_index + out_rows]
    return summed

def ssd_sequence(x_conv, b_conv, c_conv, dt_value, decay_rate, skip_gain):
    length, head_count, head_width = x_conv.shape
    block_len = math.gcd(256, TOK_DEV * N_HD)
    blocks = length // block_len
    lower_mask = (jnp.arange(block_len)[:, None] >= jnp.arange(block_len)[None, :])[:, :, None]

    def advance(carried, block_item):
        x_block, b_block, c_block, dt_block = block_item
        cum_decay = jnp.cumsum(dt_block * decay_rate[None, :], axis=0)
        spread = jnp.where(lower_mask, cum_decay[:, None, :] - cum_decay[None, :, :], 0.0)
        decays = jnp.where(lower_mask, jnp.exp(spread), 0.0)
        inner_prod = jnp.dot(c_block, b_block.T, precision=highest, preferred_element_type=jnp.float32)
        mixing = decays * inner_prod[:, :, None] * dt_block[None, :, :]
        within = jnp.einsum('tsh,shp->thp', mixing, x_block, precision=highest)
        from_state = jnp.exp(cum_decay)[:, :, None] * jnp.einsum('tn,hpn->thp', c_block, carried, precision=highest)
        end_weight = jnp.exp(cum_decay[-1:, :] - cum_decay) * dt_block
        updated = jnp.exp(cum_decay[-1])[:, None, None] * carried + jnp.einsum('sh,shp,sn->hpn', end_weight, x_block, b_block, precision=highest)
        return (updated, within + from_state + skip_gain[None, :, None] * x_block)
    start_state = jnp.zeros((head_count, head_width, b_conv.shape[1]), jnp.float32)
    pieces = (x_conv.reshape(blocks, block_len, head_count, head_width), b_conv.reshape(blocks, block_len, -1), c_conv.reshape(blocks, block_len, -1), dt_value.reshape(blocks, block_len, head_count))
    _, outputs = lax.scan(jax.checkpoint(advance), start_state, pieces)
    return outputs.reshape(length, head_count, head_width)

def attention_group(queries, keys, values, documents):
    length = keys.shape[0]
    q_heads = queries.shape[1]
    block_len = math.gcd(512, length)
    score_scale = 1.0 / math.sqrt(HDIM)
    positions = jnp.arange(length, dtype=jnp.int32)

    def one_block(block_item):
        rows_in, query_pos, query_docs = block_item
        raw_scores = low_back(jnp.dot(rows_in, keys.T, precision=highest, preferred_element_type=jnp.float32) * score_scale)
        allowed = (positions[None, :] <= query_pos[:, None]) & (documents[None, :] == query_docs[:, None])
        scores = jnp.where(allowed, raw_scores, masked)
        row_top = lax.optimization_barrier(jnp.max(scores, axis=1, keepdims=True))
        weights = jnp.where(allowed, jnp.exp(scores - row_top), 0.0)
        probs = weights / lax.optimization_barrier(jnp.sum(weights, axis=1, keepdims=True))
        return jnp.dot(low(probs), values, precision=highest, preferred_element_type=jnp.float32)
    block_count = length // block_len
    row_blocks = queries.reshape(block_count, block_len * q_heads, HDIM)
    pos_blocks = jnp.repeat(positions, q_heads).reshape(block_count, block_len * q_heads)
    doc_blocks = jnp.repeat(documents, q_heads).reshape(block_count, block_len * q_heads)
    result = lax.map(jax.checkpoint(one_block), (row_blocks, pos_blocks, doc_blocks))
    return result.reshape(length, q_heads * HDIM)

def forward_one(x_seq, documents, norm1, w_in, w_dt, conv_w, conv_b, dt_bias, a_log, d_skip, gate_norm, w_mo, w_ao, norm2, w_gu, w_down):
    length = x_seq.shape[0]
    d_ssm = HM * HDIM
    x_part = d_ssm // KVH
    heads_part = HM // KVH
    q_heads = QH // KVH
    positions = jnp.arange(length, dtype=jnp.int32)
    normed1 = low(rms_norm(x_seq, norm1))
    projected = jnp.dot(normed1, w_in, precision=highest, preferred_element_type=jnp.float32)
    dt_raw = low(low_back(jnp.dot(normed1, w_dt, precision=highest, preferred_element_type=jnp.float32)))
    gate_z = low_back(projected[:, :d_ssm])
    x_stream = low(low_back(projected[:, d_ssm:2 * d_ssm]))
    bc_base = low_back(projected[:, 2 * d_ssm:2 * d_ssm + 2 * NST])
    q_start = 2 * d_ssm + 2 * NST
    k_start = q_start + QH * HDIM
    v_start = k_start + KVH * HDIM
    queries = low(low_back(rotate(low_back(projected[:, q_start:k_start]).reshape(length, QH, HDIM), positions)))
    keys = low(low_back(rotate(low_back(projected[:, k_start:v_start]).reshape(length, KVH, HDIM), positions)))
    values = low(low_back(projected[:, v_start:])).reshape(length, KVH, HDIM)
    mamba_parts = []
    attn_parts = []
    for group_index in range(KVH):
        col_lo = group_index * x_part
        head_lo = group_index * heads_part
        bc_copy = low(low_back(bc_base))
        conv_taps = jnp.concatenate([conv_w[:, col_lo:col_lo + x_part], conv_w[:, d_ssm:]], axis=1)
        conv_shift = jnp.concatenate([conv_b[col_lo:col_lo + x_part], conv_b[d_ssm:]], axis=0)
        stream = jnp.concatenate([x_stream[:, col_lo:col_lo + x_part], bc_copy], axis=1)
        padded = jnp.concatenate([jnp.zeros((conv_taps.shape[0] - 1, stream.shape[1]), jnp.float32), stream], axis=0)
        activated = jax.nn.silu(causal_conv(padded, conv_taps, conv_shift))
        x_conv = activated[:, :x_part].reshape(length, heads_part, HDIM)
        b_conv = activated[:, x_part:x_part + NST]
        c_conv = activated[:, x_part + NST:]
        dt_value = jax.nn.softplus(dt_raw[:, head_lo:head_lo + heads_part] + dt_bias[head_lo:head_lo + heads_part])
        decay_rate = -jnp.exp(a_log[head_lo:head_lo + heads_part])
        y_part = ssd_sequence(x_conv, b_conv, c_conv, dt_value, decay_rate, d_skip[head_lo:head_lo + heads_part])
        mamba_parts.append(low(low_back(y_part.reshape(length, x_part))))
        att_part = attention_group(queries[:, group_index * q_heads:(group_index + 1) * q_heads], keys[:, group_index], values[:, group_index], documents)
        attn_parts.append(low(low_back(att_part)))
    y_all = jnp.concatenate(mamba_parts, axis=1)
    att_all = jnp.concatenate(attn_parts, axis=1)
    gated = low(rms_norm(y_all * jax.nn.silu(gate_z), gate_norm))
    mixed = low_back(jnp.dot(gated, w_mo, precision=highest, preferred_element_type=jnp.float32) + jnp.dot(att_all, w_ao, precision=highest, preferred_element_type=jnp.float32))
    mid = x_seq + mixed
    normed2 = low(rms_norm(mid, norm2))
    gate_up = low_back(jnp.dot(normed2, w_gu, precision=highest, preferred_element_type=jnp.float32))
    hidden = low(jax.nn.silu(gate_up[:, :FF]) * gate_up[:, FF:])
    ffn_out = low_back(jnp.dot(hidden, w_down, precision=highest, preferred_element_type=jnp.float32))
    return mid + ffn_out

def reference(tokens, doc_ids, cotangent, w_in, w_dt, w_mo, w_ao, w_gu, w_down, norm1, norm2, gate_norm, conv_w, conv_b, dt_bias, a_log, d_skip):
    params = (norm1, w_in.astype(jnp.float32), w_dt.astype(jnp.float32), conv_w, conv_b, dt_bias, a_log, d_skip, gate_norm, w_mo.astype(jnp.float32), w_ao.astype(jnp.float32), norm2, w_gu.astype(jnp.float32), w_down.astype(jnp.float32))

    def whole(x_all, *weights):
        return jax.vmap(lambda seq_row, seq_docs: forward_one(seq_row, seq_docs, *weights))(x_all, doc_ids)
    result, pullback = jax.vjp(whole, tokens.astype(jnp.float32), *params)
    grads = pullback(cotangent.astype(jnp.float32))
    g_x, g_norm1, g_w_in, g_w_dt, g_conv_w, g_conv_b, g_dt_bias, g_a_log, g_d_skip, g_gate_norm, g_w_mo, g_w_ao, g_norm2, g_w_gu, g_w_down = grads
    return (result.astype(jnp.bfloat16), g_x.astype(jnp.bfloat16), g_w_in, g_w_dt, g_w_mo, g_w_ao, g_w_gu, g_w_down, g_norm1, g_norm2, g_gate_norm, g_conv_w, g_conv_b, g_dt_bias, g_a_log, g_d_skip)
```

```python
import math

import jax
import jax.numpy as jnp
from jax import lax
from jax.experimental import pallas as pl
from jax.experimental.pallas import tpu as pltpu
from jax.sharding import PartitionSpec as P

HM = 24
HDIM = 64
NST = 128
QH = 8
KVH = 2
FF = 2048

eps_norm = 1e-05
rope_base = 100000000000.0
masked = -1e30
highest = lax.Precision.HIGHEST
low_type = jnp.bfloat16
f32 = jnp.float32
chunk_len = 128
vmem_bytes = 56 * 1024 * 1024


def swap(value, axis, bit):
    count = lax.axis_size(axis)
    return lax.ppermute(value, axis, [(i, i ^ bit) for i in range(count)])


def shifted(value, axis, steps):
    count = lax.axis_size(axis)
    initial, last = (max(0, -steps), min(count, count - steps))
    return lax.ppermute(value, axis, [(source, source + steps) for source in range(initial, last)])


def has_bit(axis, bit):
    return (lax.axis_index(axis) & bit) != 0


def in_order(mine, other, high, dim, join):
    return join([jnp.where(high, other, mine), jnp.where(high, mine, other)], dim)


def gather_cp(value):
    rows, cols = value.shape
    held = value[None]
    bit = lax.axis_size("cp") // 2
    while bit:
        other = swap(held, "cp", bit)
        held = in_order(held, other, has_bit("cp", bit), 1, jnp.stack).reshape(-1, rows, cols)
        bit //= 2
    return held.reshape(-1, cols)


def gather_pair(value, axis, dim):
    return in_order(value, swap(value, axis, 1), has_bit(axis, 1), dim, jnp.concatenate)


def fold(value, axis, bit, dim):
    high = has_bit(axis, bit)
    first = lax.index_in_dim(value, 0, dim, False)
    second = lax.index_in_dim(value, 1, dim, False)
    got = swap(jnp.where(high, first, second).astype(low_type), axis, bit)
    return jnp.where(high, second, first).astype(f32) + got.astype(f32)


def fold_cp(value, order):
    count = lax.axis_size("cp")
    bits = count.bit_length() - 1
    held = value.reshape((2,) * bits + value.shape[1:])
    left = [1 << (bits - 1 - d) for d in range(bits)]
    for bit in order:
        dim = left.index(bit)
        held = fold(held, "cp", bit, dim)
        left.pop(dim)
        if left:
            held = held.astype(low_type)
    return held


def low_first():
    return [1 << d for d in range(lax.axis_size("cp").bit_length() - 1)]


def low_last():
    bits = low_first()
    return bits[1:] + bits[:1]


def after(value, earlier):
    return value + (earlier.reshape(-1)[0].astype(f32) * 0.0).astype(value.dtype)


def state_scan(log_decay, state, forward):
    heads = log_decay.shape[0]
    width = state.shape[1] // heads
    pre_log, pre_state = jnp.zeros_like(log_decay), jnp.zeros_like(state)
    count = lax.axis_size("cp")
    bit = 1

    def spread(values):
        return jnp.repeat(jnp.exp(values), width)[None, :]

    while bit < count:
        top = log_decay.astype(low_type)
        rest = (log_decay - top.astype(f32)).astype(low_type)
        tail = jnp.concatenate([top, rest, jnp.zeros((state.shape[1] - 2 * heads,), low_type)])
        tail = jnp.concatenate([tail[None], jnp.zeros((15, state.shape[1]), low_type)], axis=0)
        got = swap(jnp.concatenate([state.astype(low_type), tail], axis=0), "cp", bit)
        got_state = got[:-16].astype(f32)
        got_log = got[-16, :heads].astype(f32) + got[-16, heads : 2 * heads].astype(f32)
        joins = has_bit("cp", bit) if forward else jnp.logical_not(has_bit("cp", bit))
        pre_state = jnp.where(joins, spread(pre_log) * got_state + pre_state, pre_state)
        pre_log = jnp.where(joins, pre_log + got_log, pre_log)
        state = jnp.where(
            joins, spread(log_decay) * got_state + state, spread(got_log) * state + got_state
        )
        log_decay = log_decay + got_log
        bit *= 2
    return pre_state


def rms_norm(values, gain_vec):
    return (
        values * lax.rsqrt(jnp.mean(values * values, axis=-1, keepdims=True) + eps_norm) * gain_vec
    )


def turn(values, cosines, sines):
    half_width = values.shape[-1] // 2
    first_half = values[..., :half_width]
    second_half = values[..., half_width:]
    return jnp.concatenate(
        [first_half * cosines - second_half * sines, second_half * cosines + first_half * sines],
        axis=-1,
    )


def causal_conv(padded, conv_taps, conv_shift):
    tap_count = conv_taps.shape[0]
    out_rows = padded.shape[0] - tap_count + 1
    summed = conv_shift[None, :]
    for tap_index in range(tap_count):
        summed = summed + conv_taps[tap_index][None, :] * padded[tap_index : tap_index + out_rows]
    return summed


def t_dot(left, right, precision=None):
    return lax.dot_general(
        left,
        right,
        (((0,), (0,)), ((), ())),
        preferred_element_type=f32,
        precision=precision,
    )


def dot_t(left, right, precision=None):
    return lax.dot_general(
        left,
        right,
        (((1,), (1,)), ((), ())),
        preferred_element_type=f32,
        precision=precision,
    )


def dot(left, right, precision=None):
    return jnp.dot(left, right, preferred_element_type=f32, precision=precision)


def att_fwd_kernel(where_ref, q_ref, kv_ref, start_ref, out_ref, lse_ref, top_s, sum_s, acc_s):
    span = q_ref.shape[0]
    place = where_ref[0]
    latest = where_ref[1]
    queries = q_ref[...]
    top_s[...] = jnp.full(top_s.shape, masked, f32)
    sum_s[...] = jnp.zeros(sum_s.shape, f32)
    acc_s[...] = jnp.zeros(acc_s.shape, f32)

    def block(turn_index, _):
        j = place - turn_index
        base = pl.multiple_of(j * span, span)
        keys = kv_ref[pl.ds(base, span), :]
        raw = dot_t(queries, keys)

        def hide(scores):
            key_pos = base + lax.broadcasted_iota(jnp.int32, scores.shape, 1)
            row_pos = place * span + lax.broadcasted_iota(jnp.int32, scores.shape, 0)
            return jnp.where((key_pos <= row_pos) & (key_pos >= start_ref[...]), scores, masked)

        def work(scores):
            old_top = top_s[...]
            new_top = jnp.maximum(old_top, jnp.max(scores, axis=1, keepdims=True))
            weights = jnp.exp(scores - new_top)
            fall = jnp.exp(old_top - new_top)
            sum_s[...] = sum_s[...] * fall + jnp.sum(weights, axis=1, keepdims=True)
            acc_s[...] = acc_s[...] * fall + dot(weights.astype(low_type), keys)
            top_s[...] = new_top

        needs = (j == place) | (latest > base)

        @pl.when(needs)
        def _():
            work(hide(raw))

        @pl.when(jnp.logical_not(needs))
        def _():
            work(raw)

        return 0

    lax.fori_loop(0, place + 1, block, 0)
    out_ref[...] = acc_s[...] / sum_s[...]
    lse_ref[...] = top_s[...] + jnp.log(sum_s[...])


def att_bwd_kernel(
    where_ref, q_ref, do_ref, kv_ref, start_ref, lse_ref, delta_ref, dq_ref, dkv_ref
):
    span = q_ref.shape[0]
    place = where_ref[0]
    latest = where_ref[1]
    queries = q_ref[...]
    grads = do_ref[...]
    dq_ref[...] = jnp.zeros(dq_ref.shape, f32)

    @pl.when(pl.program_id(0) == 0)
    def _():
        dkv_ref[...] = jnp.zeros(dkv_ref.shape, f32)

    def block(j, _):
        base = pl.multiple_of(j * span, span)
        keys = kv_ref[pl.ds(base, span), :]
        raw = dot_t(keys, queries)
        grad_probs = dot_t(keys, grads)

        def hide(scores):
            key_pos = base + lax.broadcasted_iota(jnp.int32, scores.shape, 0)
            row_pos = place * span + lax.broadcasted_iota(jnp.int32, scores.shape, 1)
            return jnp.where((key_pos <= row_pos) & (key_pos >= start_ref[...]), scores, masked)

        def work(scores):
            probs = jnp.exp(scores - lse_ref[...])
            grad_scores = (probs * (grad_probs - delta_ref[...])).astype(low_type)
            dq_ref[...] += t_dot(grad_scores, keys)
            dkv_ref[pl.ds(base, span), :] += dot(grad_scores, queries) + dot(
                probs.astype(low_type), grads
            )

        needs = (j == place) | (latest > base)

        @pl.when(needs)
        def _():
            work(hide(raw))

        @pl.when(jnp.logical_not(needs))
        def _():
            work(raw)

        return 0

    lax.fori_loop(0, place + 1, block, 0)


def whole_spec(shape):
    return pl.BlockSpec(shape, lambda *_: (0,) * len(shape))


def head_spec(*shape):
    return pl.BlockSpec((None,) + shape, lambda i: (i,) + (0,) * len(shape))


def att_cost(span, heads, keys, matmuls):
    return pl.CostEstimate(
        flops=2 * matmuls * span * heads * keys * 256,
        bytes_accessed=4 * keys * 128,
        transcendentals=span * heads * keys,
    )


def attention_forward(where, queries, kv_all, starts):
    heads, span, width = queries.shape
    return pl.pallas_call(
        att_fwd_kernel,
        grid=(heads,),
        in_specs=[
            pl.BlockSpec(memory_space=pltpu.SMEM),
            head_spec(span, width),
            whole_spec(kv_all.shape),
            whole_spec((span, 1)),
        ],
        out_specs=[head_spec(span, width), head_spec(span, 1)],
        out_shape=[
            jax.ShapeDtypeStruct((heads, span, width), f32),
            jax.ShapeDtypeStruct((heads, span, 1), f32),
        ],
        scratch_shapes=[
            pltpu.VMEM((span, 1), f32),
            pltpu.VMEM((span, 1), f32),
            pltpu.VMEM((span, width), f32),
        ],
        compiler_params=pltpu.CompilerParams(vmem_limit_bytes=vmem_bytes),
        cost_estimate=att_cost(span, heads, kv_all.shape[0], 4),
        name="attention_forward",
    )(where, queries, kv_all, starts.reshape(span, 1))


def attention_backward(where, queries, grads, kv_all, starts, lse, delta):
    heads, span, width = queries.shape
    return pl.pallas_call(
        att_bwd_kernel,
        grid=(heads,),
        in_specs=[
            pl.BlockSpec(memory_space=pltpu.SMEM),
            head_spec(span, width),
            head_spec(span, width),
            whole_spec(kv_all.shape),
            whole_spec((1, span)),
            head_spec(1, span),
            head_spec(1, span),
        ],
        out_specs=[head_spec(span, width), whole_spec(kv_all.shape)],
        out_shape=[
            jax.ShapeDtypeStruct((heads, span, width), f32),
            jax.ShapeDtypeStruct(kv_all.shape, f32),
        ],
        compiler_params=pltpu.CompilerParams(vmem_limit_bytes=vmem_bytes),
        cost_estimate=att_cost(span, heads, kv_all.shape[0], 10),
        name="attention_backward",
    )(
        where,
        queries,
        grads,
        kv_all,
        starts.reshape(1, span),
        lse.reshape(heads, 1, span),
        delta.reshape(heads, 1, span),
    )


def pair_blocks(pair):
    left = lax.broadcasted_iota(jnp.int32, pair.shape, 1) < HDIM
    return jnp.where(left, pair, 0.0), jnp.where(left, 0.0, pair)


def ssd_fwd_kernel(xd_ref, b_ref, c_ref, cs_ref, cst_ref, csx_ref, in_ref, y_ref, before_ref, s_s):
    @pl.when(pl.program_id(0) == 0)
    def _():
        s_s[...] = in_ref[...]

    rows = xd_ref.shape[0]
    b, c = b_ref[...], c_ref[...]
    inner = dot_t(c, b, highest)
    lower = lax.broadcasted_iota(jnp.int32, (rows, rows), 0) >= lax.broadcasted_iota(
        jnp.int32, (rows, rows), 1
    )
    state = s_s[...]
    before_ref[...] = state
    csx = csx_ref[...]
    last = csx[rows - 1 :, :]
    carried = jnp.exp(csx) * dot(c, state, highest)

    def mixing(h):
        spread = jnp.where(lower, cs_ref[:, h : h + 1] - cst_ref[h : h + 1, :], masked)
        return jnp.exp(spread) * inner

    for pair in range(xd_ref.shape[1] // (2 * HDIM)):
        cols = slice(pair * 2 * HDIM, (pair + 1) * 2 * HDIM)
        mix = jnp.concatenate([mixing(2 * pair), mixing(2 * pair + 1)], axis=1)
        blocks = jnp.concatenate(pair_blocks(xd_ref[:, cols]), axis=0)
        y_ref[:, cols] = carried[:, cols] + dot(mix, blocks, highest)
    s_s[...] = jnp.exp(last) * state + t_dot(b, jnp.exp(last - csx) * xd_ref[...], highest)


def ssd_bwd_kernel(
    xd_ref,
    dy_ref,
    b_ref,
    c_ref,
    cs_ref,
    cst_ref,
    csx_ref,
    before_ref,
    future_ref,
    dxd_ref,
    db_ref,
    dc_ref,
    ds_s,
):
    @pl.when(pl.program_id(0) == 0)
    def _():
        ds_s[...] = future_ref[...]

    rows = xd_ref.shape[0]
    b, c = b_ref[...], c_ref[...]
    inner_t = dot_t(b, c, highest)
    row_id = lax.broadcasted_iota(jnp.int32, (rows, rows), 0)
    col_id = lax.broadcasted_iota(jnp.int32, (rows, rows), 1)
    csx = csx_ref[...]
    last = csx[rows - 1 :, :]
    grad_state = ds_s[...]
    end_fall = jnp.exp(last - csx)
    from_state = end_fall * dot(b, grad_state, highest)
    scaled_dy = jnp.exp(csx) * dy_ref[...]
    grad_inner = jnp.zeros((rows, rows), f32)

    def falls(h):
        spread = cs_ref[:, h : h + 1] - cst_ref[h : h + 1, :]
        return jnp.exp(jnp.where(row_id >= col_id, spread, masked))

    def falls_t(h):
        spread = cst_ref[h : h + 1, :] - cs_ref[:, h : h + 1]
        return jnp.exp(jnp.where(row_id <= col_id, spread, masked))

    for pair in range(xd_ref.shape[1] // (2 * HDIM)):
        cols = slice(pair * 2 * HDIM, (pair + 1) * 2 * HDIM)
        dy_left, dy_right = pair_blocks(dy_ref[:, cols])
        mix_t = jnp.concatenate(
            [falls_t(2 * pair) * inner_t, falls_t(2 * pair + 1) * inner_t], axis=1
        )
        blocks = jnp.concatenate([dy_left, dy_right], axis=0)
        dxd_ref[:, cols] = from_state[:, cols] + dot(mix_t, blocks, highest)
        xd = xd_ref[:, cols]
        grad_inner = grad_inner + falls(2 * pair) * dot_t(dy_left, xd, highest)
        grad_inner = grad_inner + falls(2 * pair + 1) * dot_t(dy_right, xd, highest)
    dc_ref[...] = dot(grad_inner, b, highest) + dot_t(scaled_dy, before_ref[...], highest)
    db_ref[...] = t_dot(grad_inner, c, highest) + dot_t(
        end_fall * xd_ref[...], grad_state, highest
    )
    ds_s[...] = jnp.exp(last) * grad_state + t_dot(c, scaled_dy, highest)


def ssd_forward(xd, b, c, cs, cst, csx, entering):
    length, width = xd.shape
    blocks = length // chunk_len
    heads = cs.shape[1]

    def rows(w):
        return pl.BlockSpec((chunk_len, w), lambda i: (i, 0))

    return pl.pallas_call(
        ssd_fwd_kernel,
        grid=(blocks,),
        in_specs=[
            rows(width),
            rows(NST),
            rows(NST),
            rows(heads),
            pl.BlockSpec((None, heads, chunk_len), lambda i: (i, 0, 0)),
            rows(width),
            whole_spec((NST, width)),
        ],
        out_specs=[rows(width), pl.BlockSpec((None, NST, width), lambda i: (i, 0, 0))],
        out_shape=[
            jax.ShapeDtypeStruct((length, width), f32),
            jax.ShapeDtypeStruct((blocks, NST, width), f32),
        ],
        scratch_shapes=[pltpu.VMEM((NST, width), f32)],
        compiler_params=pltpu.CompilerParams(vmem_limit_bytes=vmem_bytes),
        cost_estimate=pl.CostEstimate(
            flops=12 * 3 * length * width * NST, bytes_accessed=20 * length * width, transcendentals=0
        ),
        name="ssd_forward",
    )(xd, b, c, cs, cst, csx, entering)


def ssd_backward(xd, dy, b, c, cs, cst, csx, before, future):
    length, width = xd.shape
    blocks = length // chunk_len
    heads = cs.shape[1]

    def rows(w):
        return pl.BlockSpec((chunk_len, w), lambda i: (blocks - 1 - i, 0))

    def slabs(*shape):
        return pl.BlockSpec((None,) + shape, lambda i: (blocks - 1 - i, 0, 0))

    return pl.pallas_call(
        ssd_bwd_kernel,
        grid=(blocks,),
        in_specs=[
            rows(width),
            rows(width),
            rows(NST),
            rows(NST),
            rows(heads),
            slabs(heads, chunk_len),
            rows(width),
            slabs(NST, width),
            whole_spec((NST, width)),
        ],
        out_specs=[rows(width), rows(NST), rows(NST)],
        out_shape=[
            jax.ShapeDtypeStruct((length, width), f32),
            jax.ShapeDtypeStruct((length, NST), f32),
            jax.ShapeDtypeStruct((length, NST), f32),
        ],
        scratch_shapes=[pltpu.VMEM((NST, width), f32)],
        compiler_params=pltpu.CompilerParams(vmem_limit_bytes=vmem_bytes),
        cost_estimate=pl.CostEstimate(
            flops=12 * 8 * length * width * NST, bytes_accessed=24 * length * width, transcendentals=0
        ),
        name="ssd_backward",
    )(xd, dy, b, c, cs, cst, csx, before, future)


def per_device(
    tokens,
    doc_ids,
    cotangent,
    w_in,
    w_dt,
    w_mo,
    w_ao,
    w_gu,
    w_down,
    norm1,
    norm2,
    gate_norm,
    conv_w,
    conv_b,
    dt_bias,
    a_log,
    d_skip,
):
    n_hd = lax.axis_size("hd")
    n_cp = lax.axis_size("cp")
    hd_index = lax.axis_index("hd")
    cp_index = lax.axis_index("cp")
    dp_index = lax.axis_index("dp")
    hd_high = has_bit("hd", 1)
    x_in = tokens[0].astype(f32)
    tok_count, d_model = x_in.shape
    span = tok_count * n_hd
    d_ssm = HM * HDIM
    q_width = QH * HDIM
    k_width = KVH * HDIM
    x_part = d_ssm // n_hd
    heads = HM // n_hd
    q_part = q_width // n_hd
    k_part = k_width // n_hd
    q_heads = QH // n_hd
    bc_width = 2 * NST
    tap_count = conv_w.shape[0]
    score_scale = 1.0 / math.sqrt(HDIM)
    documents = doc_ids[0]

    def group(array, begin, width, dim=1):
        part = width // n_hd
        return lax.dynamic_slice_in_dim(array, begin + hd_index * part, part, dim)

    q_start = 2 * d_ssm + bc_width
    k_start = q_start + q_width
    v_start = k_start + k_width
    dt_pad = 128 - heads
    early = jnp.concatenate(
        [
            group(w_in, d_ssm, d_ssm),
            w_in[:, 2 * d_ssm : q_start],
            group(w_in, q_start, q_width),
            group(w_in, k_start, k_width),
            group(w_in, v_start, k_width),
            group(w_dt, 0, HM),
            jnp.zeros((w_dt.shape[0], dt_pad), low_type),
        ],
        axis=1,
    )
    early_cp = gather_cp(early)
    w_early = gather_pair(early_cp, "dp", 0)
    w_z = gather_pair(gather_cp(after(group(w_in, 0, d_ssm), early_cp)), "dp", 0)

    out_rows = jnp.concatenate([after(w_mo, early_cp), w_ao], axis=0)
    half_cols = d_model // 2
    handed = swap(out_rows[:, half_cols:], "dp", 1)
    holds = dp_index == hd_index
    out_half = jnp.where(holds, out_rows[:, :half_cols], handed)
    out_gathered = gather_cp(out_half)
    out_other = swap(out_gathered, "dp", 1)
    w_out = in_order(out_gathered, out_other, jnp.logical_not(holds), 1, jnp.concatenate)
    mo_rows, ao_rows = w_mo.shape[0], w_ao.shape[0]
    w_out = w_out.reshape(n_cp, mo_rows + ao_rows, d_model)
    w_out = jnp.concatenate(
        [
            w_out[:, :mo_rows].reshape(n_cp * mo_rows, d_model),
            w_out[:, mo_rows:].reshape(n_cp * ao_rows, d_model),
        ],
        axis=0,
    )

    gu_half = gather_cp(after(group(w_gu, 0, 2 * FF), out_gathered))
    w_gate_up = gather_pair(gather_pair(gu_half, "hd", 1), "dp", 0)
    down_half = gather_cp(after(group(w_down, 0, d_model), gu_half))
    w_back = gather_pair(gather_pair(down_half, "hd", 1), "dp", 0)

    tokens_all = gather_pair(tokens[0], "hd", 0)
    normed1_all = rms_norm(tokens_all.astype(f32), norm1).astype(low_type)
    proj = dot(normed1_all, w_early)
    x_bc = proj[:, : x_part + bc_width].astype(low_type)
    at = x_part + bc_width
    qk = proj[:, at : at + q_part + k_part].reshape(span, q_heads + 1, HDIM)
    v_low = proj[:, at + q_part + k_part : at + q_part + 2 * k_part].astype(low_type)
    at = at + q_part + 2 * k_part
    dt_raw = proj[:, at : at + heads].astype(low_type).astype(f32)
    positions = cp_index * span + jnp.arange(span, dtype=jnp.int32)
    half_width = HDIM // 2
    frequency = rope_base ** (-2.0 * jnp.arange(half_width, dtype=f32) / HDIM)
    angles = positions.astype(f32)[:, None] * frequency[None, :]
    cosines = jnp.cos(angles)[:, None, :]
    sines = jnp.sin(angles)[:, None, :]
    qk_rot = turn(qk, cosines, sines).astype(low_type)
    kv_local = jnp.concatenate([qk_rot[:, q_heads], v_low], axis=1)
    kv_all = gather_cp(kv_local)

    rim_rows = shifted(x_bc[span - (tap_count - 1) :], "cp", 1)
    padded = jnp.concatenate([rim_rows, x_bc], axis=0).astype(f32)
    conv_taps = jnp.concatenate([group(conv_w, 0, d_ssm), conv_w[:, d_ssm:]], axis=1)
    conv_shift = jnp.concatenate([group(conv_b, 0, d_ssm, 0), conv_b[d_ssm:]], axis=0)
    dt_shift = group(dt_bias, 0, HM, 0)
    log_scale = group(a_log, 0, HM, 0)
    skip_gain = group(d_skip, 0, HM, 0)
    skip_x = jnp.repeat(skip_gain, HDIM)[None, :]

    def prepare(padded_in, taps_in, shift_in, dt_in, dt_shift_in, log_in):
        activated = jax.nn.silu(causal_conv(padded_in, taps_in, shift_in))
        return (
            activated[:, :x_part],
            activated[:, x_part : x_part + NST],
            activated[:, x_part + NST :],
            jax.nn.softplus(dt_in + dt_shift_in),
            -jnp.exp(log_in),
        )

    (x_conv, b_conv, c_conv, dt_value, decay_rate), prep_pull = jax.vjp(
        prepare, padded, conv_taps, conv_shift, dt_raw, dt_shift, log_scale
    )
    blocks = span // chunk_len
    ones_low = jnp.tril(jnp.ones((chunk_len, chunk_len), f32))
    cs_block = jnp.einsum(
        "ts,bsh->bth",
        ones_low,
        (dt_value * decay_rate[None, :]).reshape(blocks, chunk_len, heads),
        precision=highest,
    )
    block_total = cs_block[:, -1]
    block_base = jnp.concatenate(
        [jnp.zeros((1, heads), f32), jnp.cumsum(block_total, axis=0)], axis=0
    )
    cs_dev = (cs_block + block_base[:-1, None, :]).reshape(span, heads)
    cs = cs_block.reshape(span, heads)
    cst = jnp.swapaxes(cs_block, 1, 2)
    log_dev = block_base[-1]

    def wide(values):
        return jnp.repeat(values, HDIM, axis=1)

    csx = wide(cs)
    csx_dev = wide(cs_dev)
    dtx = wide(dt_value)
    xd = dtx * x_conv
    state_local = t_dot(b_conv, jnp.exp(csx_dev[-1:] - csx_dev) * xd, highest)
    state_in = state_scan(log_dev, state_local, True)

    own_docs = lax.dynamic_slice_in_dim(documents, cp_index * span, span, 0)
    doc_begin = jnp.sum(documents[None, :] < own_docs[:, None], axis=1).astype(jnp.int32)
    where = jnp.stack([cp_index, jnp.max(doc_begin)]).astype(jnp.int32)
    q_scaled = (qk_rot[:, :q_heads] * jnp.asarray(score_scale, low_type)).swapaxes(0, 1)
    q_wide = jnp.concatenate([q_scaled, jnp.zeros_like(q_scaled)], axis=-1)
    att_wide, lse = attention_forward(where, q_wide, kv_all, doc_begin)
    att_f32 = att_wide[:, :, HDIM:]
    att_low = att_f32.swapaxes(0, 1).reshape(span, q_part).astype(low_type)

    y_core, before = ssd_forward(xd, b_conv, c_conv, cs, cst, csx, state_in)
    y_low = (y_core + skip_x * x_conv).astype(low_type).astype(f32)

    gate_z = dot(normed1_all, w_z)
    gain = group(gate_norm, 0, d_ssm, 0)[None, :]
    sig_z = jax.nn.sigmoid(gate_z)
    silu_z = gate_z * sig_z
    mixed_y = y_low * silu_z
    squares = jnp.sum(mixed_y * mixed_y, axis=-1)
    squares = squares + swap(squares, "hd", 1)
    inv = lax.rsqrt(squares / d_ssm + eps_norm)[:, None]
    gated_low = (mixed_y * inv * gain).astype(low_type)
    branches = jnp.concatenate([gated_low, att_low], axis=1)
    partial = dot(branches, w_out).reshape(n_hd, tok_count, d_model)
    x_mid = x_in + fold(partial, "hd", 1, 0)

    normed2, norm2_pull = jax.vjp(rms_norm, x_mid, norm2)
    normed2_low = normed2.astype(low_type)
    gate_up = dot(normed2_low, w_gate_up)

    def swiglu(both_halves):
        return jax.nn.silu(both_halves[:, :FF]) * both_halves[:, FF:]

    hidden, swiglu_pull = jax.vjp(swiglu, gate_up)
    hidden_low = hidden.astype(low_type)
    result_seq = x_mid + dot(hidden_low, w_back)

    grad_out_low = cotangent[0]
    grad_hidden = dot_t(grad_out_low, w_back)
    grad_gate_up = swiglu_pull(grad_hidden)[0].astype(low_type)
    grad_normed2 = dot_t(grad_gate_up, w_gate_up)
    grad_mid_part, g_norm2 = norm2_pull(grad_normed2)
    grad_mid = grad_out_low.astype(f32) + grad_mid_part
    grad_mid_all = gather_pair(grad_mid.astype(low_type), "hd", 0)

    def rows_by_owner(grad):
        rows, cols = grad.shape
        return grad.reshape(2, n_cp, n_hd, rows // (2 * n_cp * n_hd), cols)

    g_down = t_dot(hidden_low, grad_out_low).astype(low_type)
    g_down = fold(rows_by_owner(g_down), "dp", 1, 0).astype(low_type)
    g_down = fold_cp(g_down, low_first()).astype(low_type)
    s_down = fold(g_down, "hd", 1, 0)
    g_gate_up = t_dot(normed2_low, grad_gate_up).astype(low_type)
    g_gate_up = fold(rows_by_owner(g_gate_up), "dp", 1, 0).astype(low_type)
    g_gate_up = fold(g_gate_up, "hd", 1, 1).astype(low_type)
    s_gu = fold_cp(g_gate_up, low_first())

    grad_branches = dot_t(grad_mid_all, w_out)
    grad_gated = grad_branches[:, :x_part]
    grad_att = grad_branches[:, x_part:].reshape(span, q_heads, HDIM).swapaxes(0, 1)
    grad_att = grad_att.astype(low_type)
    delta = jnp.sum(grad_att.astype(f32) * att_f32, axis=-1)
    grad_att_wide = jnp.concatenate([jnp.zeros_like(grad_att), grad_att], axis=-1)

    g_out = t_dot(branches, grad_mid_all).astype(low_type)
    g_out = jnp.concatenate(
        [
            g_out[:x_part].reshape(n_cp, n_hd, mo_rows // n_hd, d_model),
            g_out[x_part:].reshape(n_cp, n_hd, ao_rows // n_hd, d_model),
        ],
        axis=2,
    )
    g_out = fold_cp(fold(g_out, "dp", 1, 1).astype(low_type), low_first())
    s_out = lax.ppermute(g_out, ("dp", "hd"), [(0, 0), (1, 2), (2, 1), (3, 3)])
    s_mo, s_ao = s_out[: mo_rows // n_hd], s_out[mo_rows // n_hd :]

    gain_grad = grad_gated * gain
    along = jnp.sum(gain_grad * mixed_y, axis=-1)
    along = along + swap(along, "hd", 1)
    grad_mixed = inv * gain_grad - mixed_y * (inv * inv * inv * (along / d_ssm)[:, None])
    g_gain = jnp.sum(grad_gated * mixed_y * inv, axis=0)
    grad_y = (grad_mixed * silu_z).astype(low_type).astype(f32)
    grad_z = (grad_mixed * y_low * sig_z * (1.0 + gate_z * (1.0 - sig_z))).astype(low_type)

    scaled_dy = jnp.exp(csx_dev) * grad_y
    future = state_scan(log_dev, t_dot(c_conv, scaled_dy, highest), False)

    dq_wide, dkv = attention_backward(
        where, q_wide, grad_att_wide, kv_all, doc_begin, lse, delta
    )
    dkv = fold_cp(dkv.astype(low_type).reshape(n_cp, span, 2 * HDIM), low_first())
    dq = dq_wide[:, :, :HDIM].swapaxes(0, 1) * score_scale
    dqk = turn(jnp.concatenate([dq, dkv[:, None, :HDIM]], axis=1), cosines, -sines)
    grad_late = jnp.concatenate(
        [grad_z, dqk.reshape(span, q_part + k_part).astype(low_type), dkv[:, HDIM:].astype(low_type)],
        axis=1,
    )

    def reduced(grad):
        grad = t_dot(normed1_all, grad).astype(low_type)
        grad = grad.reshape(2, n_cp, d_model // (2 * n_cp), grad.shape[1])
        grad = fold(grad, "dp", 1, 0).astype(low_type)
        split = (grad.shape[-1] // 256) * 128
        return jnp.concatenate(
            [
                fold_cp(grad[..., :split], low_first()),
                fold_cp(grad[..., split:], low_last()),
            ],
            axis=-1,
        ).astype(low_type)

    r_late = reduced(grad_late)

    dxd, db, dc = ssd_backward(xd, grad_y, b_conv, c_conv, cs, cst, csx, before, future)

    def per_head(values):
        return jnp.sum(values.reshape(span, heads, HDIM), axis=-1)

    ddt_direct = per_head(x_conv * dxd)
    dcs = per_head(grad_y * y_core) - dt_value * ddt_direct
    state_end = jnp.exp(csx_dev[-1:]) * state_in + state_local
    end_term = jnp.sum((future * state_end).sum(axis=0).reshape(heads, HDIM), axis=-1)
    ones_up = jnp.triu(jnp.ones((span, span), f32))
    da = dot(ones_up, dcs, highest) + end_term[None, :]
    g_skip = jnp.sum(per_head(grad_y * x_conv), axis=0)
    grad_padded, grad_taps, grad_shift, grad_dt, grad_dt_shift, grad_log = prep_pull(
        (
            dtx * dxd + skip_x * grad_y,
            db,
            dc,
            ddt_direct + decay_rate[None, :] * da,
            jnp.sum(da * dt_value, axis=0),
        )
    )
    rim_back = shifted(grad_padded[: tap_count - 1], "cp", -1)
    grad_conv_in = jnp.concatenate(
        [
            grad_padded[tap_count - 1 : span],
            grad_padded[span:] + rim_back,
        ],
        axis=0,
    )
    grad_early = jnp.concatenate(
        [
            grad_conv_in.astype(low_type),
            grad_dt.astype(low_type),
            jnp.zeros((span, dt_pad), low_type),
        ],
        axis=1,
    )
    r_early = reduced(grad_early)

    conv_cols = x_part + bc_width
    qkv_cols = q_part + 2 * k_part
    grad_normed1 = (
        dot_t(grad_late[:, :x_part], w_z)
        + dot_t(grad_late[:, x_part:], w_early[:, conv_cols : conv_cols + qkv_cols])
        + dot_t(grad_early[:, :conv_cols], w_early[:, :conv_cols])
        + dot_t(grad_early[:, conv_cols:], w_early[:, conv_cols + qkv_cols :])
    )
    grad_normed1 = fold(grad_normed1.reshape(n_hd, tok_count, d_model), "hd", 1, 0)
    _, norm1_pull = jax.vjp(rms_norm, x_in, norm1)
    grad_x_part, g_norm1 = norm1_pull(grad_normed1)
    grad_tokens_out = (grad_mid + grad_x_part).astype(low_type)

    reduced_in = jnp.concatenate([r_late, r_early], axis=1)
    own_rows = reduced_in.shape[0] // n_hd
    halves = reduced_in.reshape(n_hd, own_rows, reduced_in.shape[1])
    got = swap(jnp.where(hd_high, halves[0], halves[1]), "hd", 1)
    mine = jnp.where(hd_high, halves[1], halves[0])
    group0 = jnp.where(hd_high, got, mine).astype(f32)
    group1 = jnp.where(hd_high, mine, got).astype(f32)

    def both(begin, width):
        return [group0[:, begin : begin + width], group1[:, begin : begin + width]]

    late_cols = x_part + qkv_cols
    bc0, bc1 = both(late_cols + x_part, bc_width)
    s_in = jnp.concatenate(
        both(0, x_part)
        + both(late_cols, x_part)
        + [bc0 + bc1]
        + both(x_part, q_part)
        + both(x_part + q_part, k_part)
        + both(x_part + q_part + k_part, k_part),
        axis=1,
    )
    s_dt = jnp.concatenate(both(late_cols + conv_cols, heads), axis=1)

    def placed(values, width):
        full = jnp.zeros(values.shape[:-1] + (width,), f32)
        return lax.dynamic_update_slice_in_dim(
            full, values, hd_index * values.shape[-1], values.ndim - 1
        )

    g_conv_w = jnp.concatenate([placed(grad_taps[:, :x_part], d_ssm), grad_taps[:, x_part:]], axis=1)
    g_conv_b = jnp.concatenate([placed(grad_shift[:x_part], d_ssm), grad_shift[x_part:]], axis=0)
    small = [
        g_norm1,
        g_norm2,
        placed(g_gain, d_ssm),
        g_conv_w,
        g_conv_b,
        placed(grad_dt_shift, HM),
        placed(grad_log, HM),
        placed(g_skip, HM),
    ]
    flat = jnp.concatenate([s.reshape(-1) for s in small])
    length = flat.shape[0]
    flat = jnp.pad(flat, (0, -length % 1024)).reshape(-1, 128)
    flat = flat + swap(flat, "dp", 1)
    flat = flat + swap(flat, "hd", 1)
    for bit in low_first():
        flat = flat + swap(flat, "cp", bit)
    flat = flat.reshape(-1)
    sums = []
    begin = 0
    for s in small:
        sums.append(flat[begin : begin + s.size].reshape(s.shape))
        begin += s.size
    return (
        result_seq.astype(low_type)[None],
        grad_tokens_out[None],
        s_in,
        s_dt,
        s_mo,
        s_ao,
        s_gu,
        s_down,
        *sums,
    )


def solution(mesh):
    weight = P(("dp", "cp"), None)
    grad = P(("dp", "cp", "hd"), None)
    seq = P("dp", ("cp", "hd"), None)
    in_specs = (seq, P("dp", None), seq) + (weight,) * 6 + (P(),) * 8
    out_specs = (seq, seq) + (grad,) * 6 + (P(),) * 8
    return jax.shard_map(
        per_device, mesh=mesh, in_specs=in_specs, out_specs=out_specs, check_vma=False
    )
```

```python
import math

import jax
import jax.numpy as jnp
from jax import lax
from jax.experimental import pallas as pl
from jax.experimental.pallas import tpu as pltpu
from jax.sharding import PartitionSpec as P

HM = 24
HDIM = 64
NST = 128
QH = 8
KVH = 2
FF = 2048

eps_norm = 1e-05
rope_base = 100000000000.0
masked = -1e30
highest = lax.Precision.HIGHEST
low_type = jnp.bfloat16
f32 = jnp.float32
chunk_len = 128
vmem_bytes = 56 * 1024 * 1024


def swap(value, axis, bit):
    count = lax.axis_size(axis)
    return lax.ppermute(value, axis, [(i, i ^ bit) for i in range(count)])


def shifted(value, axis, steps):
    count = lax.axis_size(axis)
    initial, last = (max(0, -steps), min(count, count - steps))
    return lax.ppermute(value, axis, [(source, source + steps) for source in range(initial, last)])


def has_bit(axis, bit):
    return (lax.axis_index(axis) & bit) != 0


def in_order(mine, other, high, dim, join):
    return join([jnp.where(high, other, mine), jnp.where(high, mine, other)], dim)


def gather_cp(value, gates=()):
    rows, cols = value.shape
    held = value[None]
    steps = []
    bit = lax.axis_size("cp") // 2
    while bit:
        ahead = bit.bit_length() - 1
        if ahead < len(gates) and gates[-1 - ahead] is not None:
            held = after(held, gates[-1 - ahead])
        other = swap(held, "cp", bit)
        held = in_order(held, other, has_bit("cp", bit), 1, jnp.stack).reshape(-1, rows, cols)
        steps.append(held)
        bit //= 2
    return held.reshape(-1, cols), steps


def gather_pair(value, axis, dim):
    return in_order(value, swap(value, axis, 1), has_bit(axis, 1), dim, jnp.concatenate)


def fold(value, axis, bit, dim):
    high = has_bit(axis, bit)
    first = lax.index_in_dim(value, 0, dim, False)
    second = lax.index_in_dim(value, 1, dim, False)
    got = swap(jnp.where(high, first, second).astype(low_type), axis, bit)
    return jnp.where(high, second, first).astype(f32) + got.astype(f32)


def fold_cp(value, order, gates=(None,) * 8):
    count = lax.axis_size("cp")
    bits = count.bit_length() - 1
    held = value.reshape((2,) * bits + value.shape[1:])
    left = [1 << (bits - 1 - d) for d in range(bits)]
    steps = []
    for gate, bit in zip(gates, order):
        dim = left.index(bit)
        if gate is not None:
            held = after(held, gate)
        held = fold(held, "cp", bit, dim)
        left.pop(dim)
        if left:
            held = held.astype(low_type)
        steps.append(held)
    return held, steps


def low_first():
    return [1 << d for d in range(lax.axis_size("cp").bit_length() - 1)]


def low_last():
    bits = low_first()
    return bits[1:] + bits[:1]


def after(value, earlier):
    first = lax.slice(earlier, (0,) * earlier.ndim, (1,) * earlier.ndim).reshape(())
    return value + (first.astype(f32) * 0.0).astype(value.dtype)


def state_scan(log_decay, state, forward):
    heads = log_decay.shape[0]
    width = state.shape[1] // heads
    pre_log, pre_state = jnp.zeros_like(log_decay), jnp.zeros_like(state)
    count = lax.axis_size("cp")
    bit = 1

    def spread(values):
        return dot(jnp.exp(values)[None, :], expander(heads, width), highest)

    while bit < count:
        top = log_decay.astype(low_type)
        rest = (log_decay - top.astype(f32)).astype(low_type)
        tail = jnp.concatenate([top, rest, jnp.zeros((state.shape[1] - 2 * heads,), low_type)])
        tail = jnp.concatenate([tail[None], jnp.zeros((15, state.shape[1]), low_type)], axis=0)
        sent = jnp.concatenate([state.astype(low_type), tail], axis=0)
        gate = yield sent
        if gate is not None:
            sent = after(sent, gate)
        got = swap(sent, "cp", bit)
        got_state = got[:-16].astype(f32)
        got_log = got[-16, :heads].astype(f32) + got[-16, heads : 2 * heads].astype(f32)
        joins = has_bit("cp", bit) if forward else jnp.logical_not(has_bit("cp", bit))
        pre_state = jnp.where(joins, spread(pre_log) * got_state + pre_state, pre_state)
        pre_log = jnp.where(joins, pre_log + got_log, pre_log)
        state = jnp.where(
            joins, spread(log_decay) * got_state + state, spread(got_log) * state + got_state
        )
        log_decay = log_decay + got_log
        bit *= 2
    yield pre_state


def rms_norm(values, gain_vec):
    return (
        values * lax.rsqrt(jnp.mean(values * values, axis=-1, keepdims=True) + eps_norm) * gain_vec
    )


def expander(heads, width):
    column = jnp.arange(heads * width, dtype=jnp.int32)[None, :] // width
    return (column == jnp.arange(heads, dtype=jnp.int32)[:, None]).astype(f32)


def half_turner(width):
    column = jnp.arange(width, dtype=jnp.int32)
    half = HDIM // 2
    partner = jnp.where(column % HDIM < half, column + half, column - half)
    return (column[:, None] == partner[None, :]).astype(f32)


def causal_conv(padded, conv_taps, conv_shift):
    tap_count = conv_taps.shape[0]
    out_rows = padded.shape[0] - tap_count + 1
    summed = conv_shift[None, :]
    for tap_index in range(tap_count):
        summed = summed + conv_taps[tap_index][None, :] * padded[tap_index : tap_index + out_rows]
    return summed


def t_dot(left, right, precision=None):
    return lax.dot_general(
        left,
        right,
        (((0,), (0,)), ((), ())),
        preferred_element_type=f32,
        precision=precision,
    )


def dot_t(left, right, precision=None):
    return lax.dot_general(
        left,
        right,
        (((1,), (1,)), ((), ())),
        preferred_element_type=f32,
        precision=precision,
    )


def dot(left, right, precision=None):
    return jnp.dot(left, right, preferred_element_type=f32, precision=precision)


def left_half(shape):
    return lax.broadcasted_iota(jnp.int32, shape, 1) < HDIM


def both_heads(pair):
    left = left_half(pair.shape)
    pair = pair.astype(f32)
    return (
        jnp.where(left, pair, 0.0).astype(low_type),
        jnp.where(left, 0.0, pair).astype(low_type),
    )


def att_fwd_kernel(where_ref, q_ref, kk_ref, vv_ref, start_ref, *rest):
    out_ref, lse_ref, top_s, sum_s, acc_s = rest[-5:]
    span = q_ref.shape[0]
    place = where_ref[0]
    latest = where_ref[1]
    queries = both_heads(q_ref[...])
    top_s[...] = jnp.full(top_s.shape, masked, f32)
    sum_s[...] = jnp.zeros(sum_s.shape, f32)
    acc_s[...] = jnp.zeros(acc_s.shape, f32)

    def block(turn_index, _):
        j = place - turn_index
        base = pl.multiple_of(j * span, span)
        keys = kk_ref[pl.ds(base, span), :]
        values = vv_ref[pl.ds(base, span), :]

        def hide(scores):
            key_pos = base + lax.broadcasted_iota(jnp.int32, scores.shape, 1)
            row_pos = place * span + lax.broadcasted_iota(jnp.int32, scores.shape, 0)
            return jnp.where((key_pos <= row_pos) & (key_pos >= start_ref[...]), scores, masked)

        def work(shape_scores):
            for e in range(2):
                scores = shape_scores(dot_t(queries[e], keys))
                old_top = top_s[e]
                new_top = jnp.maximum(old_top, jnp.max(scores, axis=1, keepdims=True))
                weights = jnp.exp(scores - new_top)
                fall = jnp.exp(old_top - new_top)
                sum_s[e] = sum_s[e] * fall + jnp.sum(weights, axis=1, keepdims=True)
                acc_s[e] = acc_s[e] * fall + dot(weights.astype(low_type), values)
                top_s[e] = new_top

        needs = (j == place) | (latest > base)

        @pl.when(needs)
        def _():
            work(hide)

        @pl.when(jnp.logical_not(needs))
        def _():
            work(lambda scores: scores)

        return 0

    lax.fori_loop(0, place + 1, block, 0)
    outs = [acc_s[e] / sum_s[e] for e in range(2)]
    out_ref[...] = jnp.where(left_half(outs[0].shape), outs[0], outs[1])
    for e in range(2):
        lse_ref[e] = top_s[e] + jnp.log(sum_s[e])


def att_bwd_kernel(
    where_ref, q_ref, do_ref, kk_ref, vv_ref, start_ref, lse_ref, delta_ref, *rest
):
    dq_ref, dkv_ref, dq_s = rest[-3:]
    span = q_ref.shape[0]
    place = where_ref[0]
    latest = where_ref[1]
    queries = both_heads(q_ref[...])
    grads = both_heads(do_ref[...])
    dq_s[...] = jnp.zeros(dq_s.shape, f32)

    def block(j, _):
        base = pl.multiple_of(j * span, span)
        keys = kk_ref[pl.ds(base, span), :]
        values = vv_ref[pl.ds(base, span), :]

        def hide(scores):
            key_pos = base + lax.broadcasted_iota(jnp.int32, scores.shape, 0)
            row_pos = place * span + lax.broadcasted_iota(jnp.int32, scores.shape, 1)
            return jnp.where((key_pos <= row_pos) & (key_pos >= start_ref[...]), scores, masked)

        def work(shape_scores):
            dkk, dvv = [], []
            for e in range(2):
                scores = shape_scores(dot_t(keys, queries[e]))
                grad_probs = dot_t(values, grads[e])
                probs = jnp.exp(scores - lse_ref[e])
                grad_scores = (probs * (grad_probs - delta_ref[e])).astype(low_type)
                dq_s[e] += t_dot(grad_scores, keys)
                dkk.append(dot(grad_scores, queries[e]))
                dvv.append(dot(probs.astype(low_type), grads[e]))
            dkk, dvv = dkk[0] + dkk[1], dvv[0] + dvv[1]
            dkk = dkk + pltpu.roll(dkk, HDIM, 1)
            dvv = dvv + pltpu.roll(dvv, HDIM, 1)
            dkv_ref[pl.ds(base, span), :] = jnp.where(left_half(dkk.shape), dkk, dvv).astype(
                low_type
            )

        needs = (j == place) | (latest > base)

        @pl.when(needs)
        def _():
            work(hide)

        @pl.when(jnp.logical_not(needs))
        def _():
            work(lambda scores: scores)

        return 0

    lax.fori_loop(0, place + 1, block, 0)

    def clear(j, _):
        base = pl.multiple_of(j * span, span)
        dkv_ref[pl.ds(base, span), :] = jnp.zeros((span, 2 * HDIM), low_type)
        return 0

    lax.fori_loop(place + 1, dkv_ref.shape[0] // span, clear, 0)
    dq_ref[...] = jnp.where(left_half(dq_ref.shape), dq_s[0], dq_s[1])


def whole_spec(shape):
    return pl.BlockSpec(shape, lambda *_: (0,) * len(shape))


def any_specs(count):
    return [pl.BlockSpec(memory_space=pl.ANY)] * count


def att_cost(span, keys, matmuls):
    return pl.CostEstimate(
        flops=2 * matmuls * span * 2 * keys * 256,
        bytes_accessed=4 * keys * 128,
        transcendentals=span * 2 * keys,
    )


def attention_forward(where, queries, kk, vv, starts, deps):
    span, width = queries.shape
    return pl.pallas_call(
        att_fwd_kernel,
        in_specs=[
            pl.BlockSpec(memory_space=pltpu.SMEM),
            whole_spec((span, width)),
            whole_spec(kk.shape),
            whole_spec(vv.shape),
            whole_spec((span, 1)),
        ]
        + any_specs(len(deps)),
        out_specs=[whole_spec((span, width)), whole_spec((2, span, 1))],
        out_shape=[
            jax.ShapeDtypeStruct((span, width), f32),
            jax.ShapeDtypeStruct((2, span, 1), f32),
        ],
        grid=(1,),
        scratch_shapes=[
            pltpu.VMEM((2, span, 1), f32),
            pltpu.VMEM((2, span, 1), f32),
            pltpu.VMEM((2, span, width), f32),
        ],
        compiler_params=pltpu.CompilerParams(vmem_limit_bytes=vmem_bytes),
        cost_estimate=att_cost(span, kk.shape[0], 4),
        name="attention_forward",
    )(where, queries, kk, vv, starts.reshape(span, 1), *deps)


def attention_backward(where, queries, grads, kk, vv, starts, lse, delta, deps):
    span, width = queries.shape
    return pl.pallas_call(
        att_bwd_kernel,
        in_specs=[
            pl.BlockSpec(memory_space=pltpu.SMEM),
            whole_spec((span, width)),
            whole_spec((span, width)),
            whole_spec(kk.shape),
            whole_spec(vv.shape),
            whole_spec((1, span)),
            whole_spec((2, 1, span)),
            whole_spec((2, 1, span)),
        ]
        + any_specs(len(deps)),
        out_specs=[whole_spec((span, width)), whole_spec(kk.shape)],
        out_shape=[
            jax.ShapeDtypeStruct((span, width), f32),
            jax.ShapeDtypeStruct(kk.shape, low_type),
        ],
        grid=(1,),
        scratch_shapes=[
            pltpu.VMEM((2, span, width), f32),
        ],
        compiler_params=pltpu.CompilerParams(vmem_limit_bytes=vmem_bytes),
        cost_estimate=att_cost(span, kk.shape[0], 10),
        name="attention_backward",
    )(
        where,
        queries,
        grads,
        kk,
        vv,
        starts.reshape(1, span),
        lse.reshape(2, 1, span),
        delta.reshape(2, 1, span),
        *deps,
    )


def pair_blocks(pair):
    left = lax.broadcasted_iota(jnp.int32, pair.shape, 1) < HDIM
    return jnp.where(left, pair, 0.0), jnp.where(left, 0.0, pair)


def ssd_fwd_kernel(xd_ref, b_ref, c_ref, cs_ref, cst_ref, csx_ref, in_ref, *rest):
    y_ref, before_ref, s_s = rest[-3:]

    @pl.when(pl.program_id(0) == 0)
    def _():
        s_s[...] = in_ref[...]

    rows = xd_ref.shape[0]
    b, c = b_ref[...], c_ref[...]
    inner = dot_t(c, b, highest)
    lower = lax.broadcasted_iota(jnp.int32, (rows, rows), 0) >= lax.broadcasted_iota(
        jnp.int32, (rows, rows), 1
    )
    state = s_s[...]
    before_ref[...] = state
    csx = csx_ref[...]
    last = csx[rows - 1 :, :]
    carried = jnp.exp(csx) * dot(c, state, highest)

    def mixing(h):
        spread = jnp.where(lower, cs_ref[:, h : h + 1] - cst_ref[h : h + 1, :], masked)
        return jnp.exp(spread) * inner

    for pair in range(xd_ref.shape[1] // (2 * HDIM)):
        cols = slice(pair * 2 * HDIM, (pair + 1) * 2 * HDIM)
        mix = jnp.concatenate([mixing(2 * pair), mixing(2 * pair + 1)], axis=1)
        blocks = jnp.concatenate(pair_blocks(xd_ref[:, cols]), axis=0)
        y_ref[:, cols] = carried[:, cols] + dot(mix, blocks, highest)
    s_s[...] = jnp.exp(last) * state + t_dot(b, jnp.exp(last - csx) * xd_ref[...], highest)


def ssd_bwd_kernel(
    xd_ref,
    dy_ref,
    b_ref,
    c_ref,
    cs_ref,
    cst_ref,
    csx_ref,
    before_ref,
    future_ref,
    *rest,
):
    dxd_ref, db_ref, dc_ref, ds_s = rest[-4:]

    @pl.when(pl.program_id(0) == 0)
    def _():
        ds_s[...] = future_ref[...]

    rows = xd_ref.shape[0]
    b, c = b_ref[...], c_ref[...]
    inner_t = dot_t(b, c, highest)
    row_id = lax.broadcasted_iota(jnp.int32, (rows, rows), 0)
    col_id = lax.broadcasted_iota(jnp.int32, (rows, rows), 1)
    csx = csx_ref[...]
    last = csx[rows - 1 :, :]
    grad_state = ds_s[...]
    end_fall = jnp.exp(last - csx)
    from_state = end_fall * dot(b, grad_state, highest)
    scaled_dy = jnp.exp(csx) * dy_ref[...]
    grad_inner = jnp.zeros((rows, rows), f32)

    def falls(h):
        spread = cs_ref[:, h : h + 1] - cst_ref[h : h + 1, :]
        return jnp.exp(jnp.where(row_id >= col_id, spread, masked))

    def falls_t(h):
        spread = cst_ref[h : h + 1, :] - cs_ref[:, h : h + 1]
        return jnp.exp(jnp.where(row_id <= col_id, spread, masked))

    for pair in range(xd_ref.shape[1] // (2 * HDIM)):
        cols = slice(pair * 2 * HDIM, (pair + 1) * 2 * HDIM)
        dy_left, dy_right = pair_blocks(dy_ref[:, cols])
        mix_t = jnp.concatenate(
            [falls_t(2 * pair) * inner_t, falls_t(2 * pair + 1) * inner_t], axis=1
        )
        blocks = jnp.concatenate([dy_left, dy_right], axis=0)
        dxd_ref[:, cols] = from_state[:, cols] + dot(mix_t, blocks, highest)
        xd = xd_ref[:, cols]
        grad_inner = grad_inner + falls(2 * pair) * dot_t(dy_left, xd, highest)
        grad_inner = grad_inner + falls(2 * pair + 1) * dot_t(dy_right, xd, highest)
    dc_ref[...] = dot(grad_inner, b, highest) + dot_t(scaled_dy, before_ref[...], highest)
    db_ref[...] = t_dot(grad_inner, c, highest) + dot_t(
        end_fall * xd_ref[...], grad_state, highest
    )
    ds_s[...] = jnp.exp(last) * grad_state + t_dot(c, scaled_dy, highest)


def ssd_forward(xd, b, c, cs, cst, csx, entering, deps):
    length, width = xd.shape
    blocks = length // chunk_len
    heads = cs.shape[1]

    def rows(w):
        return pl.BlockSpec((chunk_len, w), lambda i: (i, 0))

    return pl.pallas_call(
        ssd_fwd_kernel,
        grid=(blocks,),
        in_specs=[
            rows(width),
            rows(NST),
            rows(NST),
            rows(heads),
            pl.BlockSpec((None, heads, chunk_len), lambda i: (i, 0, 0)),
            rows(width),
            whole_spec((NST, width)),
        ]
        + any_specs(len(deps)),
        out_specs=[rows(width), pl.BlockSpec((None, NST, width), lambda i: (i, 0, 0))],
        out_shape=[
            jax.ShapeDtypeStruct((length, width), f32),
            jax.ShapeDtypeStruct((blocks, NST, width), f32),
        ],
        scratch_shapes=[pltpu.VMEM((NST, width), f32)],
        compiler_params=pltpu.CompilerParams(vmem_limit_bytes=vmem_bytes),
        cost_estimate=pl.CostEstimate(
            flops=12 * 3 * length * width * NST, bytes_accessed=20 * length * width, transcendentals=0
        ),
        name="ssd_forward",
    )(xd, b, c, cs, cst, csx, entering, *deps)


def ssd_backward(xd, dy, b, c, cs, cst, csx, before, future, deps):
    length, width = xd.shape
    blocks = length // chunk_len
    heads = cs.shape[1]

    def rows(w):
        return pl.BlockSpec((chunk_len, w), lambda i: (blocks - 1 - i, 0))

    def slabs(*shape):
        return pl.BlockSpec((None,) + shape, lambda i: (blocks - 1 - i, 0, 0))

    return pl.pallas_call(
        ssd_bwd_kernel,
        grid=(blocks,),
        in_specs=[
            rows(width),
            rows(width),
            rows(NST),
            rows(NST),
            rows(heads),
            slabs(heads, chunk_len),
            rows(width),
            slabs(NST, width),
            whole_spec((NST, width)),
        ]
        + any_specs(len(deps)),
        out_specs=[rows(width), rows(NST), rows(NST)],
        out_shape=[
            jax.ShapeDtypeStruct((length, width), f32),
            jax.ShapeDtypeStruct((length, NST), f32),
            jax.ShapeDtypeStruct((length, NST), f32),
        ],
        scratch_shapes=[pltpu.VMEM((NST, width), f32)],
        compiler_params=pltpu.CompilerParams(vmem_limit_bytes=vmem_bytes),
        cost_estimate=pl.CostEstimate(
            flops=12 * 8 * length * width * NST, bytes_accessed=24 * length * width, transcendentals=0
        ),
        name="ssd_backward",
    )(xd, dy, b, c, cs, cst, csx, before, future, *deps)


def per_device(
    tokens,
    doc_ids,
    cotangent,
    w_in,
    w_dt,
    w_mo,
    w_ao,
    w_gu,
    w_down,
    norm1,
    norm2,
    gate_norm,
    conv_w,
    conv_b,
    dt_bias,
    a_log,
    d_skip,
):
    n_hd = lax.axis_size("hd")
    n_cp = lax.axis_size("cp")
    hd_index = lax.axis_index("hd")
    cp_index = lax.axis_index("cp")
    dp_index = lax.axis_index("dp")
    hd_high = has_bit("hd", 1)
    x_in = tokens[0].astype(f32)
    tok_count, d_model = x_in.shape
    span = tok_count * n_hd
    d_ssm = HM * HDIM
    q_width = QH * HDIM
    k_width = KVH * HDIM
    x_part = d_ssm // n_hd
    heads = HM // n_hd
    q_part = q_width // n_hd
    k_part = k_width // n_hd
    bc_width = 2 * NST
    qkv_cols = q_part + 2 * k_part
    tap_count = conv_w.shape[0]
    score_scale = 1.0 / math.sqrt(HDIM)
    documents = doc_ids[0]

    def group(array, begin, width, dim=1):
        part = width // n_hd
        return lax.dynamic_slice_in_dim(array, begin + hd_index * part, part, dim)

    tokens_all = gather_pair(tokens[0], "hd", 0)

    normed1_all = rms_norm(tokens_all.astype(f32), norm1).astype(low_type)
    rim_tokens = shifted(tokens_all[span - 16 :], "cp", 1)
    normed1_rim = rms_norm(rim_tokens.astype(f32), norm1).astype(low_type)

    own_docs = lax.dynamic_slice_in_dim(documents, cp_index * span, span, 0)
    doc_begin = jnp.sum(documents[None, :] < own_docs[:, None], axis=1).astype(jnp.int32)
    where = jnp.stack([cp_index, jnp.max(doc_begin)]).astype(jnp.int32)

    positions = cp_index * span + jnp.arange(span, dtype=jnp.int32)
    half_width = HDIM // 2
    column = jnp.arange(qkv_cols, dtype=jnp.int32)
    turns = column < q_part + k_part
    power = (column % half_width).astype(f32)
    frequency = jnp.where(turns, rope_base ** (-2.0 * power / HDIM), 0.0)
    sign = jnp.where(column % HDIM < half_width, -1.0, 1.0)
    angles = positions.astype(f32)[:, None] * frequency[None, :]
    cosines = jnp.cos(angles)
    sines = jnp.sin(angles) * sign[None, :]
    cosines, sines = lax.optimization_barrier((cosines, sines))
    turner = half_turner(qkv_cols).astype(low_type)

    def half_turn(values):
        top = values.astype(low_type)
        return dot(top, turner) + dot((values - top.astype(f32)).astype(low_type), turner)

    q_start = 2 * d_ssm + bc_width
    k_start = q_start + q_width
    v_start = k_start + k_width
    dt_pad = 128 - heads
    shard_misc = jnp.concatenate(
        [
            group(w_in, q_start, q_width),
            group(w_in, k_start, k_width),
            group(w_in, v_start, k_width),
            w_in[:, 2 * d_ssm : q_start],
            group(w_dt, 0, HM),
            jnp.zeros((w_dt.shape[0], dt_pad), low_type),
        ],
        axis=1,
    )
    misc_cp, _ = gather_cp(shard_misc, (where, normed1_all))
    w_misc = gather_pair(after(after(misc_cp, cosines), normed1_rim), "dp", 0)
    xs_cp, xs_steps = gather_cp(after(group(w_in, d_ssm, d_ssm), w_misc))
    out_rows = jnp.concatenate([w_mo, w_ao], axis=0)
    half_cols = d_model // 2
    handed = swap(out_rows[:, half_cols:], "dp", 1)
    holds = dp_index == hd_index
    out_half = jnp.where(holds, out_rows[:, :half_cols], handed)
    w_back = lax.all_gather(w_down, ("dp", "cp"), axis=0, tiled=True)
    w_xs = gather_pair(after(xs_cp, w_back), "dp", 0)

    proj = dot(normed1_all, w_misc)
    qkv = proj[:, :qkv_cols]
    qkv_low = (qkv * cosines + half_turn(qkv) * sines).astype(low_type)
    kv_all, _ = gather_cp(qkv_low[:, q_part:], (xs_steps[0], xs_steps[1]))
    q_scaled = qkv_low[:, :q_part] * jnp.asarray(score_scale, low_type)
    bc = proj[:, qkv_cols : qkv_cols + bc_width].astype(low_type)
    at = qkv_cols + bc_width
    dt_raw = proj[:, at : at + heads].astype(low_type).astype(f32)
    x_bc = jnp.concatenate([dot(normed1_all, w_xs).astype(low_type), bc], axis=1)
    w_bc = w_misc[:, qkv_cols : qkv_cols + bc_width]
    rim_rows = jnp.concatenate([dot(normed1_rim, w_xs), dot(normed1_rim, w_bc)], axis=1)
    rim_rows = rim_rows.astype(low_type)[16 - (tap_count - 1) :]

    padded = jnp.concatenate([rim_rows, x_bc], axis=0).astype(f32)
    conv_taps = jnp.concatenate([group(conv_w, 0, d_ssm), conv_w[:, d_ssm:]], axis=1)
    conv_shift = jnp.concatenate([group(conv_b, 0, d_ssm, 0), conv_b[d_ssm:]], axis=0)
    dt_shift = group(dt_bias, 0, HM, 0)
    log_scale = group(a_log, 0, HM, 0)
    skip_gain = group(d_skip, 0, HM, 0)
    expand = expander(heads, HDIM)

    def wide(values):
        return dot(values, expand, highest)

    def per_head(values):
        return dot_t(values, expand, highest)

    skip_x = wide(skip_gain[None, :])

    def prepare(padded_in, taps_in, shift_in, dt_in, dt_shift_in, log_in):
        activated = jax.nn.silu(causal_conv(padded_in, taps_in, shift_in))
        return (
            activated[:, :x_part],
            activated[:, x_part : x_part + NST],
            activated[:, x_part + NST :],
            jax.nn.softplus(dt_in + dt_shift_in),
            -jnp.exp(log_in),
        )

    (x_conv, b_conv, c_conv, dt_value, decay_rate), prep_pull = jax.vjp(
        prepare, padded, conv_taps, conv_shift, dt_raw, dt_shift, log_scale
    )
    blocks = span // chunk_len
    ones_low = jnp.tril(jnp.ones((chunk_len, chunk_len), f32))
    cs_block = jnp.einsum(
        "ts,bsh->bth",
        ones_low,
        (dt_value * decay_rate[None, :]).reshape(blocks, chunk_len, heads),
        precision=highest,
    )
    block_total = cs_block[:, -1]
    block_base = jnp.concatenate(
        [jnp.zeros((1, heads), f32), jnp.cumsum(block_total, axis=0)], axis=0
    )
    cs_dev = (cs_block + block_base[:-1, None, :]).reshape(span, heads)
    cs = cs_block.reshape(span, heads)
    cst = jnp.swapaxes(cs_block, 1, 2)
    log_dev = block_base[-1]
    csx = wide(cs)
    csx_dev = wide(cs_dev)
    dtx = wide(dt_value)
    xd = dtx * x_conv
    state_local = t_dot(b_conv, jnp.exp(csx_dev[-1:] - csx_dev) * xd, highest)
    scan = state_scan(log_dev, state_local, True)
    in_sent = [next(scan)]
    while len(in_sent) < n_cp.bit_length():
        in_sent.append(scan.send(None))
    state_in = in_sent[-1]

    kk = jnp.concatenate([kv_all[:, :HDIM], kv_all[:, :HDIM]], axis=1)
    vv = jnp.concatenate([kv_all[:, HDIM:], kv_all[:, HDIM:]], axis=1)
    w_gate_up = lax.all_gather(after(after(w_gu, kk), xs_cp), ("dp", "cp"), axis=0, tiled=True)
    pairs = [slice(p * 2 * HDIM, (p + 1) * 2 * HDIM) for p in range(q_part // (2 * HDIM))]
    att_deps = [(in_sent[0],), (in_sent[1],)]
    att_outs, lses = [], []
    for cols, deps in zip(pairs, att_deps):
        att_out, lse = attention_forward(
            where, q_scaled[:, cols], kk, vv, doc_begin, deps + tuple(att_outs)
        )
        att_outs.append(att_out)
        lses.append(lse)
    att_f32 = jnp.concatenate(att_outs, axis=1)
    att_low = att_f32.astype(low_type)

    shard_rows, out_cols = w_in.shape[0], out_half.size // w_in.shape[0]
    z_out = jnp.concatenate(
        [group(w_in, 0, d_ssm), out_half.reshape(shard_rows, out_cols)], axis=1
    )
    z_out, _ = gather_cp(after(z_out, kk), (in_sent[0], att_outs[0]))
    z_out = after(z_out, att_outs[1])
    z_out_other = swap(z_out, "dp", 1)
    w_z = in_order(
        z_out[:, :x_part], z_out_other[:, :x_part], has_bit("dp", 1), 0, jnp.concatenate
    )
    out_sides = [a[:, x_part:].reshape(-1, half_cols) for a in (z_out, z_out_other)]
    w_out = in_order(*out_sides, jnp.logical_not(holds), 1, jnp.concatenate)
    mo_rows, ao_rows = w_mo.shape[0], w_ao.shape[0]
    w_out = w_out.reshape(n_cp, mo_rows + ao_rows, d_model)
    w_out = jnp.concatenate(
        [
            w_out[:, :mo_rows].reshape(n_cp * mo_rows, d_model),
            w_out[:, mo_rows:].reshape(n_cp * ao_rows, d_model),
        ],
        axis=0,
    )

    y_core, before = ssd_forward(
        xd, b_conv, c_conv, cs, cst, csx, state_in, (att_outs[-1],)
    )
    y_low = (y_core + skip_x * x_conv).astype(low_type).astype(f32)

    gate_z = dot(normed1_all, w_z)
    gain = group(gate_norm, 0, d_ssm, 0)[None, :]
    sig_z = jax.nn.sigmoid(gate_z)
    silu_z = gate_z * sig_z
    mixed_y = y_low * silu_z
    squares = jnp.sum(mixed_y * mixed_y, axis=-1)
    squares = squares + swap(squares, "hd", 1)
    inv = lax.rsqrt(squares / d_ssm + eps_norm)[:, None]
    gated_low = (mixed_y * inv * gain).astype(low_type)
    branches = jnp.concatenate([gated_low, att_low], axis=1)
    partial = dot(branches, w_out).reshape(n_hd, tok_count, d_model)
    x_mid = x_in + fold(partial, "hd", 1, 0)

    normed2, norm2_pull = jax.vjp(rms_norm, x_mid, norm2)
    normed2_low = normed2.astype(low_type)
    gate_up = dot(normed2_low, w_gate_up)

    def swiglu(both_halves):
        return jax.nn.silu(both_halves[:, :FF]) * both_halves[:, FF:]

    hidden, swiglu_pull = jax.vjp(swiglu, gate_up)
    hidden_low = hidden.astype(low_type)

    grad_out_low = cotangent[0]
    grad_hidden = dot_t(grad_out_low, w_back)
    grad_gate_up = swiglu_pull(grad_hidden)[0].astype(low_type)
    grad_normed2 = dot_t(grad_gate_up, w_gate_up)
    grad_mid_part, g_norm2 = norm2_pull(grad_normed2)
    grad_mid = grad_out_low.astype(f32) + grad_mid_part
    grad_mid_low = grad_mid.astype(low_type)
    grad_mid_all = gather_pair(grad_mid_low, "hd", 0)

    def rows_by_owner(grad):
        rows, cols = grad.shape
        return grad.reshape(2, n_cp, n_hd, rows // (2 * n_cp * n_hd), cols)

    def to_owner(grad):
        grad = grad.reshape((-1,) + grad.shape[-1:])
        return lax.psum_scatter(grad, ("cp", "hd"), scatter_dimension=0, tiled=True).astype(f32)

    def halves_by_core(values):
        part = values.shape[1] // 2
        kept = lax.dynamic_slice_in_dim(values, dp_index * part, part, 1)
        given = lax.dynamic_slice_in_dim(values, (1 - dp_index) * part, part, 1)
        return jnp.concatenate([kept, swap(given, "dp", 1)], axis=0)

    def cores(values):
        return jnp.concatenate([values, swap(values, "dp", 1)], axis=0)

    g_down = t_dot(halves_by_core(hidden_low), cores(grad_out_low)).astype(low_type)
    s_down = to_owner(g_down)
    g_gate_up = t_dot(
        halves_by_core(after(normed2_low, grad_mid_low)), cores(grad_gate_up)
    ).astype(low_type)
    s_gu = to_owner(g_gate_up)
    result_seq = x_mid + dot(after(hidden_low, grad_mid_low), w_back)

    grad_branches = dot_t(grad_mid_all, w_out)
    grad_gated = grad_branches[:, :x_part]
    grad_att = grad_branches[:, x_part:].astype(low_type)
    delta = jnp.transpose(
        dot_t(grad_att.astype(f32) * att_f32, expander(q_part // HDIM, HDIM), highest)
    )

    gain_grad = grad_gated * gain
    along = jnp.sum(gain_grad * mixed_y, axis=-1)
    along = along + swap(along, "hd", 1)
    grad_mixed = inv * gain_grad - mixed_y * (inv * inv * inv * (along / d_ssm)[:, None])
    g_gain = jnp.sum(grad_gated * mixed_y * inv, axis=0)
    grad_y = (grad_mixed * silu_z).astype(low_type).astype(f32)
    grad_z = (grad_mixed * y_low * sig_z * (1.0 + gate_z * (1.0 - sig_z))).astype(low_type)

    scaled_dy = jnp.exp(csx_dev) * grad_y
    scan = state_scan(log_dev, t_dot(c_conv, scaled_dy, highest), False)
    future = next(scan)

    normed1_half = halves_by_core(normed1_all)

    def by_owner(grad):
        grad = t_dot(normed1_half, cores(grad)).astype(low_type)
        return grad.reshape(n_cp, d_model // (2 * n_cp), grad.shape[1])

    g_out = t_dot(after(branches, scaled_dy), grad_mid_all).astype(low_type)
    g_out = jnp.concatenate(
        [
            g_out[:x_part].reshape(n_cp, n_hd, mo_rows // n_hd, d_model),
            g_out[x_part:].reshape(n_cp, n_hd, ao_rows // n_hd, d_model),
        ],
        axis=2,
    )
    g_out = fold(g_out, "dp", 1, 1).astype(low_type)
    dqs, dkvs = [], []
    bwd_deps = (g_gate_up, g_down, g_out)
    for p, cols in enumerate(pairs):
        dq, dkv = attention_backward(
            where,
            q_scaled[:, cols],
            grad_att[:, cols],
            kk,
            vv,
            doc_begin,
            lses[p],
            delta[2 * p : 2 * p + 2],
            bwd_deps + (future,),
        )
        dqs.append(dq)
        future = scan.send(dq)
        bwd_deps = ()
        dkvs.append(dkv.reshape(n_cp, span, 2 * HDIM))
    dkv_sum = dkvs[0].astype(f32)
    for dkv in dkvs[1:]:
        dkv_sum = dkv_sum + dkv.astype(f32)
    dkv_low = dkv_sum.astype(low_type)
    dkv, dkv_steps = fold_cp(dkv_low, low_first())
    for last_sent in scan:
        future = last_sent

    out_grad, out_folds = fold_cp(g_out, low_first(), (None, dqs[0], dqs[1]) + (None,) * 5)
    s_out = lax.ppermute(out_grad, ("dp", "hd"), [(0, 0), (1, 2), (2, 1), (3, 3)])
    s_mo, s_ao = s_out[: mo_rows // n_hd], s_out[mo_rows // n_hd :]


    dxd, db, dc = ssd_backward(
        xd,
        grad_y,
        b_conv,
        c_conv,
        cs,
        cst,
        csx,
        before,
        future,
        (dqs[-1], out_folds[0], dkv_low, s_down),
    )

    ddt_direct = per_head(x_conv * dxd)
    dcs = per_head(grad_y * y_core) - dt_value * ddt_direct
    state_end = jnp.exp(csx_dev[-1:]) * state_in + state_local
    end_term = per_head(jnp.sum(future * state_end, axis=0)[None, :])
    ones_up = jnp.triu(jnp.ones((span, span), f32))
    da = dot(ones_up, dcs, highest) + end_term
    g_skip = per_head(jnp.sum(grad_y * x_conv, axis=0)[None, :])[0]
    grad_padded, grad_taps, grad_shift, grad_dt, grad_dt_shift, grad_log = prep_pull(
        (
            dtx * dxd + skip_x * grad_y,
            after(db, dkv_steps[0]),
            dc,
            ddt_direct + decay_rate[None, :] * da,
            jnp.sum(da * dt_value, axis=0),
        )
    )
    rim_back = shifted(grad_padded[: tap_count - 1], "cp", -1)
    grad_conv_in = jnp.concatenate(
        [
            grad_padded[tap_count - 1 : span],
            grad_padded[span:] + rim_back,
        ],
        axis=0,
    ).astype(low_type)
    grad_xs = after(after(grad_conv_in, dkv_steps[1]), s_gu)[:, :x_part]
    grad_bc_dt = jnp.concatenate(
        [
            grad_conv_in[:, x_part:],
            grad_dt.astype(low_type),
            jnp.zeros((span, dt_pad), low_type),
        ],
        axis=1,
    )
    g_early = by_owner(jnp.concatenate([grad_xs, grad_bc_dt], axis=1))
    grad_qkv = jnp.concatenate([dq * score_scale for dq in dqs] + [after(dkv, g_early)], axis=1)
    grad_qkv = (grad_qkv * cosines - half_turn(grad_qkv) * sines).astype(low_type)
    g_late = by_owner(jnp.concatenate([grad_z, grad_qkv], axis=1))
    r_late, _ = fold_cp(g_late, low_last())
    r_early, early_steps = fold_cp(g_early, low_first())
    grad_misc = jnp.concatenate([grad_qkv, grad_bc_dt], axis=1)

    grad_misc = after(after(grad_misc, g_early), g_late)
    grad_normed1 = dot_t(grad_z, w_z) + dot_t(grad_misc, w_misc) + dot_t(grad_xs, w_xs)
    grad_normed1 = fold(grad_normed1.reshape(n_hd, tok_count, d_model), "hd", 1, 0)
    _, norm1_pull = jax.vjp(rms_norm, x_in, norm1)
    grad_x_part, g_norm1 = norm1_pull(grad_normed1)
    grad_tokens_out = (grad_mid + grad_x_part).astype(low_type)

    reduced_in = jnp.concatenate([r_late, r_early], axis=1).astype(low_type)
    own_rows = reduced_in.shape[0] // n_hd
    halves = reduced_in.reshape(n_hd, own_rows, reduced_in.shape[1])
    got = swap(jnp.where(hd_high, halves[0], halves[1]), "hd", 1)
    mine = jnp.where(hd_high, halves[1], halves[0])
    group0 = jnp.where(hd_high, got, mine).astype(f32)
    group1 = jnp.where(hd_high, mine, got).astype(f32)

    def both(begin, width):
        return [group0[:, begin : begin + width], group1[:, begin : begin + width]]

    xs_at = x_part + qkv_cols
    bc0, bc1 = both(xs_at + x_part, bc_width)
    s_in = jnp.concatenate(
        both(0, x_part)
        + both(xs_at, x_part)
        + [bc0 + bc1]
        + both(x_part, q_part)
        + both(x_part + q_part, k_part)
        + both(x_part + q_part + k_part, k_part),
        axis=1,
    )
    s_dt = jnp.concatenate(both(xs_at + x_part + bc_width, heads), axis=1)

    def placed(values, width):
        full = jnp.zeros(values.shape[:-1] + (width,), f32)
        return lax.dynamic_update_slice_in_dim(
            full, values, hd_index * values.shape[-1], values.ndim - 1
        )

    g_conv_w = jnp.concatenate([placed(grad_taps[:, :x_part], d_ssm), grad_taps[:, x_part:]], axis=1)
    g_conv_b = jnp.concatenate([placed(grad_shift[:x_part], d_ssm), grad_shift[x_part:]], axis=0)
    small = [
        g_norm1,
        g_norm2,
        placed(g_gain, d_ssm),
        g_conv_w,
        g_conv_b,
        placed(grad_dt_shift, HM),
        placed(grad_log, HM),
        placed(g_skip, HM),
    ]
    flat = jnp.concatenate([s.reshape(-1) for s in small])
    length = flat.shape[0]
    flat = jnp.pad(flat, (0, -length % 1024)).reshape(-1, 128)
    flat = flat + swap(flat, "dp", 1)
    flat = flat + swap(flat, "hd", 1)
    for bit in low_first():
        flat = flat + swap(flat, "cp", bit)
    flat = flat.reshape(-1)
    sums = []
    begin = 0
    for s in small:
        sums.append(flat[begin : begin + s.size].reshape(s.shape))
        begin += s.size
    return (
        result_seq.astype(low_type)[None],
        grad_tokens_out[None],
        s_in,
        s_dt,
        s_mo,
        s_ao,
        s_gu,
        s_down,
        *sums,
    )


def solution(mesh):
    weight = P(("dp", "cp"), None)
    grad = P(("dp", "cp", "hd"), None)
    seq = P("dp", ("cp", "hd"), None)
    in_specs = (seq, P("dp", None), seq) + (weight,) * 6 + (P(),) * 8
    out_specs = (seq, seq) + (grad,) * 6 + (P(),) * 8
    return jax.shard_map(
        per_device, mesh=mesh, in_specs=in_specs, out_specs=out_specs, check_vma=False
    )
```

```python
import math

import jax
import jax.numpy as jnp
from jax import lax
from jax.experimental import pallas as pl
from jax.experimental.pallas import tpu as pltpu
from jax.sharding import PartitionSpec as P

HM = 24
HDIM = 64
NST = 128
QH = 8
KVH = 2
FF = 2048

eps_norm = 1e-05
rope_base = 100000000000.0
masked = -1e30
highest = lax.Precision.HIGHEST
low_type = jnp.bfloat16
f32 = jnp.float32
chunk_len = 128
vmem_bytes = 56 * 1024 * 1024


def swap(value, axis, bit):
    count = lax.axis_size(axis)
    return lax.ppermute(value, axis, [(i, i ^ bit) for i in range(count)])


def shifted(value, axis, steps):
    count = lax.axis_size(axis)
    initial, last = (max(0, -steps), min(count, count - steps))
    return lax.ppermute(value, axis, [(source, source + steps) for source in range(initial, last)])


def has_bit(axis, bit):
    return (lax.axis_index(axis) & bit) != 0


def in_order(mine, other, high, dim, join):
    return join([jnp.where(high, other, mine), jnp.where(high, mine, other)], dim)


def gather_cp(value, gates=()):
    rows, cols = value.shape
    held = value[None]
    steps = []
    bit = lax.axis_size("cp") // 2
    while bit:
        ahead = bit.bit_length() - 1
        if ahead < len(gates) and gates[-1 - ahead] is not None:
            held = after(held, gates[-1 - ahead])
        other = swap(held, "cp", bit)
        held = in_order(held, other, has_bit("cp", bit), 1, jnp.stack).reshape(-1, rows, cols)
        steps.append(held)
        bit //= 2
    return held.reshape(-1, cols), steps


def gather_pair(value, axis, dim):
    return in_order(value, swap(value, axis, 1), has_bit(axis, 1), dim, jnp.concatenate)


def fold(value, axis, bit, dim, sents=None):
    high = has_bit(axis, bit)
    first = lax.index_in_dim(value, 0, dim, False)
    second = lax.index_in_dim(value, 1, dim, False)
    sent = jnp.where(high, first, second).astype(low_type)
    if sents is not None:
        sents.append(sent)
    got = swap(sent, axis, bit)
    return jnp.where(high, second, first).astype(f32) + got.astype(f32)


def fold_cp(value, order, gates=(None,) * 8):
    count = lax.axis_size("cp")
    bits = count.bit_length() - 1
    held = value.reshape((2,) * bits + value.shape[1:])
    left = [1 << (bits - 1 - d) for d in range(bits)]
    steps, sents = [], []
    for gate, bit in zip(gates, order):
        dim = left.index(bit)
        if gate is not None:
            held = after(held, gate)
        held = fold(held, "cp", bit, dim, sents)
        left.pop(dim)
        if left:
            held = held.astype(low_type)
        steps.append(held)
    return held, steps, sents


def low_first():
    return [1 << d for d in range(lax.axis_size("cp").bit_length() - 1)]


def low_last():
    bits = low_first()
    return bits[1:] + bits[:1]


def after(value, earlier):
    first = lax.slice(earlier, (0,) * earlier.ndim, (1,) * earlier.ndim).reshape(())
    return value + (first.astype(f32) * 0.0).astype(value.dtype)


def state_scan(log_decay, state, forward):
    heads = log_decay.shape[0]
    width = state.shape[1] // heads
    pre_log, pre_state = jnp.zeros_like(log_decay), jnp.zeros_like(state)
    count = lax.axis_size("cp")
    bit = 1
    gate = None

    def spread(values):
        return dot(jnp.exp(values)[None, :], expander(heads, width), highest)

    while bit < count:
        top = log_decay.astype(low_type)
        rest = (log_decay - top.astype(f32)).astype(low_type)
        tail = jnp.concatenate([top, rest, jnp.zeros((state.shape[1] - 2 * heads,), low_type)])
        tail = jnp.concatenate([tail[None], jnp.zeros((15, state.shape[1]), low_type)], axis=0)
        sent = jnp.concatenate([state.astype(low_type), tail], axis=0)
        if gate is not None:
            sent = after(sent, gate)
        gate = yield sent
        got = swap(sent, "cp", bit)
        got_state = got[:-16].astype(f32)
        got_log = got[-16, :heads].astype(f32) + got[-16, heads : 2 * heads].astype(f32)
        joins = has_bit("cp", bit) if forward else jnp.logical_not(has_bit("cp", bit))
        pre_state = jnp.where(joins, spread(pre_log) * got_state + pre_state, pre_state)
        pre_log = jnp.where(joins, pre_log + got_log, pre_log)
        state = jnp.where(
            joins, spread(log_decay) * got_state + state, spread(got_log) * state + got_state
        )
        log_decay = log_decay + got_log
        bit *= 2
    yield pre_state


def rms_norm(values, gain_vec):
    return (
        values * lax.rsqrt(jnp.mean(values * values, axis=-1, keepdims=True) + eps_norm) * gain_vec
    )


def expander(heads, width):
    column = jnp.arange(heads * width, dtype=jnp.int32)[None, :] // width
    return (column == jnp.arange(heads, dtype=jnp.int32)[:, None]).astype(f32)


def half_turner(width):
    column = jnp.arange(width, dtype=jnp.int32)
    half = HDIM // 2
    partner = jnp.where(column % HDIM < half, column + half, column - half)
    return (column[:, None] == partner[None, :]).astype(f32)


def causal_conv(padded, conv_taps, conv_shift):
    tap_count = conv_taps.shape[0]
    out_rows = padded.shape[0] - tap_count + 1
    summed = conv_shift[None, :]
    for tap_index in range(tap_count):
        summed = summed + conv_taps[tap_index][None, :] * padded[tap_index : tap_index + out_rows]
    return summed


def t_dot(left, right, precision=None):
    return lax.dot_general(
        left,
        right,
        (((0,), (0,)), ((), ())),
        preferred_element_type=f32,
        precision=precision,
    )


def dot_t(left, right, precision=None):
    return lax.dot_general(
        left,
        right,
        (((1,), (1,)), ((), ())),
        preferred_element_type=f32,
        precision=precision,
    )


def dot(left, right, precision=None):
    return jnp.dot(left, right, preferred_element_type=f32, precision=precision)


def left_half(shape):
    return lax.broadcasted_iota(jnp.int32, shape, 1) < HDIM


def both_heads(pair):
    left = left_half(pair.shape)
    pair = pair.astype(f32)
    return (
        jnp.where(left, pair, 0.0).astype(low_type),
        jnp.where(left, 0.0, pair).astype(low_type),
    )


def att_fwd_kernel(where_ref, q_ref, kk_ref, vv_ref, start_ref, *rest):
    out_ref, lse_ref, top_s, sum_s, acc_s = rest[-5:]
    span = q_ref.shape[0]
    place = where_ref[0]
    latest = where_ref[1]
    queries = both_heads(q_ref[...])
    top_s[...] = jnp.full(top_s.shape, masked, f32)
    sum_s[...] = jnp.zeros(sum_s.shape, f32)
    acc_s[...] = jnp.zeros(acc_s.shape, f32)

    def block(turn_index, _):
        j = place - turn_index
        base = pl.multiple_of(j * span, span)
        keys = kk_ref[pl.ds(base, span), :]
        values = vv_ref[pl.ds(base, span), :]

        def hide(scores):
            key_pos = base + lax.broadcasted_iota(jnp.int32, scores.shape, 1)
            row_pos = place * span + lax.broadcasted_iota(jnp.int32, scores.shape, 0)
            return jnp.where((key_pos <= row_pos) & (key_pos >= start_ref[...]), scores, masked)

        def work(shape_scores):
            for e in range(2):
                scores = shape_scores(dot_t(queries[e], keys))
                old_top = top_s[e]
                new_top = jnp.maximum(old_top, jnp.max(scores, axis=1, keepdims=True))
                weights = jnp.exp(scores - new_top)
                fall = jnp.exp(old_top - new_top)
                sum_s[e] = sum_s[e] * fall + jnp.sum(weights, axis=1, keepdims=True)
                acc_s[e] = acc_s[e] * fall + dot(weights.astype(low_type), values)
                top_s[e] = new_top

        needs = (j == place) | (latest > base)

        @pl.when(needs)
        def _():
            work(hide)

        @pl.when(jnp.logical_not(needs))
        def _():
            work(lambda scores: scores)

        return 0

    lax.fori_loop(0, place + 1, block, 0)
    outs = [acc_s[e] / sum_s[e] for e in range(2)]
    out_ref[...] = jnp.where(left_half(outs[0].shape), outs[0], outs[1])
    for e in range(2):
        lse_ref[e] = top_s[e] + jnp.log(sum_s[e])


def att_bwd_kernel(
    where_ref, q_ref, do_ref, kk_ref, vv_ref, start_ref, lse_ref, delta_ref, *rest
):
    dq_ref, dkv_ref, dq_s = rest[-3:]
    span = q_ref.shape[0]
    place = where_ref[0]
    latest = where_ref[1]
    queries = both_heads(q_ref[...])
    grads = both_heads(do_ref[...])
    dq_s[...] = jnp.zeros(dq_s.shape, f32)

    def block(j, _):
        base = pl.multiple_of(j * span, span)
        keys = kk_ref[pl.ds(base, span), :]
        values = vv_ref[pl.ds(base, span), :]

        def hide(scores):
            key_pos = base + lax.broadcasted_iota(jnp.int32, scores.shape, 0)
            row_pos = place * span + lax.broadcasted_iota(jnp.int32, scores.shape, 1)
            return jnp.where((key_pos <= row_pos) & (key_pos >= start_ref[...]), scores, masked)

        def work(shape_scores):
            dkk, dvv = [], []
            for e in range(2):
                scores = shape_scores(dot_t(keys, queries[e]))
                grad_probs = dot_t(values, grads[e])
                probs = jnp.exp(scores - lse_ref[e])
                grad_scores = (probs * (grad_probs - delta_ref[e])).astype(low_type)
                dq_s[e] += t_dot(grad_scores, keys)
                dkk.append(dot(grad_scores, queries[e]))
                dvv.append(dot(probs.astype(low_type), grads[e]))
            dkk, dvv = dkk[0] + dkk[1], dvv[0] + dvv[1]
            dkk = dkk + pltpu.roll(dkk, HDIM, 1)
            dvv = dvv + pltpu.roll(dvv, HDIM, 1)
            dkv_ref[pl.ds(base, span), :] = jnp.where(left_half(dkk.shape), dkk, dvv).astype(
                low_type
            )

        needs = (j == place) | (latest > base)

        @pl.when(needs)
        def _():
            work(hide)

        @pl.when(jnp.logical_not(needs))
        def _():
            work(lambda scores: scores)

        return 0

    lax.fori_loop(0, place + 1, block, 0)

    def clear(j, _):
        base = pl.multiple_of(j * span, span)
        dkv_ref[pl.ds(base, span), :] = jnp.zeros((span, 2 * HDIM), low_type)
        return 0

    lax.fori_loop(place + 1, dkv_ref.shape[0] // span, clear, 0)
    dq_ref[...] = jnp.where(left_half(dq_ref.shape), dq_s[0], dq_s[1])


def whole_spec(shape):
    return pl.BlockSpec(shape, lambda *_: (0,) * len(shape))


def any_specs(count):
    return [pl.BlockSpec(memory_space=pl.ANY)] * count


def att_cost(span, keys, matmuls):
    return pl.CostEstimate(
        flops=2 * matmuls * span * 2 * keys * 256,
        bytes_accessed=4 * keys * 128,
        transcendentals=span * 2 * keys,
    )


def attention_forward(where, queries, kk, vv, starts, deps):
    span, width = queries.shape
    return pl.pallas_call(
        att_fwd_kernel,
        in_specs=[
            pl.BlockSpec(memory_space=pltpu.SMEM),
            whole_spec((span, width)),
            whole_spec(kk.shape),
            whole_spec(vv.shape),
            whole_spec((span, 1)),
        ]
        + any_specs(len(deps)),
        out_specs=[whole_spec((span, width)), whole_spec((2, span, 1))],
        out_shape=[
            jax.ShapeDtypeStruct((span, width), f32),
            jax.ShapeDtypeStruct((2, span, 1), f32),
        ],
        grid=(1,),
        scratch_shapes=[
            pltpu.VMEM((2, span, 1), f32),
            pltpu.VMEM((2, span, 1), f32),
            pltpu.VMEM((2, span, width), f32),
        ],
        compiler_params=pltpu.CompilerParams(vmem_limit_bytes=vmem_bytes),
        cost_estimate=att_cost(span, kk.shape[0], 4),
        name="attention_forward",
    )(where, queries, kk, vv, starts.reshape(span, 1), *deps)


def attention_backward(where, queries, grads, kk, vv, starts, lse, delta, deps):
    span, width = queries.shape
    return pl.pallas_call(
        att_bwd_kernel,
        in_specs=[
            pl.BlockSpec(memory_space=pltpu.SMEM),
            whole_spec((span, width)),
            whole_spec((span, width)),
            whole_spec(kk.shape),
            whole_spec(vv.shape),
            whole_spec((1, span)),
            whole_spec((2, 1, span)),
            whole_spec((2, 1, span)),
        ]
        + any_specs(len(deps)),
        out_specs=[whole_spec((span, width)), whole_spec(kk.shape)],
        out_shape=[
            jax.ShapeDtypeStruct((span, width), f32),
            jax.ShapeDtypeStruct(kk.shape, low_type),
        ],
        grid=(1,),
        scratch_shapes=[
            pltpu.VMEM((2, span, width), f32),
        ],
        compiler_params=pltpu.CompilerParams(vmem_limit_bytes=vmem_bytes),
        cost_estimate=att_cost(span, kk.shape[0], 10),
        name="attention_backward",
    )(
        where,
        queries,
        grads,
        kk,
        vv,
        starts.reshape(1, span),
        lse.reshape(2, 1, span),
        delta.reshape(2, 1, span),
        *deps,
    )


def pair_blocks(pair):
    left = lax.broadcasted_iota(jnp.int32, pair.shape, 1) < HDIM
    return jnp.where(left, pair, 0.0), jnp.where(left, 0.0, pair)


def ssd_fwd_kernel(xd_ref, b_ref, c_ref, cs_ref, cst_ref, csx_ref, *rest):
    y_ref, before_ref, s_s = rest[-3:]

    @pl.when(pl.program_id(0) == 0)
    def _():
        s_s[...] = jnp.zeros(s_s.shape, f32)

    rows = xd_ref.shape[0]
    b, c = b_ref[...], c_ref[...]
    inner = dot_t(c, b, highest)
    lower = lax.broadcasted_iota(jnp.int32, (rows, rows), 0) >= lax.broadcasted_iota(
        jnp.int32, (rows, rows), 1
    )
    state = s_s[...]
    before_ref[...] = state
    csx = csx_ref[...]
    last = csx[rows - 1 :, :]
    carried = jnp.exp(csx) * dot(c, state, highest)

    def mixing(h):
        spread = jnp.where(lower, cs_ref[:, h : h + 1] - cst_ref[h : h + 1, :], masked)
        return jnp.exp(spread) * inner

    for pair in range(xd_ref.shape[1] // (2 * HDIM)):
        cols = slice(pair * 2 * HDIM, (pair + 1) * 2 * HDIM)
        mix = jnp.concatenate([mixing(2 * pair), mixing(2 * pair + 1)], axis=1)
        blocks = jnp.concatenate(pair_blocks(xd_ref[:, cols]), axis=0)
        y_ref[:, cols] = carried[:, cols] + dot(mix, blocks, highest)
    s_s[...] = jnp.exp(last) * state + t_dot(b, jnp.exp(last - csx) * xd_ref[...], highest)


def ssd_bwd_kernel(
    xd_ref,
    dy_ref,
    b_ref,
    c_ref,
    cs_ref,
    cst_ref,
    csx_ref,
    before_ref,
    *rest,
):
    dxd_ref, db_ref, dc_ref, ds_s = rest[-4:]

    @pl.when(pl.program_id(0) == 0)
    def _():
        ds_s[...] = jnp.zeros(ds_s.shape, f32)

    rows = xd_ref.shape[0]
    b, c = b_ref[...], c_ref[...]
    inner_t = dot_t(b, c, highest)
    row_id = lax.broadcasted_iota(jnp.int32, (rows, rows), 0)
    col_id = lax.broadcasted_iota(jnp.int32, (rows, rows), 1)
    csx = csx_ref[...]
    last = csx[rows - 1 :, :]
    grad_state = ds_s[...]
    end_fall = jnp.exp(last - csx)
    from_state = end_fall * dot(b, grad_state, highest)
    scaled_dy = jnp.exp(csx) * dy_ref[...]
    grad_inner = jnp.zeros((rows, rows), f32)

    def falls(h):
        spread = cs_ref[:, h : h + 1] - cst_ref[h : h + 1, :]
        return jnp.exp(jnp.where(row_id >= col_id, spread, masked))

    def falls_t(h):
        spread = cst_ref[h : h + 1, :] - cs_ref[:, h : h + 1]
        return jnp.exp(jnp.where(row_id <= col_id, spread, masked))

    for pair in range(xd_ref.shape[1] // (2 * HDIM)):
        cols = slice(pair * 2 * HDIM, (pair + 1) * 2 * HDIM)
        dy_left, dy_right = pair_blocks(dy_ref[:, cols])
        mix_t = jnp.concatenate(
            [falls_t(2 * pair) * inner_t, falls_t(2 * pair + 1) * inner_t], axis=1
        )
        blocks = jnp.concatenate([dy_left, dy_right], axis=0)
        dxd_ref[:, cols] = from_state[:, cols] + dot(mix_t, blocks, highest)
        xd = xd_ref[:, cols]
        grad_inner = grad_inner + falls(2 * pair) * dot_t(dy_left, xd, highest)
        grad_inner = grad_inner + falls(2 * pair + 1) * dot_t(dy_right, xd, highest)
    dc_ref[...] = dot(grad_inner, b, highest) + dot_t(scaled_dy, before_ref[...], highest)
    db_ref[...] = t_dot(grad_inner, c, highest) + dot_t(
        end_fall * xd_ref[...], grad_state, highest
    )
    ds_s[...] = jnp.exp(last) * grad_state + t_dot(c, scaled_dy, highest)


def ssd_forward(xd, b, c, cs, cst, csx, deps):
    length, width = xd.shape
    blocks = length // chunk_len
    heads = cs.shape[1]

    def rows(w):
        return pl.BlockSpec((chunk_len, w), lambda i: (i, 0))

    return pl.pallas_call(
        ssd_fwd_kernel,
        grid=(blocks,),
        in_specs=[
            rows(width),
            rows(NST),
            rows(NST),
            rows(heads),
            pl.BlockSpec((None, heads, chunk_len), lambda i: (i, 0, 0)),
            rows(width),
        ]
        + any_specs(len(deps)),
        out_specs=[rows(width), pl.BlockSpec((None, NST, width), lambda i: (i, 0, 0))],
        out_shape=[
            jax.ShapeDtypeStruct((length, width), f32),
            jax.ShapeDtypeStruct((blocks, NST, width), f32),
        ],
        scratch_shapes=[pltpu.VMEM((NST, width), f32)],
        compiler_params=pltpu.CompilerParams(vmem_limit_bytes=vmem_bytes),
        cost_estimate=pl.CostEstimate(
            flops=12 * 3 * length * width * NST, bytes_accessed=20 * length * width, transcendentals=0
        ),
        name="ssd_forward",
    )(xd, b, c, cs, cst, csx, *deps)


def ssd_backward(xd, dy, b, c, cs, cst, csx, before, deps):
    length, width = xd.shape
    blocks = length // chunk_len
    heads = cs.shape[1]

    def rows(w):
        return pl.BlockSpec((chunk_len, w), lambda i: (blocks - 1 - i, 0))

    def slabs(*shape):
        return pl.BlockSpec((None,) + shape, lambda i: (blocks - 1 - i, 0, 0))

    return pl.pallas_call(
        ssd_bwd_kernel,
        grid=(blocks,),
        in_specs=[
            rows(width),
            rows(width),
            rows(NST),
            rows(NST),
            rows(heads),
            slabs(heads, chunk_len),
            rows(width),
            slabs(NST, width),
        ]
        + any_specs(len(deps)),
        out_specs=[rows(width), rows(NST), rows(NST)],
        out_shape=[
            jax.ShapeDtypeStruct((length, width), f32),
            jax.ShapeDtypeStruct((length, NST), f32),
            jax.ShapeDtypeStruct((length, NST), f32),
        ],
        scratch_shapes=[pltpu.VMEM((NST, width), f32)],
        compiler_params=pltpu.CompilerParams(vmem_limit_bytes=vmem_bytes),
        cost_estimate=pl.CostEstimate(
            flops=12 * 8 * length * width * NST, bytes_accessed=24 * length * width, transcendentals=0
        ),
        name="ssd_backward",
    )(xd, dy, b, c, cs, cst, csx, before, *deps)


def per_device(
    tokens,
    doc_ids,
    cotangent,
    w_in,
    w_dt,
    w_mo,
    w_ao,
    w_gu,
    w_down,
    norm1,
    norm2,
    gate_norm,
    conv_w,
    conv_b,
    dt_bias,
    a_log,
    d_skip,
):
    n_hd = lax.axis_size("hd")
    n_cp = lax.axis_size("cp")
    hd_index = lax.axis_index("hd")
    cp_index = lax.axis_index("cp")
    dp_index = lax.axis_index("dp")
    hd_high = has_bit("hd", 1)
    x_in = tokens[0].astype(f32)
    tok_count, d_model = x_in.shape
    span = tok_count * n_hd
    d_ssm = HM * HDIM
    q_width = QH * HDIM
    k_width = KVH * HDIM
    x_part = d_ssm // n_hd
    heads = HM // n_hd
    q_part = q_width // n_hd
    k_part = k_width // n_hd
    bc_width = 2 * NST
    qkv_cols = q_part + 2 * k_part
    tap_count = conv_w.shape[0]
    score_scale = 1.0 / math.sqrt(HDIM)
    documents = doc_ids[0]

    def group(array, begin, width, dim=1):
        part = width // n_hd
        return lax.dynamic_slice_in_dim(array, begin + hd_index * part, part, dim)

    tokens_all = gather_pair(tokens[0], "hd", 0)

    normed1_all = rms_norm(tokens_all.astype(f32), norm1).astype(low_type)
    rim_tokens = shifted(tokens_all[span - 16 :], "cp", 1)
    normed1_rim = rms_norm(rim_tokens.astype(f32), norm1).astype(low_type)

    own_docs = lax.dynamic_slice_in_dim(documents, cp_index * span, span, 0)
    doc_begin = jnp.sum(documents[None, :] < own_docs[:, None], axis=1).astype(jnp.int32)
    where = jnp.stack([cp_index, jnp.max(doc_begin)]).astype(jnp.int32)

    positions = cp_index * span + jnp.arange(span, dtype=jnp.int32)
    half_width = HDIM // 2
    column = jnp.arange(qkv_cols, dtype=jnp.int32)
    turns = column < q_part + k_part
    power = (column % half_width).astype(f32)
    frequency = jnp.where(turns, rope_base ** (-2.0 * power / HDIM), 0.0)
    sign = jnp.where(column % HDIM < half_width, -1.0, 1.0)
    angles = positions.astype(f32)[:, None] * frequency[None, :]
    cosines = jnp.cos(angles)
    sines = jnp.sin(angles) * sign[None, :]
    cosines, sines = lax.optimization_barrier((cosines, sines))
    turner = half_turner(qkv_cols).astype(low_type)

    def half_turn(values):
        top = values.astype(low_type)
        return dot(top, turner) + dot((values - top.astype(f32)).astype(low_type), turner)

    q_start = 2 * d_ssm + bc_width
    k_start = q_start + q_width
    v_start = k_start + k_width
    dt_pad = 128 - heads
    shard_misc = jnp.concatenate(
        [
            group(w_in, q_start, q_width),
            group(w_in, k_start, k_width),
            group(w_in, v_start, k_width),
            w_in[:, 2 * d_ssm : q_start],
            group(w_dt, 0, HM),
            jnp.zeros((w_dt.shape[0], dt_pad), low_type),
        ],
        axis=1,
    )
    misc_cp, _ = gather_cp(shard_misc, (where, normed1_all))
    w_misc = gather_pair(after(after(misc_cp, cosines), normed1_rim), "dp", 0)
    xs_cp, xs_steps = gather_cp(after(group(w_in, d_ssm, d_ssm), w_misc))
    out_rows = jnp.concatenate([w_mo, w_ao], axis=0)
    half_cols = d_model // 2
    handed = swap(out_rows[:, half_cols:], "dp", 1)
    holds = dp_index == hd_index
    out_half = jnp.where(holds, out_rows[:, :half_cols], handed)
    w_xs = gather_pair(xs_cp, "dp", 0)

    proj = dot(normed1_all, w_misc)
    qkv = proj[:, :qkv_cols]
    qkv_low = (qkv * cosines + half_turn(qkv) * sines).astype(low_type)
    kv_all, _ = gather_cp(qkv_low[:, q_part:], (xs_steps[0], xs_steps[1]))
    q_scaled = qkv_low[:, :q_part] * jnp.asarray(score_scale, low_type)
    bc = proj[:, qkv_cols : qkv_cols + bc_width].astype(low_type)
    at = qkv_cols + bc_width
    dt_raw = proj[:, at : at + heads].astype(low_type).astype(f32)
    x_bc = jnp.concatenate([dot(normed1_all, w_xs).astype(low_type), bc], axis=1)
    w_bc = w_misc[:, qkv_cols : qkv_cols + bc_width]
    rim_rows = jnp.concatenate([dot(normed1_rim, w_xs), dot(normed1_rim, w_bc)], axis=1)
    rim_rows = rim_rows.astype(low_type)[16 - (tap_count - 1) :]

    padded = jnp.concatenate([rim_rows, x_bc], axis=0).astype(f32)
    conv_taps = jnp.concatenate([group(conv_w, 0, d_ssm), conv_w[:, d_ssm:]], axis=1)
    conv_shift = jnp.concatenate([group(conv_b, 0, d_ssm, 0), conv_b[d_ssm:]], axis=0)
    dt_shift = group(dt_bias, 0, HM, 0)
    log_scale = group(a_log, 0, HM, 0)
    skip_gain = group(d_skip, 0, HM, 0)
    expand = expander(heads, HDIM)

    def wide(values):
        return dot(values, expand, highest)

    def per_head(values):
        return dot_t(values, expand, highest)

    skip_x = wide(skip_gain[None, :])

    def prepare(padded_in, taps_in, shift_in, dt_in, dt_shift_in, log_in):
        activated = jax.nn.silu(causal_conv(padded_in, taps_in, shift_in))
        return (
            activated[:, :x_part],
            activated[:, x_part : x_part + NST],
            activated[:, x_part + NST :],
            jax.nn.softplus(dt_in + dt_shift_in),
            -jnp.exp(log_in),
        )

    (x_conv, b_conv, c_conv, dt_value, decay_rate), prep_pull = jax.vjp(
        prepare, padded, conv_taps, conv_shift, dt_raw, dt_shift, log_scale
    )
    blocks = span // chunk_len
    ones_low = jnp.tril(jnp.ones((chunk_len, chunk_len), f32))
    cs_block = jnp.einsum(
        "ts,bsh->bth",
        ones_low,
        (dt_value * decay_rate[None, :]).reshape(blocks, chunk_len, heads),
        precision=highest,
    )
    block_total = cs_block[:, -1]
    block_base = jnp.concatenate(
        [jnp.zeros((1, heads), f32), jnp.cumsum(block_total, axis=0)], axis=0
    )
    cs_dev = (cs_block + block_base[:-1, None, :]).reshape(span, heads)
    cs = cs_block.reshape(span, heads)
    cst = jnp.swapaxes(cs_block, 1, 2)
    log_dev = block_base[-1]
    csx = wide(cs)
    csx_dev = wide(cs_dev)
    dtx = wide(dt_value)
    xd = dtx * x_conv
    ending_xd = jnp.exp(csx_dev[-1:] - csx_dev) * xd
    state_local = t_dot(b_conv, ending_xd, highest)
    scan = state_scan(log_dev, state_local, True)
    in_sent = next(scan)
    y_own, before = ssd_forward(xd, b_conv, c_conv, cs, cst, csx, (in_sent,))
    in_sent = scan.send(y_own)

    kk = after(jnp.concatenate([kv_all[:, :HDIM], kv_all[:, :HDIM]], axis=1), w_xs)
    vv = jnp.concatenate([kv_all[:, HDIM:], kv_all[:, HDIM:]], axis=1)
    w_gate_up = after(after(w_gu, kk), xs_cp)
    w_gate_up = lax.all_gather(w_gate_up, ("dp", "cp"), axis=0, tiled=True)
    pairs = [slice(p * 2 * HDIM, (p + 1) * 2 * HDIM) for p in range(q_part // (2 * HDIM))]
    att_deps = [(), ()]
    att_outs, lses = [], []
    for cols, deps in zip(pairs, att_deps):
        att_out, lse = attention_forward(
            where, q_scaled[:, cols], kk, vv, doc_begin, deps + tuple(att_outs) + (in_sent,)
        )
        att_outs.append(att_out)
        lses.append(lse)
        in_sent = scan.send(att_out)
    for last_sent in scan:
        in_sent = last_sent
    state_in = in_sent
    att_f32 = jnp.concatenate(att_outs, axis=1)
    att_low = att_f32.astype(low_type)

    w_back = lax.all_gather(after(w_down, att_outs[0]), ("dp", "cp"), axis=0, tiled=True)

    shard_rows, out_cols = w_in.shape[0], out_half.size // w_in.shape[0]
    z_out = jnp.concatenate(
        [group(w_in, 0, d_ssm), out_half.reshape(shard_rows, out_cols)], axis=1
    )
    z_out, _ = gather_cp(after(z_out, w_misc), (xs_cp, y_own))
    z_out = after(z_out, att_outs[0])
    z_out_other = swap(z_out, "dp", 1)
    w_z = in_order(
        z_out[:, :x_part], z_out_other[:, :x_part], has_bit("dp", 1), 0, jnp.concatenate
    )
    out_sides = [a[:, x_part:].reshape(-1, half_cols) for a in (z_out, z_out_other)]
    w_out = in_order(*out_sides, jnp.logical_not(holds), 1, jnp.concatenate)
    mo_rows, ao_rows = w_mo.shape[0], w_ao.shape[0]
    w_out = w_out.reshape(n_cp, mo_rows + ao_rows, d_model)
    w_out = jnp.concatenate(
        [
            w_out[:, :mo_rows].reshape(n_cp * mo_rows, d_model),
            w_out[:, mo_rows:].reshape(n_cp * ao_rows, d_model),
        ],
        axis=0,
    )

    state_in = after(after(state_in, w_out), w_z)
    y_core = y_own + jnp.exp(csx_dev) * dot(c_conv, state_in, highest)
    y_low = (y_core + skip_x * x_conv).astype(low_type).astype(f32)

    gate_z = dot(normed1_all, w_z)
    gain = group(gate_norm, 0, d_ssm, 0)[None, :]
    sig_z = jax.nn.sigmoid(gate_z)
    silu_z = gate_z * sig_z
    mixed_y = y_low * silu_z
    squares = jnp.sum(mixed_y * mixed_y, axis=-1)
    squares = squares + swap(squares, "hd", 1)
    inv = lax.rsqrt(squares / d_ssm + eps_norm)[:, None]
    gated_low = (mixed_y * inv * gain).astype(low_type)
    branches = jnp.concatenate([gated_low, att_low], axis=1)
    partial = dot(branches, w_out).reshape(n_hd, tok_count, d_model)
    x_mid = x_in + fold(partial, "hd", 1, 0)

    normed2, norm2_pull = jax.vjp(rms_norm, x_mid, norm2)
    normed2_low = normed2.astype(low_type)
    gate_up = dot(normed2_low, w_gate_up)

    def swiglu(both_halves):
        return jax.nn.silu(both_halves[:, :FF]) * both_halves[:, FF:]

    hidden, swiglu_pull = jax.vjp(swiglu, gate_up)
    hidden_low = hidden.astype(low_type)

    grad_out_low = cotangent[0]
    grad_hidden = dot_t(grad_out_low, w_back)
    grad_gate_up = swiglu_pull(grad_hidden)[0].astype(low_type)
    grad_normed2 = dot_t(grad_gate_up, w_gate_up)
    grad_mid_part, g_norm2 = norm2_pull(grad_normed2)
    grad_mid = grad_out_low.astype(f32) + grad_mid_part
    grad_mid_low = grad_mid.astype(low_type)

    def rows_by_owner(grad):
        rows, cols = grad.shape
        return grad.reshape(2, n_cp, n_hd, rows // (2 * n_cp * n_hd), cols)

    def to_owner(grad):
        grad = grad.reshape((-1,) + grad.shape[-1:])
        return lax.psum_scatter(grad, ("cp", "hd"), scatter_dimension=0, tiled=True).astype(f32)

    def halves_by_core(values):
        part = values.shape[1] // 2
        kept = lax.dynamic_slice_in_dim(values, dp_index * part, part, 1)
        given = lax.dynamic_slice_in_dim(values, (1 - dp_index) * part, part, 1)
        return jnp.concatenate([kept, swap(given, "dp", 1)], axis=0)

    def cores(values):
        return jnp.concatenate([values, swap(values, "dp", 1)], axis=0)

    g_down = t_dot(halves_by_core(after(hidden_low, grad_mid_low)), cores(grad_out_low))
    g_down = g_down.astype(low_type)
    result_low = (x_mid + dot(after(hidden_low, grad_mid_low), w_back)).astype(low_type)
    grad_mid_all = in_order(
        after(after(grad_mid_low, g_down), result_low),
        swap(grad_mid_low, "hd", 1),
        hd_high,
        0,
        jnp.concatenate,
    )
    s_down = to_owner(after(g_down, grad_mid_all))
    g_gate_up = t_dot(
        halves_by_core(after(normed2_low, grad_mid_all)), cores(grad_gate_up)
    ).astype(low_type)
    s_gu = to_owner(g_gate_up)

    grad_branches = dot_t(grad_mid_all, w_out)
    grad_gated = grad_branches[:, :x_part]
    grad_att = grad_branches[:, x_part:].astype(low_type)
    delta = jnp.transpose(
        dot_t(grad_att.astype(f32) * att_f32, expander(q_part // HDIM, HDIM), highest)
    )

    gain_grad = grad_gated * gain
    along = jnp.sum(gain_grad * mixed_y, axis=-1)
    along = along + swap(along, "hd", 1)
    grad_mixed = inv * gain_grad - mixed_y * (inv * inv * inv * (along / d_ssm)[:, None])
    g_gain = jnp.sum(grad_gated * mixed_y * inv, axis=0)
    grad_y = (grad_mixed * silu_z).astype(low_type).astype(f32)
    grad_z = (grad_mixed * y_low * sig_z * (1.0 + gate_z * (1.0 - sig_z))).astype(low_type)

    scaled_dy = jnp.exp(csx_dev) * grad_y
    scan = state_scan(log_dev, t_dot(c_conv, scaled_dy, highest), False)
    future = next(scan)

    normed1_half = halves_by_core(normed1_all)

    def by_owner(grad):
        grad = t_dot(normed1_half, cores(grad)).astype(low_type)
        return grad.reshape(n_cp, d_model // (2 * n_cp), grad.shape[1])

    dqs, dkvs = [], []
    bwd_deps = (g_gate_up, g_down)
    dxd_own, db_own, dc_own = ssd_backward(
        xd, grad_y, b_conv, c_conv, cs, cst, csx, before, (future,) + bwd_deps
    )
    future = scan.send(dxd_own)
    for p, cols in enumerate(pairs):
        dq, dkv = attention_backward(
            where,
            q_scaled[:, cols],
            grad_att[:, cols],
            kk,
            vv,
            doc_begin,
            lses[p],
            delta[2 * p : 2 * p + 2],
            bwd_deps + (future,),
        )
        dqs.append(dq)
        future = scan.send(dq)
        bwd_deps = ()
        dkvs.append(dkv.reshape(n_cp, span, 2 * HDIM))
    dkv_sum = dkvs[0].astype(f32)
    for dkv in dkvs[1:]:
        dkv_sum = dkv_sum + dkv.astype(f32)
    dkv_low = dkv_sum.astype(low_type)
    dkv, dkv_steps, _ = fold_cp(dkv_low, low_first())
    for last_sent in scan:
        future = last_sent
    g_out = t_dot(after(branches, dqs[0]), grad_mid_all).astype(low_type)
    g_out = jnp.concatenate(
        [
            g_out[:x_part].reshape(n_cp, n_hd, mo_rows // n_hd, d_model),
            g_out[x_part:].reshape(n_cp, n_hd, ao_rows // n_hd, d_model),
        ],
        axis=2,
    )
    g_out = fold(g_out, "dp", 1, 1).astype(low_type)
    out_grad, out_folds, _ = fold_cp(g_out, low_first(), (dqs[1],) + (None,) * 7)
    s_out = lax.ppermute(out_grad, ("dp", "hd"), [(0, 0), (1, 2), (2, 1), (3, 3)])
    s_mo, s_ao = s_out[: mo_rows // n_hd], s_out[mo_rows // n_hd :]


    dxd = dxd_own + jnp.exp(csx_dev[-1:] - csx_dev) * dot(b_conv, future, highest)
    db = db_own + dot_t(ending_xd, future, highest)
    dc = dc_own + dot_t(scaled_dy, state_in, highest)

    ddt_direct = per_head(x_conv * dxd)
    dcs = per_head(grad_y * y_core) - dt_value * ddt_direct
    state_end = jnp.exp(csx_dev[-1:]) * state_in + state_local
    end_term = per_head(jnp.sum(future * state_end, axis=0)[None, :])
    ones_up = jnp.triu(jnp.ones((span, span), f32))
    da = dot(ones_up, dcs, highest) + end_term
    g_skip = per_head(jnp.sum(grad_y * x_conv, axis=0)[None, :])[0]
    grad_padded, grad_taps, grad_shift, grad_dt, grad_dt_shift, grad_log = prep_pull(
        (
            dtx * dxd + skip_x * grad_y,
            after(db, dkv_steps[0]),
            dc,
            ddt_direct + decay_rate[None, :] * da,
            jnp.sum(da * dt_value, axis=0),
        )
    )
    rim_back = shifted(grad_padded[: tap_count - 1], "cp", -1)
    grad_conv_in = jnp.concatenate(
        [
            grad_padded[tap_count - 1 : span],
            grad_padded[span:] + rim_back,
        ],
        axis=0,
    ).astype(low_type)
    grad_xs = after(after(grad_conv_in, dkv_steps[1]), s_gu)[:, :x_part]
    grad_bc_dt = jnp.concatenate(
        [
            grad_conv_in[:, x_part:],
            grad_dt.astype(low_type),
            jnp.zeros((span, dt_pad), low_type),
        ],
        axis=1,
    )
    g_early = by_owner(jnp.concatenate([grad_xs, grad_bc_dt], axis=1))
    grad_qkv = jnp.concatenate([dq * score_scale for dq in dqs] + [after(dkv, g_early)], axis=1)
    grad_qkv = (grad_qkv * cosines - half_turn(grad_qkv) * sines).astype(low_type)
    g_late = by_owner(jnp.concatenate([grad_z, grad_qkv], axis=1))
    r_late, late_steps, late_sents = fold_cp(g_late, low_last())
    r_early, _, early_sents = fold_cp(g_early, low_first())
    grad_misc = jnp.concatenate([grad_qkv, grad_bc_dt], axis=1)

    grad_misc = after(after(grad_misc, early_sents[0]), late_sents[0])
    grad_normed1 = dot_t(grad_z, w_z) + dot_t(grad_misc, w_misc) + dot_t(grad_xs, w_xs)
    grad_normed1 = fold(grad_normed1.reshape(n_hd, tok_count, d_model), "hd", 1, 0)
    grad_normed1 = after(grad_normed1, late_steps[0])
    _, norm1_pull = jax.vjp(rms_norm, x_in, norm1)
    grad_x_part, g_norm1 = norm1_pull(grad_normed1)
    grad_tokens_out = (grad_mid + grad_x_part).astype(low_type)

    reduced_in = jnp.concatenate([r_late, r_early], axis=1).astype(low_type)
    own_rows = reduced_in.shape[0] // n_hd
    halves = reduced_in.reshape(n_hd, own_rows, reduced_in.shape[1])
    got = swap(jnp.where(hd_high, halves[0], halves[1]), "hd", 1)
    mine = jnp.where(hd_high, halves[1], halves[0])
    group0 = jnp.where(hd_high, got, mine).astype(f32)
    group1 = jnp.where(hd_high, mine, got).astype(f32)

    def both(begin, width):
        return [group0[:, begin : begin + width], group1[:, begin : begin + width]]

    xs_at = x_part + qkv_cols
    bc0, bc1 = both(xs_at + x_part, bc_width)
    s_in = jnp.concatenate(
        both(0, x_part)
        + both(xs_at, x_part)
        + [bc0 + bc1]
        + both(x_part, q_part)
        + both(x_part + q_part, k_part)
        + both(x_part + q_part + k_part, k_part),
        axis=1,
    )
    s_dt = jnp.concatenate(both(xs_at + x_part + bc_width, heads), axis=1)

    def placed(values, width):
        full = jnp.zeros(values.shape[:-1] + (width,), f32)
        return lax.dynamic_update_slice_in_dim(
            full, values, hd_index * values.shape[-1], values.ndim - 1
        )

    g_conv_w = jnp.concatenate([placed(grad_taps[:, :x_part], d_ssm), grad_taps[:, x_part:]], axis=1)
    g_conv_b = jnp.concatenate([placed(grad_shift[:x_part], d_ssm), grad_shift[x_part:]], axis=0)
    small = [
        g_norm1,
        g_norm2,
        placed(g_gain, d_ssm),
        g_conv_w,
        g_conv_b,
        placed(grad_dt_shift, HM),
        placed(grad_log, HM),
        placed(g_skip, HM),
    ]
    flat = jnp.concatenate([s.reshape(-1) for s in small])
    length = flat.shape[0]
    flat = jnp.pad(flat, (0, -length % 1024)).reshape(-1, 128)
    flat = flat + swap(flat, "dp", 1)
    flat = flat + swap(flat, "hd", 1)
    for bit in low_first():
        flat = flat + swap(flat, "cp", bit)
    flat = flat.reshape(-1)
    sums = []
    begin = 0
    for s in small:
        sums.append(flat[begin : begin + s.size].reshape(s.shape))
        begin += s.size
    return (
        result_low[None],
        grad_tokens_out[None],
        s_in,
        s_dt,
        s_mo,
        s_ao,
        s_gu,
        s_down,
        *sums,
    )


def solution(mesh):
    weight = P(("dp", "cp"), None)
    grad = P(("dp", "cp", "hd"), None)
    seq = P("dp", ("cp", "hd"), None)
    in_specs = (seq, P("dp", None), seq) + (weight,) * 6 + (P(),) * 8
    out_specs = (seq, seq) + (grad,) * 6 + (P(),) * 8
    return jax.shard_map(
        per_device, mesh=mesh, in_specs=in_specs, out_specs=out_specs, check_vma=False
    )
```

```python
import math

import jax
import jax.numpy as jnp
from jax import lax
from jax.experimental import pallas as pl
from jax.experimental.pallas import tpu as pltpu
from jax.sharding import PartitionSpec as P

HM = 24
HDIM = 64
NST = 128
QH = 8
KVH = 2
FF = 2048

eps_norm = 1e-05
rope_base = 100000000000.0
masked = -1e30
highest = lax.Precision.HIGHEST
low_type = jnp.bfloat16
f32 = jnp.float32
chunk_len = 128
vmem_bytes = 56 * 1024 * 1024


def swap(value, axis, bit):
    count = lax.axis_size(axis)
    return lax.ppermute(value, axis, [(i, i ^ bit) for i in range(count)])


def shifted(value, axis, steps):
    count = lax.axis_size(axis)
    initial, last = (max(0, -steps), min(count, count - steps))
    return lax.ppermute(value, axis, [(source, source + steps) for source in range(initial, last)])


def has_bit(axis, bit):
    return (lax.axis_index(axis) & bit) != 0


def in_order(mine, other, high, dim, join):
    return join([jnp.where(high, other, mine), jnp.where(high, mine, other)], dim)


def gather_cp(value, gates=()):
    rows, cols = value.shape
    held = value[None]
    steps = []
    bit = lax.axis_size("cp") // 2
    while bit:
        ahead = bit.bit_length() - 1
        if ahead < len(gates) and gates[-1 - ahead] is not None:
            held = after(held, gates[-1 - ahead])
        other = swap(held, "cp", bit)
        held = in_order(held, other, has_bit("cp", bit), 1, jnp.stack).reshape(-1, rows, cols)
        steps.append(held)
        bit //= 2
    return held.reshape(-1, cols), steps


def gather_pair(value, axis, dim):
    return in_order(value, swap(value, axis, 1), has_bit(axis, 1), dim, jnp.concatenate)


def fold(value, axis, bit, dim, sents=None):
    high = has_bit(axis, bit)
    first = lax.index_in_dim(value, 0, dim, False)
    second = lax.index_in_dim(value, 1, dim, False)
    sent = jnp.where(high, first, second).astype(low_type)
    if sents is not None:
        sents.append(sent)
    got = swap(sent, axis, bit)
    return jnp.where(high, second, first).astype(f32) + got.astype(f32)


def fold_cp(value, order, gates=(None,) * 8):
    count = lax.axis_size("cp")
    bits = count.bit_length() - 1
    held = value.reshape((2,) * bits + value.shape[1:])
    left = [1 << (bits - 1 - d) for d in range(bits)]
    steps, sents = [], []
    for gate, bit in zip(gates, order):
        dim = left.index(bit)
        if gate is not None:
            held = after(held, gate)
        held = fold(held, "cp", bit, dim, sents)
        left.pop(dim)
        if left:
            held = held.astype(low_type)
        steps.append(held)
    return held, steps, sents


def low_first():
    return [1 << d for d in range(lax.axis_size("cp").bit_length() - 1)]


def low_last():
    bits = low_first()
    return bits[1:] + bits[:1]


def after(value, earlier):
    first = lax.slice(earlier, (0,) * earlier.ndim, (1,) * earlier.ndim).reshape(())
    return value + (first.astype(f32) * 0.0).astype(value.dtype)


def state_scan(log_decay, state, forward):
    heads = log_decay.shape[0]
    width = state.shape[1] // heads
    pre_log, pre_state = jnp.zeros_like(log_decay), jnp.zeros_like(state)
    count = lax.axis_size("cp")
    bit = 1
    gate = None

    def spread(values):
        return dot(jnp.exp(values)[None, :], expander(heads, width), highest)

    while bit < count:
        top = log_decay.astype(low_type)
        rest = (log_decay - top.astype(f32)).astype(low_type)
        tail = jnp.concatenate([top, rest, jnp.zeros((state.shape[1] - 2 * heads,), low_type)])
        tail = jnp.concatenate([tail[None], jnp.zeros((15, state.shape[1]), low_type)], axis=0)
        sent = jnp.concatenate([state.astype(low_type), tail], axis=0)
        if gate is not None:
            sent = after(sent, gate)
        gate = yield sent
        got = swap(sent, "cp", bit)
        got_state = got[:-16].astype(f32)
        got_log = got[-16, :heads].astype(f32) + got[-16, heads : 2 * heads].astype(f32)
        joins = has_bit("cp", bit) if forward else jnp.logical_not(has_bit("cp", bit))
        pre_state = jnp.where(joins, spread(pre_log) * got_state + pre_state, pre_state)
        pre_log = jnp.where(joins, pre_log + got_log, pre_log)
        state = jnp.where(
            joins, spread(log_decay) * got_state + state, spread(got_log) * state + got_state
        )
        log_decay = log_decay + got_log
        bit *= 2
    yield pre_state


def rms_norm(values, gain_vec):
    return (
        values * lax.rsqrt(jnp.mean(values * values, axis=-1, keepdims=True) + eps_norm) * gain_vec
    )


def expander(heads, width):
    column = jnp.arange(heads * width, dtype=jnp.int32)[None, :] // width
    return (column == jnp.arange(heads, dtype=jnp.int32)[:, None]).astype(f32)


def half_turner(width):
    column = jnp.arange(width, dtype=jnp.int32)
    half = HDIM // 2
    partner = jnp.where(column % HDIM < half, column + half, column - half)
    return (column[:, None] == partner[None, :]).astype(f32)


def causal_conv(padded, conv_taps, conv_shift):
    tap_count = conv_taps.shape[0]
    out_rows = padded.shape[0] - tap_count + 1
    summed = conv_shift[None, :]
    for tap_index in range(tap_count):
        summed = summed + conv_taps[tap_index][None, :] * padded[tap_index : tap_index + out_rows]
    return summed


def t_dot(left, right, precision=None):
    return lax.dot_general(
        left,
        right,
        (((0,), (0,)), ((), ())),
        preferred_element_type=f32,
        precision=precision,
    )


def dot_t(left, right, precision=None):
    return lax.dot_general(
        left,
        right,
        (((1,), (1,)), ((), ())),
        preferred_element_type=f32,
        precision=precision,
    )


def dot(left, right, precision=None):
    return jnp.dot(left, right, preferred_element_type=f32, precision=precision)


def left_half(shape):
    return lax.broadcasted_iota(jnp.int32, shape, 1) < HDIM


def both_heads(pair):
    left = left_half(pair.shape)
    pair = pair.astype(f32)
    return (
        jnp.where(left, pair, 0.0).astype(low_type),
        jnp.where(left, 0.0, pair).astype(low_type),
    )


def att_fwd_kernel(where_ref, q_ref, kk_ref, vv_ref, start_ref, *rest):
    out_ref, lse_ref, top_s, sum_s, acc_s = rest[-5:]
    span = q_ref.shape[0]
    place = where_ref[0]
    latest = where_ref[1]
    queries = both_heads(q_ref[...])
    top_s[...] = jnp.full(top_s.shape, masked, f32)
    sum_s[...] = jnp.zeros(sum_s.shape, f32)
    acc_s[...] = jnp.zeros(acc_s.shape, f32)

    def block(turn_index, _):
        j = place - turn_index
        base = pl.multiple_of(j * span, span)
        keys = kk_ref[pl.ds(base, span), :]
        values = vv_ref[pl.ds(base, span), :]

        def hide(scores):
            key_pos = base + lax.broadcasted_iota(jnp.int32, scores.shape, 1)
            row_pos = place * span + lax.broadcasted_iota(jnp.int32, scores.shape, 0)
            return jnp.where((key_pos <= row_pos) & (key_pos >= start_ref[...]), scores, masked)

        def work(shape_scores):
            for e in range(2):
                scores = shape_scores(dot_t(queries[e], keys))
                old_top = top_s[e]
                new_top = jnp.maximum(old_top, jnp.max(scores, axis=1, keepdims=True))
                weights = jnp.exp(scores - new_top)
                fall = jnp.exp(old_top - new_top)
                sum_s[e] = sum_s[e] * fall + jnp.sum(weights, axis=1, keepdims=True)
                acc_s[e] = acc_s[e] * fall + dot(weights.astype(low_type), values)
                top_s[e] = new_top

        needs = (j == place) | (latest > base)

        @pl.when(needs)
        def _():
            work(hide)

        @pl.when(jnp.logical_not(needs))
        def _():
            work(lambda scores: scores)

        return 0

    lax.fori_loop(0, place + 1, block, 0)
    outs = [acc_s[e] / sum_s[e] for e in range(2)]
    out_ref[...] = jnp.where(left_half(outs[0].shape), outs[0], outs[1])
    for e in range(2):
        lse_ref[e] = top_s[e] + jnp.log(sum_s[e])


def att_bwd_kernel(
    where_ref, q_ref, do_ref, kk_ref, vv_ref, start_ref, lse_ref, delta_ref, *rest
):
    dq_ref, dkv_ref, dq_s = rest[-3:]
    span = q_ref.shape[0]
    place = where_ref[0]
    latest = where_ref[1]
    queries = both_heads(q_ref[...])
    grads = both_heads(do_ref[...])
    dq_s[...] = jnp.zeros(dq_s.shape, f32)

    def block(j, _):
        base = pl.multiple_of(j * span, span)
        keys = kk_ref[pl.ds(base, span), :]
        values = vv_ref[pl.ds(base, span), :]

        def hide(scores):
            key_pos = base + lax.broadcasted_iota(jnp.int32, scores.shape, 0)
            row_pos = place * span + lax.broadcasted_iota(jnp.int32, scores.shape, 1)
            return jnp.where((key_pos <= row_pos) & (key_pos >= start_ref[...]), scores, masked)

        def work(shape_scores):
            dkk, dvv = [], []
            for e in range(2):
                scores = shape_scores(dot_t(keys, queries[e]))
                grad_probs = dot_t(values, grads[e])
                probs = jnp.exp(scores - lse_ref[e])
                grad_scores = (probs * (grad_probs - delta_ref[e])).astype(low_type)
                dq_s[e] += t_dot(grad_scores, keys)
                dkk.append(dot(grad_scores, queries[e]))
                dvv.append(dot(probs.astype(low_type), grads[e]))
            dkk, dvv = dkk[0] + dkk[1], dvv[0] + dvv[1]
            dkk = dkk + pltpu.roll(dkk, HDIM, 1)
            dvv = dvv + pltpu.roll(dvv, HDIM, 1)
            dkv_ref[pl.ds(base, span), :] = jnp.where(left_half(dkk.shape), dkk, dvv).astype(
                low_type
            )

        needs = (j == place) | (latest > base)

        @pl.when(needs)
        def _():
            work(hide)

        @pl.when(jnp.logical_not(needs))
        def _():
            work(lambda scores: scores)

        return 0

    lax.fori_loop(0, place + 1, block, 0)

    def clear(j, _):
        base = pl.multiple_of(j * span, span)
        dkv_ref[pl.ds(base, span), :] = jnp.zeros((span, 2 * HDIM), low_type)
        return 0

    lax.fori_loop(place + 1, dkv_ref.shape[0] // span, clear, 0)
    dq_ref[...] = jnp.where(left_half(dq_ref.shape), dq_s[0], dq_s[1])


def whole_spec(shape):
    return pl.BlockSpec(shape, lambda *_: (0,) * len(shape))


def any_specs(count):
    return [pl.BlockSpec(memory_space=pl.ANY)] * count


def att_cost(span, keys, matmuls):
    return pl.CostEstimate(
        flops=2 * matmuls * span * 2 * keys * 256,
        bytes_accessed=4 * keys * 128,
        transcendentals=span * 2 * keys,
    )


def attention_forward(where, queries, kk, vv, starts, deps):
    span, width = queries.shape
    return pl.pallas_call(
        att_fwd_kernel,
        in_specs=[
            pl.BlockSpec(memory_space=pltpu.SMEM),
            whole_spec((span, width)),
            whole_spec(kk.shape),
            whole_spec(vv.shape),
            whole_spec((span, 1)),
        ]
        + any_specs(len(deps)),
        out_specs=[whole_spec((span, width)), whole_spec((2, span, 1))],
        out_shape=[
            jax.ShapeDtypeStruct((span, width), f32),
            jax.ShapeDtypeStruct((2, span, 1), f32),
        ],
        grid=(1,),
        scratch_shapes=[
            pltpu.VMEM((2, span, 1), f32),
            pltpu.VMEM((2, span, 1), f32),
            pltpu.VMEM((2, span, width), f32),
        ],
        compiler_params=pltpu.CompilerParams(vmem_limit_bytes=vmem_bytes),
        cost_estimate=att_cost(span, kk.shape[0], 4),
        name="attention_forward",
    )(where, queries, kk, vv, starts.reshape(span, 1), *deps)


def attention_backward(where, queries, grads, kk, vv, starts, lse, delta, deps):
    span, width = queries.shape
    return pl.pallas_call(
        att_bwd_kernel,
        in_specs=[
            pl.BlockSpec(memory_space=pltpu.SMEM),
            whole_spec((span, width)),
            whole_spec((span, width)),
            whole_spec(kk.shape),
            whole_spec(vv.shape),
            whole_spec((1, span)),
            whole_spec((2, 1, span)),
            whole_spec((2, 1, span)),
        ]
        + any_specs(len(deps)),
        out_specs=[whole_spec((span, width)), whole_spec(kk.shape)],
        out_shape=[
            jax.ShapeDtypeStruct((span, width), f32),
            jax.ShapeDtypeStruct(kk.shape, low_type),
        ],
        grid=(1,),
        scratch_shapes=[
            pltpu.VMEM((2, span, width), f32),
        ],
        compiler_params=pltpu.CompilerParams(vmem_limit_bytes=vmem_bytes),
        cost_estimate=att_cost(span, kk.shape[0], 10),
        name="attention_backward",
    )(
        where,
        queries,
        grads,
        kk,
        vv,
        starts.reshape(1, span),
        lse.reshape(2, 1, span),
        delta.reshape(2, 1, span),
        *deps,
    )


def pair_blocks(pair):
    left = lax.broadcasted_iota(jnp.int32, pair.shape, 1) < HDIM
    return jnp.where(left, pair, 0.0), jnp.where(left, 0.0, pair)


def ssd_fwd_kernel(xd_ref, b_ref, c_ref, cs_ref, cst_ref, csx_ref, *rest):
    y_ref, before_ref, s_s = rest[-3:]

    @pl.when(pl.program_id(0) == 0)
    def _():
        s_s[...] = jnp.zeros(s_s.shape, f32)

    rows = xd_ref.shape[0]
    b, c = b_ref[...], c_ref[...]
    inner = dot_t(c, b, highest)
    lower = lax.broadcasted_iota(jnp.int32, (rows, rows), 0) >= lax.broadcasted_iota(
        jnp.int32, (rows, rows), 1
    )
    state = s_s[...]
    before_ref[...] = state
    csx = csx_ref[...]
    last = csx[rows - 1 :, :]
    carried = jnp.exp(csx) * dot(c, state, highest)

    def mixing(h):
        spread = jnp.where(lower, cs_ref[:, h : h + 1] - cst_ref[h : h + 1, :], masked)
        return jnp.exp(spread) * inner

    for pair in range(xd_ref.shape[1] // (2 * HDIM)):
        cols = slice(pair * 2 * HDIM, (pair + 1) * 2 * HDIM)
        mix = jnp.concatenate([mixing(2 * pair), mixing(2 * pair + 1)], axis=1)
        blocks = jnp.concatenate(pair_blocks(xd_ref[:, cols]), axis=0)
        y_ref[:, cols] = carried[:, cols] + dot(mix, blocks, highest)
    s_s[...] = jnp.exp(last) * state + t_dot(b, jnp.exp(last - csx) * xd_ref[...], highest)


def ssd_bwd_kernel(
    xd_ref,
    dy_ref,
    b_ref,
    c_ref,
    cs_ref,
    cst_ref,
    csx_ref,
    before_ref,
    *rest,
):
    dxd_ref, db_ref, dc_ref, ds_s = rest[-4:]

    @pl.when(pl.program_id(0) == 0)
    def _():
        ds_s[...] = jnp.zeros(ds_s.shape, f32)

    rows = xd_ref.shape[0]
    b, c = b_ref[...], c_ref[...]
    inner_t = dot_t(b, c, highest)
    row_id = lax.broadcasted_iota(jnp.int32, (rows, rows), 0)
    col_id = lax.broadcasted_iota(jnp.int32, (rows, rows), 1)
    csx = csx_ref[...]
    last = csx[rows - 1 :, :]
    grad_state = ds_s[...]
    end_fall = jnp.exp(last - csx)
    from_state = end_fall * dot(b, grad_state, highest)
    scaled_dy = jnp.exp(csx) * dy_ref[...]
    grad_inner = jnp.zeros((rows, rows), f32)

    def falls(h):
        spread = cs_ref[:, h : h + 1] - cst_ref[h : h + 1, :]
        return jnp.exp(jnp.where(row_id >= col_id, spread, masked))

    def falls_t(h):
        spread = cst_ref[h : h + 1, :] - cs_ref[:, h : h + 1]
        return jnp.exp(jnp.where(row_id <= col_id, spread, masked))

    for pair in range(xd_ref.shape[1] // (2 * HDIM)):
        cols = slice(pair * 2 * HDIM, (pair + 1) * 2 * HDIM)
        dy_left, dy_right = pair_blocks(dy_ref[:, cols])
        mix_t = jnp.concatenate(
            [falls_t(2 * pair) * inner_t, falls_t(2 * pair + 1) * inner_t], axis=1
        )
        blocks = jnp.concatenate([dy_left, dy_right], axis=0)
        dxd_ref[:, cols] = from_state[:, cols] + dot(mix_t, blocks, highest)
        xd = xd_ref[:, cols]
        grad_inner = grad_inner + falls(2 * pair) * dot_t(dy_left, xd, highest)
        grad_inner = grad_inner + falls(2 * pair + 1) * dot_t(dy_right, xd, highest)
    dc_ref[...] = dot(grad_inner, b, highest) + dot_t(scaled_dy, before_ref[...], highest)
    db_ref[...] = t_dot(grad_inner, c, highest) + dot_t(
        end_fall * xd_ref[...], grad_state, highest
    )
    ds_s[...] = jnp.exp(last) * grad_state + t_dot(c, scaled_dy, highest)


def ssd_forward(xd, b, c, cs, cst, csx, deps):
    length, width = xd.shape
    blocks = length // chunk_len
    heads = cs.shape[1]

    def rows(w):
        return pl.BlockSpec((chunk_len, w), lambda i: (i, 0))

    return pl.pallas_call(
        ssd_fwd_kernel,
        grid=(blocks,),
        in_specs=[
            rows(width),
            rows(NST),
            rows(NST),
            rows(heads),
            pl.BlockSpec((None, heads, chunk_len), lambda i: (i, 0, 0)),
            rows(width),
        ]
        + any_specs(len(deps)),
        out_specs=[rows(width), pl.BlockSpec((None, NST, width), lambda i: (i, 0, 0))],
        out_shape=[
            jax.ShapeDtypeStruct((length, width), f32),
            jax.ShapeDtypeStruct((blocks, NST, width), f32),
        ],
        scratch_shapes=[pltpu.VMEM((NST, width), f32)],
        compiler_params=pltpu.CompilerParams(vmem_limit_bytes=vmem_bytes),
        cost_estimate=pl.CostEstimate(
            flops=12 * 3 * length * width * NST, bytes_accessed=20 * length * width, transcendentals=0
        ),
        name="ssd_forward",
    )(xd, b, c, cs, cst, csx, *deps)


def ssd_backward(xd, dy, b, c, cs, cst, csx, before, deps):
    length, width = xd.shape
    blocks = length // chunk_len
    heads = cs.shape[1]

    def rows(w):
        return pl.BlockSpec((chunk_len, w), lambda i: (blocks - 1 - i, 0))

    def slabs(*shape):
        return pl.BlockSpec((None,) + shape, lambda i: (blocks - 1 - i, 0, 0))

    return pl.pallas_call(
        ssd_bwd_kernel,
        grid=(blocks,),
        in_specs=[
            rows(width),
            rows(width),
            rows(NST),
            rows(NST),
            rows(heads),
            slabs(heads, chunk_len),
            rows(width),
            slabs(NST, width),
        ]
        + any_specs(len(deps)),
        out_specs=[rows(width), rows(NST), rows(NST)],
        out_shape=[
            jax.ShapeDtypeStruct((length, width), f32),
            jax.ShapeDtypeStruct((length, NST), f32),
            jax.ShapeDtypeStruct((length, NST), f32),
        ],
        scratch_shapes=[pltpu.VMEM((NST, width), f32)],
        compiler_params=pltpu.CompilerParams(vmem_limit_bytes=vmem_bytes),
        cost_estimate=pl.CostEstimate(
            flops=12 * 8 * length * width * NST, bytes_accessed=24 * length * width, transcendentals=0
        ),
        name="ssd_backward",
    )(xd, dy, b, c, cs, cst, csx, before, *deps)


def per_device(
    tokens,
    doc_ids,
    cotangent,
    w_in,
    w_dt,
    w_mo,
    w_ao,
    w_gu,
    w_down,
    norm1,
    norm2,
    gate_norm,
    conv_w,
    conv_b,
    dt_bias,
    a_log,
    d_skip,
):
    n_hd = lax.axis_size("hd")
    n_cp = lax.axis_size("cp")
    hd_index = lax.axis_index("hd")
    cp_index = lax.axis_index("cp")
    dp_index = lax.axis_index("dp")
    hd_high = has_bit("hd", 1)
    x_in = tokens[0].astype(f32)
    tok_count, d_model = x_in.shape
    span = tok_count * n_hd
    d_ssm = HM * HDIM
    q_width = QH * HDIM
    k_width = KVH * HDIM
    x_part = d_ssm // n_hd
    heads = HM // n_hd
    q_part = q_width // n_hd
    k_part = k_width // n_hd
    bc_width = 2 * NST
    qkv_cols = q_part + 2 * k_part
    tap_count = conv_w.shape[0]
    score_scale = 1.0 / math.sqrt(HDIM)
    documents = doc_ids[0]

    def group(array, begin, width, dim=1):
        part = width // n_hd
        return lax.dynamic_slice_in_dim(array, begin + hd_index * part, part, dim)

    tokens_all = gather_pair(tokens[0], "hd", 0)

    normed1_all = rms_norm(tokens_all.astype(f32), norm1).astype(low_type)
    rim_tokens = shifted(tokens_all[span - 16 :], "cp", 1)
    normed1_rim = rms_norm(rim_tokens.astype(f32), norm1).astype(low_type)

    own_docs = lax.dynamic_slice_in_dim(documents, cp_index * span, span, 0)
    doc_begin = jnp.sum(documents[None, :] < own_docs[:, None], axis=1).astype(jnp.int32)
    where = jnp.stack([cp_index, jnp.max(doc_begin)]).astype(jnp.int32)

    positions = cp_index * span + jnp.arange(span, dtype=jnp.int32)
    half_width = HDIM // 2
    column = jnp.arange(qkv_cols, dtype=jnp.int32)
    turns = column < q_part + k_part
    power = (column % half_width).astype(f32)
    frequency = jnp.where(turns, rope_base ** (-2.0 * power / HDIM), 0.0)
    sign = jnp.where(column % HDIM < half_width, -1.0, 1.0)
    angles = positions.astype(f32)[:, None] * frequency[None, :]
    cosines = jnp.cos(angles)
    sines = jnp.sin(angles) * sign[None, :]
    cosines, sines = lax.optimization_barrier((cosines, sines))
    turner = half_turner(qkv_cols).astype(low_type)

    def half_turn(values):
        top = values.astype(low_type)
        return dot(top, turner) + dot((values - top.astype(f32)).astype(low_type), turner)

    q_start = 2 * d_ssm + bc_width
    k_start = q_start + q_width
    v_start = k_start + k_width
    dt_pad = 128 - heads
    shard_misc = jnp.concatenate(
        [
            group(w_in, q_start, q_width),
            group(w_in, k_start, k_width),
            group(w_in, v_start, k_width),
            w_in[:, 2 * d_ssm : q_start],
            group(w_dt, 0, HM),
            jnp.zeros((w_dt.shape[0], dt_pad), low_type),
        ],
        axis=1,
    )
    misc_cp, misc_steps = gather_cp(shard_misc, (where, normed1_all))
    w_misc = gather_pair(after(after(misc_cp, cosines), normed1_rim), "dp", 0)
    xs_cp, xs_steps = gather_cp(after(group(w_in, d_ssm, d_ssm), w_misc))
    out_rows = jnp.concatenate([w_mo, w_ao], axis=0)
    half_cols = d_model // 2
    handed = swap(out_rows[:, half_cols:], "dp", 1)
    holds = dp_index == hd_index
    out_half = jnp.where(holds, out_rows[:, :half_cols], handed)
    shard_rows, out_cols = w_in.shape[0], out_half.size // w_in.shape[0]
    z_out = jnp.concatenate(
        [group(w_in, 0, d_ssm), out_half.reshape(shard_rows, out_cols)], axis=1
    )
    z_out = lax.all_gather(after(z_out, misc_steps[1]), ("dp", "cp"), axis=0, tiled=True)
    w_z = z_out[:, :x_part]
    out_sides = z_out[:, x_part:].reshape(2, -1, half_cols)
    w_out = in_order(out_sides[0], out_sides[1], hd_high, 1, jnp.concatenate)
    w_xs = gather_pair(xs_cp, "dp", 0)

    proj = dot(normed1_all, w_misc)
    qkv = proj[:, :qkv_cols]
    qkv_low = (qkv * cosines + half_turn(qkv) * sines).astype(low_type)
    kv_all, _ = gather_cp(qkv_low[:, q_part:], (xs_steps[0], xs_steps[1]))
    q_scaled = qkv_low[:, :q_part] * jnp.asarray(score_scale, low_type)
    bc = proj[:, qkv_cols : qkv_cols + bc_width].astype(low_type)
    at = qkv_cols + bc_width
    dt_raw = proj[:, at : at + heads].astype(low_type).astype(f32)
    x_bc = jnp.concatenate([dot(normed1_all, w_xs).astype(low_type), bc], axis=1)
    w_bc = w_misc[:, qkv_cols : qkv_cols + bc_width]
    rim_rows = jnp.concatenate([dot(normed1_rim, w_xs), dot(normed1_rim, w_bc)], axis=1)
    rim_rows = rim_rows.astype(low_type)[16 - (tap_count - 1) :]

    padded = jnp.concatenate([rim_rows, x_bc], axis=0).astype(f32)
    conv_taps = jnp.concatenate([group(conv_w, 0, d_ssm), conv_w[:, d_ssm:]], axis=1)
    conv_shift = jnp.concatenate([group(conv_b, 0, d_ssm, 0), conv_b[d_ssm:]], axis=0)
    dt_shift = group(dt_bias, 0, HM, 0)
    log_scale = group(a_log, 0, HM, 0)
    skip_gain = group(d_skip, 0, HM, 0)
    expand = expander(heads, HDIM)

    def wide(values):
        return dot(values, expand, highest)

    def per_head(values):
        return dot_t(values, expand, highest)

    skip_x = wide(skip_gain[None, :])

    def prepare(padded_in, taps_in, shift_in, dt_in, dt_shift_in, log_in):
        activated = jax.nn.silu(causal_conv(padded_in, taps_in, shift_in))
        return (
            activated[:, :x_part],
            activated[:, x_part : x_part + NST],
            activated[:, x_part + NST :],
            jax.nn.softplus(dt_in + dt_shift_in),
            -jnp.exp(log_in),
        )

    (x_conv, b_conv, c_conv, dt_value, decay_rate), prep_pull = jax.vjp(
        prepare, padded, conv_taps, conv_shift, dt_raw, dt_shift, log_scale
    )
    blocks = span // chunk_len
    ones_low = jnp.tril(jnp.ones((chunk_len, chunk_len), f32))
    cs_block = jnp.einsum(
        "ts,bsh->bth",
        ones_low,
        (dt_value * decay_rate[None, :]).reshape(blocks, chunk_len, heads),
        precision=highest,
    )
    block_total = cs_block[:, -1]
    block_base = jnp.concatenate(
        [jnp.zeros((1, heads), f32), jnp.cumsum(block_total, axis=0)], axis=0
    )
    cs_dev = (cs_block + block_base[:-1, None, :]).reshape(span, heads)
    cs = cs_block.reshape(span, heads)
    cst = jnp.swapaxes(cs_block, 1, 2)
    log_dev = block_base[-1]
    csx = wide(cs)
    csx_dev = wide(cs_dev)
    dtx = wide(dt_value)
    xd = dtx * x_conv
    ending_xd = jnp.exp(csx_dev[-1:] - csx_dev) * xd
    state_local = t_dot(b_conv, ending_xd, highest)
    scan = state_scan(log_dev, state_local, True)
    in_sent = next(scan)
    y_own, before = ssd_forward(xd, b_conv, c_conv, cs, cst, csx, (in_sent,))
    in_sent = scan.send(y_own)

    kk = after(jnp.concatenate([kv_all[:, :HDIM], kv_all[:, :HDIM]], axis=1), w_xs)
    vv = jnp.concatenate([kv_all[:, HDIM:], kv_all[:, HDIM:]], axis=1)
    w_gate_up = after(after(w_gu, kk), xs_cp)
    w_gate_up = lax.all_gather(w_gate_up, ("dp", "cp"), axis=0, tiled=True)
    pairs = [slice(p * 2 * HDIM, (p + 1) * 2 * HDIM) for p in range(q_part // (2 * HDIM))]
    att_deps = [(z_out,), ()]
    att_outs, lses = [], []
    for cols, deps in zip(pairs, att_deps):
        att_out, lse = attention_forward(
            where, q_scaled[:, cols], kk, vv, doc_begin, deps + tuple(att_outs) + (in_sent,)
        )
        att_outs.append(att_out)
        lses.append(lse)
        in_sent = scan.send(att_out)
    for last_sent in scan:
        in_sent = last_sent
    state_in = in_sent
    att_f32 = jnp.concatenate(att_outs, axis=1)
    att_low = att_f32.astype(low_type)

    w_back = lax.all_gather(after(w_down, att_outs[0]), ("dp", "cp"), axis=0, tiled=True)


    mo_rows, ao_rows = w_mo.shape[0], w_ao.shape[0]
    w_out = w_out.reshape(n_cp, mo_rows + ao_rows, d_model)
    w_out = jnp.concatenate(
        [
            w_out[:, :mo_rows].reshape(n_cp * mo_rows, d_model),
            w_out[:, mo_rows:].reshape(n_cp * ao_rows, d_model),
        ],
        axis=0,
    )

    state_in = after(state_in, w_out)
    y_core = y_own + jnp.exp(csx_dev) * dot(c_conv, state_in, highest)
    y_low = (y_core + skip_x * x_conv).astype(low_type).astype(f32)

    gate_z = dot(normed1_all, w_z)
    gain = group(gate_norm, 0, d_ssm, 0)[None, :]
    sig_z = jax.nn.sigmoid(gate_z)
    silu_z = gate_z * sig_z
    mixed_y = y_low * silu_z
    squares = jnp.sum(mixed_y * mixed_y, axis=-1)
    squares = squares + swap(squares, "hd", 1)
    inv = lax.rsqrt(squares / d_ssm + eps_norm)[:, None]
    gated_low = (mixed_y * inv * gain).astype(low_type)
    branches = jnp.concatenate([gated_low, att_low], axis=1)
    partial = dot(branches, w_out).reshape(n_hd, tok_count, d_model)
    x_mid = x_in + fold(partial, "hd", 1, 0)

    normed2, norm2_pull = jax.vjp(rms_norm, x_mid, norm2)
    normed2_low = normed2.astype(low_type)
    gate_up = dot(normed2_low, w_gate_up)

    def swiglu(both_halves):
        return jax.nn.silu(both_halves[:, :FF]) * both_halves[:, FF:]

    hidden, swiglu_pull = jax.vjp(swiglu, gate_up)
    hidden_low = hidden.astype(low_type)

    grad_out_low = cotangent[0]
    grad_hidden = dot_t(grad_out_low, w_back)
    grad_gate_up = swiglu_pull(grad_hidden)[0].astype(low_type)
    grad_normed2 = dot_t(grad_gate_up, w_gate_up)
    grad_mid_part, g_norm2 = norm2_pull(grad_normed2)
    grad_mid = grad_out_low.astype(f32) + grad_mid_part
    grad_mid_low = grad_mid.astype(low_type)

    def rows_by_owner(grad):
        rows, cols = grad.shape
        return grad.reshape(2, n_cp, n_hd, rows // (2 * n_cp * n_hd), cols)

    def to_owner(grad):
        grad = grad.reshape((-1,) + grad.shape[-1:])
        return lax.psum_scatter(grad, ("cp", "hd"), scatter_dimension=0, tiled=True).astype(f32)

    def halves_by_core(values):
        part = values.shape[1] // 2
        kept = lax.dynamic_slice_in_dim(values, dp_index * part, part, 1)
        given = lax.dynamic_slice_in_dim(values, (1 - dp_index) * part, part, 1)
        return jnp.concatenate([kept, swap(given, "dp", 1)], axis=0)

    def cores(values):
        return jnp.concatenate([values, swap(values, "dp", 1)], axis=0)

    g_down = t_dot(halves_by_core(after(hidden_low, grad_mid_low)), cores(grad_out_low))
    g_down = g_down.astype(low_type)
    result_low = (x_mid + dot(after(hidden_low, grad_mid_low), w_back)).astype(low_type)
    grad_mid_all = in_order(
        after(after(grad_mid_low, g_down), result_low),
        swap(grad_mid_low, "hd", 1),
        hd_high,
        0,
        jnp.concatenate,
    )
    s_down = to_owner(after(g_down, grad_mid_all))
    g_gate_up = t_dot(
        halves_by_core(after(normed2_low, grad_mid_all)), cores(grad_gate_up)
    ).astype(low_type)
    s_gu = to_owner(g_gate_up)

    grad_branches = dot_t(grad_mid_all, w_out)
    grad_gated = grad_branches[:, :x_part]
    grad_att = grad_branches[:, x_part:].astype(low_type)
    delta = jnp.transpose(
        dot_t(grad_att.astype(f32) * att_f32, expander(q_part // HDIM, HDIM), highest)
    )

    gain_grad = grad_gated * gain
    along = jnp.sum(gain_grad * mixed_y, axis=-1)
    along = along + swap(along, "hd", 1)
    grad_mixed = inv * gain_grad - mixed_y * (inv * inv * inv * (along / d_ssm)[:, None])
    g_gain = jnp.sum(grad_gated * mixed_y * inv, axis=0)
    grad_y = (grad_mixed * silu_z).astype(low_type).astype(f32)
    grad_z = (grad_mixed * y_low * sig_z * (1.0 + gate_z * (1.0 - sig_z))).astype(low_type)

    scaled_dy = jnp.exp(csx_dev) * grad_y
    scan = state_scan(log_dev, t_dot(c_conv, scaled_dy, highest), False)
    future = next(scan)

    normed1_half = halves_by_core(normed1_all)

    def by_owner(grad):
        grad = t_dot(normed1_half, cores(grad)).astype(low_type)
        return grad.reshape(n_cp, d_model // (2 * n_cp), grad.shape[1])

    dqs, dkvs = [], []
    g_out = t_dot(branches, grad_mid_all).astype(low_type)
    g_out = jnp.concatenate(
        [
            g_out[:x_part].reshape(n_cp, n_hd, mo_rows // n_hd, d_model),
            g_out[x_part:].reshape(n_cp, n_hd, ao_rows // n_hd, d_model),
        ],
        axis=2,
    )
    g_out = fold(g_out, "dp", 1, 1).astype(low_type)
    bwd_deps = (g_gate_up, g_down, g_out)
    dxd_own, db_own, dc_own = ssd_backward(
        xd, grad_y, b_conv, c_conv, cs, cst, csx, before, (future,) + bwd_deps
    )
    future = scan.send(dxd_own)
    for p, cols in enumerate(pairs):
        dq, dkv = attention_backward(
            where,
            q_scaled[:, cols],
            grad_att[:, cols],
            kk,
            vv,
            doc_begin,
            lses[p],
            delta[2 * p : 2 * p + 2],
            bwd_deps + (future,),
        )
        dqs.append(dq)
        future = scan.send(dq)
        bwd_deps = ()
        dkvs.append(dkv.reshape(n_cp, span, 2 * HDIM))
    dkv_sum = dkvs[0].astype(f32)
    for dkv in dkvs[1:]:
        dkv_sum = dkv_sum + dkv.astype(f32)
    dkv_low = dkv_sum.astype(low_type)
    dkv, dkv_steps, _ = fold_cp(dkv_low, low_first())
    for last_sent in scan:
        future = last_sent
    out_grad, out_folds, _ = fold_cp(g_out, low_first(), (None, dxd_own, dqs[0]) + (None,) * 5)
    s_out = lax.ppermute(out_grad, ("dp", "hd"), [(0, 0), (1, 2), (2, 1), (3, 3)])
    s_mo, s_ao = s_out[: mo_rows // n_hd], s_out[mo_rows // n_hd :]


    dxd = dxd_own + jnp.exp(csx_dev[-1:] - csx_dev) * dot(b_conv, future, highest)
    db = db_own + dot_t(ending_xd, future, highest)
    dc = dc_own + dot_t(scaled_dy, state_in, highest)

    ddt_direct = per_head(x_conv * dxd)
    dcs = per_head(grad_y * y_core) - dt_value * ddt_direct
    state_end = jnp.exp(csx_dev[-1:]) * state_in + state_local
    end_term = per_head(jnp.sum(future * state_end, axis=0)[None, :])
    ones_up = jnp.triu(jnp.ones((span, span), f32))
    da = dot(ones_up, dcs, highest) + end_term
    g_skip = per_head(jnp.sum(grad_y * x_conv, axis=0)[None, :])[0]
    grad_padded, grad_taps, grad_shift, grad_dt, grad_dt_shift, grad_log = prep_pull(
        (
            dtx * dxd + skip_x * grad_y,
            after(db, dkv_steps[0]),
            dc,
            ddt_direct + decay_rate[None, :] * da,
            jnp.sum(da * dt_value, axis=0),
        )
    )
    rim_back = shifted(grad_padded[: tap_count - 1], "cp", -1)
    grad_conv_in = jnp.concatenate(
        [
            grad_padded[tap_count - 1 : span],
            grad_padded[span:] + rim_back,
        ],
        axis=0,
    ).astype(low_type)
    grad_xs = after(after(grad_conv_in, dkv_steps[1]), s_gu)[:, :x_part]
    grad_bc_dt = jnp.concatenate(
        [
            grad_conv_in[:, x_part:],
            grad_dt.astype(low_type),
            jnp.zeros((span, dt_pad), low_type),
        ],
        axis=1,
    )
    g_early = by_owner(jnp.concatenate([grad_xs, grad_bc_dt], axis=1))
    grad_qkv = jnp.concatenate([dq * score_scale for dq in dqs] + [after(dkv, g_early)], axis=1)
    grad_qkv = (grad_qkv * cosines - half_turn(grad_qkv) * sines).astype(low_type)
    g_late = by_owner(jnp.concatenate([grad_z, grad_qkv], axis=1))
    r_late, late_steps, late_sents = fold_cp(g_late, low_last())
    r_early, _, early_sents = fold_cp(g_early, low_first())
    grad_misc = jnp.concatenate([grad_qkv, grad_bc_dt], axis=1)

    grad_misc = after(after(grad_misc, early_sents[0]), late_sents[0])
    grad_normed1 = dot_t(grad_z, w_z) + dot_t(grad_misc, w_misc) + dot_t(grad_xs, w_xs)
    grad_normed1 = fold(grad_normed1.reshape(n_hd, tok_count, d_model), "hd", 1, 0)
    grad_normed1 = after(grad_normed1, late_steps[0])
    _, norm1_pull = jax.vjp(rms_norm, x_in, norm1)
    grad_x_part, g_norm1 = norm1_pull(grad_normed1)
    grad_tokens_out = (grad_mid + grad_x_part).astype(low_type)

    reduced_in = jnp.concatenate([r_late, r_early], axis=1).astype(low_type)
    own_rows = reduced_in.shape[0] // n_hd
    halves = reduced_in.reshape(n_hd, own_rows, reduced_in.shape[1])
    got = swap(jnp.where(hd_high, halves[0], halves[1]), "hd", 1)
    mine = jnp.where(hd_high, halves[1], halves[0])
    group0 = jnp.where(hd_high, got, mine).astype(f32)
    group1 = jnp.where(hd_high, mine, got).astype(f32)

    def both(begin, width):
        return [group0[:, begin : begin + width], group1[:, begin : begin + width]]

    xs_at = x_part + qkv_cols
    bc0, bc1 = both(xs_at + x_part, bc_width)
    s_in = jnp.concatenate(
        both(0, x_part)
        + both(xs_at, x_part)
        + [bc0 + bc1]
        + both(x_part, q_part)
        + both(x_part + q_part, k_part)
        + both(x_part + q_part + k_part, k_part),
        axis=1,
    )
    s_dt = jnp.concatenate(both(xs_at + x_part + bc_width, heads), axis=1)

    def placed(values, width):
        full = jnp.zeros(values.shape[:-1] + (width,), f32)
        return lax.dynamic_update_slice_in_dim(
            full, values, hd_index * values.shape[-1], values.ndim - 1
        )

    g_conv_w = jnp.concatenate([placed(grad_taps[:, :x_part], d_ssm), grad_taps[:, x_part:]], axis=1)
    g_conv_b = jnp.concatenate([placed(grad_shift[:x_part], d_ssm), grad_shift[x_part:]], axis=0)
    small = [
        g_norm1,
        g_norm2,
        placed(g_gain, d_ssm),
        g_conv_w,
        g_conv_b,
        placed(grad_dt_shift, HM),
        placed(grad_log, HM),
        placed(g_skip, HM),
    ]
    flat = jnp.concatenate([s.reshape(-1) for s in small])
    length = flat.shape[0]
    flat = jnp.pad(flat, (0, -length % 1024)).reshape(-1, 128)
    flat = flat + swap(flat, "dp", 1)
    flat = flat + swap(flat, "hd", 1)
    for bit in low_first():
        flat = flat + swap(flat, "cp", bit)
    flat = flat.reshape(-1)
    sums = []
    begin = 0
    for s in small:
        sums.append(flat[begin : begin + s.size].reshape(s.shape))
        begin += s.size
    return (
        result_low[None],
        grad_tokens_out[None],
        s_in,
        s_dt,
        s_mo,
        s_ao,
        s_gu,
        s_down,
        *sums,
    )


def solution(mesh):
    weight = P(("dp", "cp"), None)
    grad = P(("dp", "cp", "hd"), None)
    seq = P("dp", ("cp", "hd"), None)
    in_specs = (seq, P("dp", None), seq) + (weight,) * 6 + (P(),) * 8
    out_specs = (seq, seq) + (grad,) * 6 + (P(),) * 8
    return jax.shard_map(
        per_device, mesh=mesh, in_specs=in_specs, out_specs=out_specs, check_vma=False
    )
```

```python
import math

import jax
import jax.numpy as jnp
from jax import lax
from jax.experimental import pallas as pl
from jax.experimental.pallas import tpu as pltpu
from jax.sharding import PartitionSpec as P

HM = 24
HDIM = 64
NST = 128
QH = 8
KVH = 2
FF = 2048

eps_norm = 1e-05
rope_base = 100000000000.0
masked = -1e30
highest = lax.Precision.HIGHEST
fine = lax.Precision.HIGH
low_type = jnp.bfloat16
f32 = jnp.float32
chunk_len = 128
vmem_bytes = 56 * 1024 * 1024


def swap(value, axis, bit):
    count = lax.axis_size(axis)
    return lax.ppermute(value, axis, [(i, i ^ bit) for i in range(count)])


def shifted(value, axis, steps):
    count = lax.axis_size(axis)
    initial, last = (max(0, -steps), min(count, count - steps))
    return lax.ppermute(value, axis, [(source, source + steps) for source in range(initial, last)])


def has_bit(axis, bit):
    return (lax.axis_index(axis) & bit) != 0


def in_order(mine, other, high, dim, join):
    return join([jnp.where(high, other, mine), jnp.where(high, mine, other)], dim)


def gather_cp(value, gates=()):
    rows, cols = value.shape
    held = value[None]
    steps = []
    bit = lax.axis_size("cp") // 2
    while bit:
        ahead = bit.bit_length() - 1
        if ahead < len(gates) and gates[-1 - ahead] is not None:
            held = after(held, gates[-1 - ahead])
        other = swap(held, "cp", bit)
        held = in_order(held, other, has_bit("cp", bit), 1, jnp.stack).reshape(-1, rows, cols)
        steps.append(held)
        bit //= 2
    return held.reshape(-1, cols), steps


def gather_pair(value, axis, dim):
    return in_order(value, swap(value, axis, 1), has_bit(axis, 1), dim, jnp.concatenate)


def fold(value, axis, bit, dim, sents=None):
    high = has_bit(axis, bit)
    first = lax.index_in_dim(value, 0, dim, False)
    second = lax.index_in_dim(value, 1, dim, False)
    sent = jnp.where(high, first, second).astype(low_type)
    if sents is not None:
        sents.append(sent)
    got = swap(sent, axis, bit)
    return jnp.where(high, second, first).astype(f32) + got.astype(f32)


def fold_cp(value, order, gates=(None,) * 8):
    count = lax.axis_size("cp")
    bits = count.bit_length() - 1
    held = value.reshape((2,) * bits + value.shape[1:])
    left = [1 << (bits - 1 - d) for d in range(bits)]
    steps, sents = [], []
    for gate, bit in zip(gates, order):
        dim = left.index(bit)
        if gate is not None:
            held = after(held, gate)
        held = fold(held, "cp", bit, dim, sents)
        left.pop(dim)
        if left:
            held = held.astype(low_type)
        steps.append(held)
    return held, steps, sents


def low_first():
    return [1 << d for d in range(lax.axis_size("cp").bit_length() - 1)]


def low_last():
    bits = low_first()
    return bits[1:] + bits[:1]


def after(value, earlier):
    first = lax.slice(earlier, (0,) * earlier.ndim, (1,) * earlier.ndim).reshape(())
    return value + (first.astype(f32) * 0.0).astype(value.dtype)


def state_scan(log_decay, state, forward):
    heads = log_decay.shape[0]
    width = state.shape[1] // heads
    pre_log, pre_state = jnp.zeros_like(log_decay), jnp.zeros_like(state)
    count = lax.axis_size("cp")
    bit = 1
    gate = None

    def spread(values):
        return dot(jnp.exp(values)[None, :], expander(heads, width), highest)

    while bit < count:
        top = log_decay.astype(low_type)
        rest = (log_decay - top.astype(f32)).astype(low_type)
        tail = jnp.concatenate([top, rest, jnp.zeros((state.shape[1] - 2 * heads,), low_type)])
        tail = jnp.concatenate([tail[None], jnp.zeros((15, state.shape[1]), low_type)], axis=0)
        sent = jnp.concatenate([state.astype(low_type), tail], axis=0)
        if gate is not None:
            sent = after(sent, gate)
        gate = yield sent
        got = swap(sent, "cp", bit)
        got_state = got[:-16].astype(f32)
        got_log = got[-16, :heads].astype(f32) + got[-16, heads : 2 * heads].astype(f32)
        joins = has_bit("cp", bit) if forward else jnp.logical_not(has_bit("cp", bit))
        pre_state = jnp.where(joins, spread(pre_log) * got_state + pre_state, pre_state)
        pre_log = jnp.where(joins, pre_log + got_log, pre_log)
        state = jnp.where(
            joins, spread(log_decay) * got_state + state, spread(got_log) * state + got_state
        )
        log_decay = log_decay + got_log
        bit *= 2
    yield pre_state


def rms_norm(values, gain_vec):
    return (
        values * lax.rsqrt(jnp.mean(values * values, axis=-1, keepdims=True) + eps_norm) * gain_vec
    )


def expander(heads, width):
    column = jnp.arange(heads * width, dtype=jnp.int32)[None, :] // width
    return (column == jnp.arange(heads, dtype=jnp.int32)[:, None]).astype(f32)


def half_turner(width):
    column = jnp.arange(width, dtype=jnp.int32)
    half = HDIM // 2
    partner = jnp.where(column % HDIM < half, column + half, column - half)
    return (column[:, None] == partner[None, :]).astype(f32)


def causal_conv(padded, conv_taps, conv_shift):
    tap_count = conv_taps.shape[0]
    out_rows = padded.shape[0] - tap_count + 1
    summed = conv_shift[None, :]
    for tap_index in range(tap_count):
        summed = summed + conv_taps[tap_index][None, :] * padded[tap_index : tap_index + out_rows]
    return summed


def t_dot(left, right, precision=None):
    return lax.dot_general(
        left,
        right,
        (((0,), (0,)), ((), ())),
        preferred_element_type=f32,
        precision=precision,
    )


def dot_t(left, right, precision=None):
    return lax.dot_general(
        left,
        right,
        (((1,), (1,)), ((), ())),
        preferred_element_type=f32,
        precision=precision,
    )


def dot(left, right, precision=None):
    return jnp.dot(left, right, preferred_element_type=f32, precision=precision)


def left_half(shape):
    return lax.broadcasted_iota(jnp.int32, shape, 1) < HDIM


def both_heads(pair):
    left = left_half(pair.shape)
    pair = pair.astype(f32)
    return (
        jnp.where(left, pair, 0.0).astype(low_type),
        jnp.where(left, 0.0, pair).astype(low_type),
    )


def att_fwd_kernel(where_ref, q_ref, kk_ref, vv_ref, start_ref, *rest):
    out_ref, lse_ref, top_s, sum_s, acc_s = rest[-5:]
    span = q_ref.shape[0]
    place = where_ref[0]
    latest = where_ref[1]
    queries = both_heads(q_ref[...])
    top_s[...] = jnp.full(top_s.shape, masked, f32)
    sum_s[...] = jnp.zeros(sum_s.shape, f32)
    acc_s[...] = jnp.zeros(acc_s.shape, f32)

    def block(turn_index, _):
        j = place - turn_index
        base = pl.multiple_of(j * span, span)
        keys = kk_ref[pl.ds(base, span), :]
        values = vv_ref[pl.ds(base, span), :]

        def hide(scores):
            key_pos = base + lax.broadcasted_iota(jnp.int32, scores.shape, 1)
            row_pos = place * span + lax.broadcasted_iota(jnp.int32, scores.shape, 0)
            return jnp.where((key_pos <= row_pos) & (key_pos >= start_ref[...]), scores, masked)

        def work(shape_scores):
            for e in range(2):
                scores = shape_scores(dot_t(queries[e], keys))
                old_top = top_s[e]
                new_top = jnp.maximum(old_top, jnp.max(scores, axis=1, keepdims=True))
                weights = jnp.exp(scores - new_top)
                fall = jnp.exp(old_top - new_top)
                sum_s[e] = sum_s[e] * fall + jnp.sum(weights, axis=1, keepdims=True)
                acc_s[e] = acc_s[e] * fall + dot(weights.astype(low_type), values)
                top_s[e] = new_top

        needs = (j == place) | (latest > base)

        @pl.when(needs)
        def _():
            work(hide)

        @pl.when(jnp.logical_not(needs))
        def _():
            work(lambda scores: scores)

        return 0

    lax.fori_loop(0, place + 1, block, 0)
    outs = [acc_s[e] / sum_s[e] for e in range(2)]
    out_ref[...] = jnp.where(left_half(outs[0].shape), outs[0], outs[1])
    for e in range(2):
        lse_ref[e] = top_s[e] + jnp.log(sum_s[e])


def att_bwd_kernel(
    where_ref, q_ref, do_ref, kk_ref, vv_ref, start_ref, lse_ref, delta_ref, *rest
):
    dq_ref, dkv_ref, dq_s = rest[-3:]
    span = q_ref.shape[0]
    place = where_ref[0]
    latest = where_ref[1]
    queries = both_heads(q_ref[...])
    grads = both_heads(do_ref[...])
    dq_s[...] = jnp.zeros(dq_s.shape, f32)

    def block(j, _):
        base = pl.multiple_of(j * span, span)
        keys = kk_ref[pl.ds(base, span), :]
        values = vv_ref[pl.ds(base, span), :]

        def hide(scores):
            key_pos = base + lax.broadcasted_iota(jnp.int32, scores.shape, 0)
            row_pos = place * span + lax.broadcasted_iota(jnp.int32, scores.shape, 1)
            return jnp.where((key_pos <= row_pos) & (key_pos >= start_ref[...]), scores, masked)

        def work(shape_scores):
            dkk, dvv = [], []
            for e in range(2):
                scores = shape_scores(dot_t(keys, queries[e]))
                grad_probs = dot_t(values, grads[e])
                probs = jnp.exp(scores - lse_ref[e])
                grad_scores = (probs * (grad_probs - delta_ref[e])).astype(low_type)
                dq_s[e] += t_dot(grad_scores, keys)
                dkk.append(dot(grad_scores, queries[e]))
                dvv.append(dot(probs.astype(low_type), grads[e]))
            dkk, dvv = dkk[0] + dkk[1], dvv[0] + dvv[1]
            dkk = dkk + pltpu.roll(dkk, HDIM, 1)
            dvv = dvv + pltpu.roll(dvv, HDIM, 1)
            dkv_ref[pl.ds(base, span), :] = jnp.where(left_half(dkk.shape), dkk, dvv).astype(
                low_type
            )

        needs = (j == place) | (latest > base)

        @pl.when(needs)
        def _():
            work(hide)

        @pl.when(jnp.logical_not(needs))
        def _():
            work(lambda scores: scores)

        return 0

    lax.fori_loop(0, place + 1, block, 0)

    def clear(j, _):
        base = pl.multiple_of(j * span, span)
        dkv_ref[pl.ds(base, span), :] = jnp.zeros((span, 2 * HDIM), low_type)
        return 0

    lax.fori_loop(place + 1, dkv_ref.shape[0] // span, clear, 0)
    dq_ref[...] = jnp.where(left_half(dq_ref.shape), dq_s[0], dq_s[1])


def whole_spec(shape):
    return pl.BlockSpec(shape, lambda *_: (0,) * len(shape))


def any_specs(count):
    return [pl.BlockSpec(memory_space=pl.ANY)] * count


def att_cost(span, keys, matmuls):
    return pl.CostEstimate(
        flops=2 * matmuls * span * 2 * keys * 256,
        bytes_accessed=4 * keys * 128,
        transcendentals=span * 2 * keys,
    )


def attention_forward(where, queries, kk, vv, starts, deps):
    span, width = queries.shape
    return pl.pallas_call(
        att_fwd_kernel,
        in_specs=[
            pl.BlockSpec(memory_space=pltpu.SMEM),
            whole_spec((span, width)),
            whole_spec(kk.shape),
            whole_spec(vv.shape),
            whole_spec((span, 1)),
        ]
        + any_specs(len(deps)),
        out_specs=[whole_spec((span, width)), whole_spec((2, span, 1))],
        out_shape=[
            jax.ShapeDtypeStruct((span, width), f32),
            jax.ShapeDtypeStruct((2, span, 1), f32),
        ],
        grid=(1,),
        scratch_shapes=[
            pltpu.VMEM((2, span, 1), f32),
            pltpu.VMEM((2, span, 1), f32),
            pltpu.VMEM((2, span, width), f32),
        ],
        compiler_params=pltpu.CompilerParams(vmem_limit_bytes=vmem_bytes),
        cost_estimate=att_cost(span, kk.shape[0], 4),
        name="attention_forward",
    )(where, queries, kk, vv, starts.reshape(span, 1), *deps)


def attention_backward(where, queries, grads, kk, vv, starts, lse, delta, deps):
    span, width = queries.shape
    return pl.pallas_call(
        att_bwd_kernel,
        in_specs=[
            pl.BlockSpec(memory_space=pltpu.SMEM),
            whole_spec((span, width)),
            whole_spec((span, width)),
            whole_spec(kk.shape),
            whole_spec(vv.shape),
            whole_spec((1, span)),
            whole_spec((2, 1, span)),
            whole_spec((2, 1, span)),
        ]
        + any_specs(len(deps)),
        out_specs=[whole_spec((span, width)), whole_spec(kk.shape)],
        out_shape=[
            jax.ShapeDtypeStruct((span, width), f32),
            jax.ShapeDtypeStruct(kk.shape, low_type),
        ],
        grid=(1,),
        scratch_shapes=[
            pltpu.VMEM((2, span, width), f32),
        ],
        compiler_params=pltpu.CompilerParams(vmem_limit_bytes=vmem_bytes),
        cost_estimate=att_cost(span, kk.shape[0], 10),
        name="attention_backward",
    )(
        where,
        queries,
        grads,
        kk,
        vv,
        starts.reshape(1, span),
        lse.reshape(2, 1, span),
        delta.reshape(2, 1, span),
        *deps,
    )


def pair_blocks(pair):
    left = lax.broadcasted_iota(jnp.int32, pair.shape, 1) < HDIM
    return jnp.where(left, pair, 0.0), jnp.where(left, 0.0, pair)


def ssd_fwd_kernel(xd_ref, b_ref, c_ref, cs_ref, cst_ref, csx_ref, *rest):
    y_ref, before_ref, s_s = rest[-3:]

    @pl.when(pl.program_id(0) == 0)
    def _():
        s_s[...] = jnp.zeros(s_s.shape, f32)

    rows = xd_ref.shape[0]
    b, c = b_ref[...], c_ref[...]
    inner = dot_t(c, b, fine)
    lower = lax.broadcasted_iota(jnp.int32, (rows, rows), 0) >= lax.broadcasted_iota(
        jnp.int32, (rows, rows), 1
    )
    state = s_s[...]
    before_ref[...] = state
    csx = csx_ref[...]
    last = csx[rows - 1 :, :]
    carried = jnp.exp(csx) * dot(c, state, fine)

    def mixing(h):
        spread = jnp.where(lower, cs_ref[:, h : h + 1] - cst_ref[h : h + 1, :], masked)
        return jnp.exp(spread) * inner

    for pair in range(xd_ref.shape[1] // (2 * HDIM)):
        cols = slice(pair * 2 * HDIM, (pair + 1) * 2 * HDIM)
        mix = jnp.concatenate([mixing(2 * pair), mixing(2 * pair + 1)], axis=1)
        blocks = jnp.concatenate(pair_blocks(xd_ref[:, cols]), axis=0)
        y_ref[:, cols] = carried[:, cols] + dot(mix, blocks, fine)
    s_s[...] = jnp.exp(last) * state + t_dot(b, jnp.exp(last - csx) * xd_ref[...], fine)


def ssd_bwd_kernel(
    xd_ref,
    dy_ref,
    b_ref,
    c_ref,
    cs_ref,
    cst_ref,
    csx_ref,
    before_ref,
    *rest,
):
    dxd_ref, db_ref, dc_ref, ds_s = rest[-4:]

    @pl.when(pl.program_id(0) == 0)
    def _():
        ds_s[...] = jnp.zeros(ds_s.shape, f32)

    rows = xd_ref.shape[0]
    b, c = b_ref[...], c_ref[...]
    inner_t = dot_t(b, c, fine)
    row_id = lax.broadcasted_iota(jnp.int32, (rows, rows), 0)
    col_id = lax.broadcasted_iota(jnp.int32, (rows, rows), 1)
    csx = csx_ref[...]
    last = csx[rows - 1 :, :]
    grad_state = ds_s[...]
    end_fall = jnp.exp(last - csx)
    from_state = end_fall * dot(b, grad_state, fine)
    scaled_dy = jnp.exp(csx) * dy_ref[...]
    grad_inner = jnp.zeros((rows, rows), f32)

    def falls(h):
        spread = cs_ref[:, h : h + 1] - cst_ref[h : h + 1, :]
        return jnp.exp(jnp.where(row_id >= col_id, spread, masked))

    def falls_t(h):
        spread = cst_ref[h : h + 1, :] - cs_ref[:, h : h + 1]
        return jnp.exp(jnp.where(row_id <= col_id, spread, masked))

    for pair in range(xd_ref.shape[1] // (2 * HDIM)):
        cols = slice(pair * 2 * HDIM, (pair + 1) * 2 * HDIM)
        dy_left, dy_right = pair_blocks(dy_ref[:, cols])
        mix_t = jnp.concatenate(
            [falls_t(2 * pair) * inner_t, falls_t(2 * pair + 1) * inner_t], axis=1
        )
        blocks = jnp.concatenate([dy_left, dy_right], axis=0)
        dxd_ref[:, cols] = from_state[:, cols] + dot(mix_t, blocks, fine)
        xd = xd_ref[:, cols]
        grad_inner = grad_inner + falls(2 * pair) * dot_t(dy_left, xd, fine)
        grad_inner = grad_inner + falls(2 * pair + 1) * dot_t(dy_right, xd, fine)
    dc_ref[...] = dot(grad_inner, b, fine) + dot_t(scaled_dy, before_ref[...], fine)
    db_ref[...] = t_dot(grad_inner, c, fine) + dot_t(
        end_fall * xd_ref[...], grad_state, fine
    )
    ds_s[...] = jnp.exp(last) * grad_state + t_dot(c, scaled_dy, fine)


def ssd_forward(xd, b, c, cs, cst, csx, deps):
    length, width = xd.shape
    blocks = length // chunk_len
    heads = cs.shape[1]

    def rows(w):
        return pl.BlockSpec((chunk_len, w), lambda i: (i, 0))

    return pl.pallas_call(
        ssd_fwd_kernel,
        grid=(blocks,),
        in_specs=[
            rows(width),
            rows(NST),
            rows(NST),
            rows(heads),
            pl.BlockSpec((None, heads, chunk_len), lambda i: (i, 0, 0)),
            rows(width),
        ]
        + any_specs(len(deps)),
        out_specs=[rows(width), pl.BlockSpec((None, NST, width), lambda i: (i, 0, 0))],
        out_shape=[
            jax.ShapeDtypeStruct((length, width), f32),
            jax.ShapeDtypeStruct((blocks, NST, width), f32),
        ],
        scratch_shapes=[pltpu.VMEM((NST, width), f32)],
        compiler_params=pltpu.CompilerParams(vmem_limit_bytes=vmem_bytes),
        cost_estimate=pl.CostEstimate(
            flops=12 * 3 * length * width * NST, bytes_accessed=20 * length * width, transcendentals=0
        ),
        name="ssd_forward",
    )(xd, b, c, cs, cst, csx, *deps)


def ssd_backward(xd, dy, b, c, cs, cst, csx, before, deps):
    length, width = xd.shape
    blocks = length // chunk_len
    heads = cs.shape[1]

    def rows(w):
        return pl.BlockSpec((chunk_len, w), lambda i: (blocks - 1 - i, 0))

    def slabs(*shape):
        return pl.BlockSpec((None,) + shape, lambda i: (blocks - 1 - i, 0, 0))

    return pl.pallas_call(
        ssd_bwd_kernel,
        grid=(blocks,),
        in_specs=[
            rows(width),
            rows(width),
            rows(NST),
            rows(NST),
            rows(heads),
            slabs(heads, chunk_len),
            rows(width),
            slabs(NST, width),
        ]
        + any_specs(len(deps)),
        out_specs=[rows(width), rows(NST), rows(NST)],
        out_shape=[
            jax.ShapeDtypeStruct((length, width), f32),
            jax.ShapeDtypeStruct((length, NST), f32),
            jax.ShapeDtypeStruct((length, NST), f32),
        ],
        scratch_shapes=[pltpu.VMEM((NST, width), f32)],
        compiler_params=pltpu.CompilerParams(vmem_limit_bytes=vmem_bytes),
        cost_estimate=pl.CostEstimate(
            flops=12 * 8 * length * width * NST, bytes_accessed=24 * length * width, transcendentals=0
        ),
        name="ssd_backward",
    )(xd, dy, b, c, cs, cst, csx, before, *deps)


def per_device(
    tokens,
    doc_ids,
    cotangent,
    w_in,
    w_dt,
    w_mo,
    w_ao,
    w_gu,
    w_down,
    norm1,
    norm2,
    gate_norm,
    conv_w,
    conv_b,
    dt_bias,
    a_log,
    d_skip,
):
    n_hd = lax.axis_size("hd")
    n_cp = lax.axis_size("cp")
    hd_index = lax.axis_index("hd")
    cp_index = lax.axis_index("cp")
    dp_index = lax.axis_index("dp")
    hd_high = has_bit("hd", 1)
    x_in = tokens[0].astype(f32)
    tok_count, d_model = x_in.shape
    span = tok_count * n_hd
    d_ssm = HM * HDIM
    q_width = QH * HDIM
    k_width = KVH * HDIM
    x_part = d_ssm // n_hd
    heads = HM // n_hd
    q_part = q_width // n_hd
    k_part = k_width // n_hd
    bc_width = 2 * NST
    qkv_cols = q_part + 2 * k_part
    tap_count = conv_w.shape[0]
    score_scale = 1.0 / math.sqrt(HDIM)
    documents = doc_ids[0]

    def group(array, begin, width, dim=1):
        part = width // n_hd
        return lax.dynamic_slice_in_dim(array, begin + hd_index * part, part, dim)

    tokens_all = gather_pair(tokens[0], "hd", 0)

    normed1_all = rms_norm(tokens_all.astype(f32), norm1).astype(low_type)
    rim_tokens = shifted(tokens_all[span - 16 :], "cp", 1)
    normed1_rim = rms_norm(rim_tokens.astype(f32), norm1).astype(low_type)

    own_docs = lax.dynamic_slice_in_dim(documents, cp_index * span, span, 0)
    doc_begin = jnp.sum(documents[None, :] < own_docs[:, None], axis=1).astype(jnp.int32)
    where = jnp.stack([cp_index, jnp.max(doc_begin)]).astype(jnp.int32)

    positions = cp_index * span + jnp.arange(span, dtype=jnp.int32)
    half_width = HDIM // 2
    column = jnp.arange(qkv_cols, dtype=jnp.int32)
    turns = column < q_part + k_part
    power = (column % half_width).astype(f32)
    frequency = jnp.where(turns, rope_base ** (-2.0 * power / HDIM), 0.0)
    sign = jnp.where(column % HDIM < half_width, -1.0, 1.0)
    angles = positions.astype(f32)[:, None] * frequency[None, :]
    cosines = jnp.cos(angles)
    sines = jnp.sin(angles) * sign[None, :]
    cosines, sines = lax.optimization_barrier((cosines, sines))
    turner = half_turner(qkv_cols).astype(low_type)

    def half_turn(values):
        top = values.astype(low_type)
        return dot(top, turner) + dot((values - top.astype(f32)).astype(low_type), turner)

    q_start = 2 * d_ssm + bc_width
    k_start = q_start + q_width
    v_start = k_start + k_width
    dt_pad = 128 - heads
    shard_misc = jnp.concatenate(
        [
            group(w_in, q_start, q_width),
            group(w_in, k_start, k_width),
            group(w_in, v_start, k_width),
            w_in[:, 2 * d_ssm : q_start],
            group(w_dt, 0, HM),
            jnp.zeros((w_dt.shape[0], dt_pad), low_type),
        ],
        axis=1,
    )
    misc_cp, misc_steps = gather_cp(shard_misc, (where, normed1_all))
    w_misc = gather_pair(after(after(misc_cp, cosines), normed1_rim), "dp", 0)
    xs_cp, xs_steps = gather_cp(after(group(w_in, d_ssm, d_ssm), w_misc))
    out_rows = jnp.concatenate([w_mo, w_ao], axis=0)
    half_cols = d_model // 2
    handed = swap(out_rows[:, half_cols:], "dp", 1)
    holds = dp_index == hd_index
    out_half = jnp.where(holds, out_rows[:, :half_cols], handed)
    shard_rows, out_cols = w_in.shape[0], out_half.size // w_in.shape[0]
    z_out = jnp.concatenate(
        [group(w_in, 0, d_ssm), out_half.reshape(shard_rows, out_cols)], axis=1
    )
    z_out = lax.all_gather(after(z_out, misc_steps[1]), ("dp", "cp"), axis=0, tiled=True)
    w_z = z_out[:, :x_part]
    mo_rows, ao_rows = w_mo.shape[0], w_ao.shape[0]
    out_sides = z_out[:, x_part:].reshape(2, n_cp, mo_rows + ao_rows, half_cols)
    out_left = lax.dynamic_index_in_dim(out_sides, hd_index, 0, False)
    out_right = lax.dynamic_index_in_dim(out_sides, 1 - hd_index, 0, False)

    def out_part(begin, rows):
        sides = [a[:, begin : begin + rows].reshape(-1, half_cols) for a in (out_left, out_right)]
        return jnp.concatenate(sides, axis=1)

    w_out = jnp.concatenate([out_part(0, mo_rows), out_part(mo_rows, ao_rows)], axis=0)
    w_xs = gather_pair(xs_cp, "dp", 0)

    proj = dot(normed1_all, w_misc)
    qkv = proj[:, :qkv_cols]
    qkv_low = (qkv * cosines + half_turn(qkv) * sines).astype(low_type)
    kv_all, _ = gather_cp(qkv_low[:, q_part:], (xs_steps[0], xs_steps[1]))
    q_scaled = qkv_low[:, :q_part] * jnp.asarray(score_scale, low_type)
    bc = proj[:, qkv_cols : qkv_cols + bc_width].astype(low_type)
    at = qkv_cols + bc_width
    dt_raw = proj[:, at : at + heads].astype(low_type).astype(f32)
    x_bc = jnp.concatenate([dot(normed1_all, w_xs).astype(low_type), bc], axis=1)
    w_bc = w_misc[:, qkv_cols : qkv_cols + bc_width]
    rim_rows = jnp.concatenate([dot(normed1_rim, w_xs), dot(normed1_rim, w_bc)], axis=1)
    rim_rows = rim_rows.astype(low_type)[16 - (tap_count - 1) :]

    padded = jnp.concatenate([rim_rows, x_bc], axis=0).astype(f32)
    conv_taps = jnp.concatenate([group(conv_w, 0, d_ssm), conv_w[:, d_ssm:]], axis=1)
    conv_shift = jnp.concatenate([group(conv_b, 0, d_ssm, 0), conv_b[d_ssm:]], axis=0)
    dt_shift = group(dt_bias, 0, HM, 0)
    log_scale = group(a_log, 0, HM, 0)
    skip_gain = group(d_skip, 0, HM, 0)
    expand = expander(heads, HDIM)

    def wide(values):
        return dot(values, expand, highest)

    def per_head(values):
        return dot_t(values, expand, highest)

    skip_x = wide(skip_gain[None, :])

    def prepare(padded_in, taps_in, shift_in, dt_in, dt_shift_in, log_in):
        activated = jax.nn.silu(causal_conv(padded_in, taps_in, shift_in))
        return (
            activated[:, :x_part],
            activated[:, x_part : x_part + NST],
            activated[:, x_part + NST :],
            jax.nn.softplus(dt_in + dt_shift_in),
            -jnp.exp(log_in),
        )

    (x_conv, b_conv, c_conv, dt_value, decay_rate), prep_pull = jax.vjp(
        prepare, padded, conv_taps, conv_shift, dt_raw, dt_shift, log_scale
    )
    blocks = span // chunk_len
    ones_low = jnp.tril(jnp.ones((chunk_len, chunk_len), f32))
    cs_block = jnp.einsum(
        "ts,bsh->bth",
        ones_low,
        (dt_value * decay_rate[None, :]).reshape(blocks, chunk_len, heads),
        precision=highest,
    )
    block_total = cs_block[:, -1]
    block_base = jnp.concatenate(
        [jnp.zeros((1, heads), f32), jnp.cumsum(block_total, axis=0)], axis=0
    )
    cs_dev = (cs_block + block_base[:-1, None, :]).reshape(span, heads)
    cs = cs_block.reshape(span, heads)
    cst = jnp.swapaxes(cs_block, 1, 2)
    log_dev = block_base[-1]
    csx = wide(cs)
    csx_dev = wide(cs_dev)
    dtx = wide(dt_value)
    xd = dtx * x_conv
    ending_xd = jnp.exp(csx_dev[-1:] - csx_dev) * xd
    state_local = t_dot(b_conv, ending_xd, fine)
    scan = state_scan(log_dev, state_local, True)
    in_sent = next(scan)
    y_own, before = ssd_forward(xd, b_conv, c_conv, cs, cst, csx, (in_sent,))
    in_sent = scan.send(y_own)

    kk = after(jnp.concatenate([kv_all[:, :HDIM], kv_all[:, :HDIM]], axis=1), w_xs)
    vv = jnp.concatenate([kv_all[:, HDIM:], kv_all[:, HDIM:]], axis=1)
    w_gate_up = after(after(w_gu, kk), xs_cp)
    w_gate_up = lax.all_gather(w_gate_up, ("dp", "cp"), axis=0, tiled=True)
    pairs = [slice(p * 2 * HDIM, (p + 1) * 2 * HDIM) for p in range(q_part // (2 * HDIM))]
    att_deps = [(z_out,), ()]
    att_outs, lses = [], []
    for cols, deps in zip(pairs, att_deps):
        att_out, lse = attention_forward(
            where, q_scaled[:, cols], kk, vv, doc_begin, deps + tuple(att_outs) + (in_sent,)
        )
        att_outs.append(att_out)
        lses.append(lse)
        in_sent = scan.send(att_out)
    for last_sent in scan:
        in_sent = last_sent
    state_in = in_sent
    att_f32 = jnp.concatenate(att_outs, axis=1)
    att_low = att_f32.astype(low_type)

    w_back = lax.all_gather(after(w_down, att_outs[0]), ("dp", "cp"), axis=0, tiled=True)


    state_in = after(state_in, w_out)
    y_core = y_own + jnp.exp(csx_dev) * dot(c_conv, state_in, fine)
    y_low = (y_core + skip_x * x_conv).astype(low_type).astype(f32)

    gate_z = dot(normed1_all, w_z)
    gain = group(gate_norm, 0, d_ssm, 0)[None, :]
    sig_z = jax.nn.sigmoid(gate_z)
    silu_z = gate_z * sig_z
    mixed_y = y_low * silu_z
    squares = jnp.sum(mixed_y * mixed_y, axis=-1)
    squares = squares + swap(squares, "hd", 1)
    inv = lax.rsqrt(squares / d_ssm + eps_norm)[:, None]
    gated_low = (mixed_y * inv * gain).astype(low_type)
    branches = jnp.concatenate([gated_low, att_low], axis=1)
    partial = dot(branches, w_out).reshape(n_hd, tok_count, d_model)
    x_mid = x_in + fold(partial, "hd", 1, 0)

    normed2, norm2_pull = jax.vjp(rms_norm, x_mid, norm2)
    normed2_low = normed2.astype(low_type)
    gate_up = dot(normed2_low, w_gate_up)

    def swiglu(both_halves):
        return jax.nn.silu(both_halves[:, :FF]) * both_halves[:, FF:]

    hidden, swiglu_pull = jax.vjp(swiglu, gate_up)
    hidden_low = hidden.astype(low_type)

    grad_out_low = cotangent[0]
    grad_hidden = dot_t(grad_out_low, w_back)
    grad_gate_up = swiglu_pull(grad_hidden)[0].astype(low_type)
    grad_normed2 = dot_t(grad_gate_up, w_gate_up)
    grad_mid_part, g_norm2 = norm2_pull(grad_normed2)
    grad_mid = grad_out_low.astype(f32) + grad_mid_part
    grad_mid_low = grad_mid.astype(low_type)

    def rows_by_owner(grad):
        rows, cols = grad.shape
        return grad.reshape(2, n_cp, n_hd, rows // (2 * n_cp * n_hd), cols)

    def to_owner(grad):
        grad = grad.reshape((-1,) + grad.shape[-1:])
        return lax.psum_scatter(grad, ("cp", "hd"), scatter_dimension=0, tiled=True).astype(f32)

    def halves_by_core(values):
        part = values.shape[1] // 2
        kept = lax.dynamic_slice_in_dim(values, dp_index * part, part, 1)
        given = lax.dynamic_slice_in_dim(values, (1 - dp_index) * part, part, 1)
        return jnp.concatenate([kept, swap(given, "dp", 1)], axis=0)

    def cores(values):
        return jnp.concatenate([values, swap(values, "dp", 1)], axis=0)

    g_down = t_dot(halves_by_core(after(hidden_low, grad_mid_low)), cores(grad_out_low))
    g_down = g_down.astype(low_type)
    result_low = (x_mid + dot(after(hidden_low, grad_mid_low), w_back)).astype(low_type)
    grad_mid_all = in_order(
        after(after(grad_mid_low, g_down), result_low),
        swap(grad_mid_low, "hd", 1),
        hd_high,
        0,
        jnp.concatenate,
    )
    s_down = to_owner(after(g_down, grad_mid_all))
    g_gate_up = t_dot(
        halves_by_core(after(normed2_low, grad_mid_all)), cores(grad_gate_up)
    ).astype(low_type)
    s_gu = to_owner(g_gate_up)

    grad_branches = dot_t(grad_mid_all, w_out)
    grad_gated = grad_branches[:, :x_part]
    grad_att = grad_branches[:, x_part:].astype(low_type)
    delta = jnp.transpose(
        dot_t(grad_att.astype(f32) * att_f32, expander(q_part // HDIM, HDIM), highest)
    )

    gain_grad = grad_gated * gain
    along = jnp.sum(gain_grad * mixed_y, axis=-1)
    along = along + swap(along, "hd", 1)
    grad_mixed = inv * gain_grad - mixed_y * (inv * inv * inv * (along / d_ssm)[:, None])
    g_gain = jnp.sum(grad_gated * mixed_y * inv, axis=0)
    grad_y = (grad_mixed * silu_z).astype(low_type).astype(f32)
    grad_z = (grad_mixed * y_low * sig_z * (1.0 + gate_z * (1.0 - sig_z))).astype(low_type)

    scaled_dy = jnp.exp(csx_dev) * grad_y
    scan = state_scan(log_dev, t_dot(c_conv, scaled_dy, fine), False)
    future = next(scan)

    normed1_half = halves_by_core(normed1_all)

    def by_owner(grad):
        grad = t_dot(normed1_half, cores(grad)).astype(low_type)
        return grad.reshape(n_cp, d_model // (2 * n_cp), grad.shape[1])

    dqs, dkvs = [], []
    g_out = t_dot(branches, grad_mid_all).astype(low_type)
    g_out = jnp.concatenate(
        [
            g_out[:x_part].reshape(n_cp, n_hd, mo_rows // n_hd, d_model),
            g_out[x_part:].reshape(n_cp, n_hd, ao_rows // n_hd, d_model),
        ],
        axis=2,
    )
    g_out = fold(g_out, "dp", 1, 1).astype(low_type)
    bwd_deps = (g_gate_up, g_down, g_out)
    dxd_own, db_own, dc_own = ssd_backward(
        xd, grad_y, b_conv, c_conv, cs, cst, csx, before, (future,) + bwd_deps
    )
    future = scan.send(dxd_own)
    for p, cols in enumerate(pairs):
        dq, dkv = attention_backward(
            where,
            q_scaled[:, cols],
            grad_att[:, cols],
            kk,
            vv,
            doc_begin,
            lses[p],
            delta[2 * p : 2 * p + 2],
            bwd_deps + (future,),
        )
        dqs.append(dq)
        future = scan.send(dq)
        bwd_deps = ()
        dkvs.append(dkv.reshape(n_cp, span, 2 * HDIM))
    dkv_sum = dkvs[0].astype(f32)
    for dkv in dkvs[1:]:
        dkv_sum = dkv_sum + dkv.astype(f32)
    dkv_low = dkv_sum.astype(low_type)
    dkv, dkv_steps, _ = fold_cp(dkv_low, low_first())
    for last_sent in scan:
        future = last_sent
    out_grad, out_folds, _ = fold_cp(g_out, low_first(), (None, dxd_own, dqs[0]) + (None,) * 5)
    s_out = lax.ppermute(out_grad, ("dp", "hd"), [(0, 0), (1, 2), (2, 1), (3, 3)])
    s_mo, s_ao = s_out[: mo_rows // n_hd], s_out[mo_rows // n_hd :]


    dxd = dxd_own + jnp.exp(csx_dev[-1:] - csx_dev) * dot(b_conv, future, fine)
    db = db_own + dot_t(ending_xd, future, fine)
    dc = dc_own + dot_t(scaled_dy, state_in, fine)

    ddt_direct = per_head(x_conv * dxd)
    dcs = per_head(grad_y * y_core) - dt_value * ddt_direct
    state_end = jnp.exp(csx_dev[-1:]) * state_in + state_local
    end_term = per_head(jnp.sum(future * state_end, axis=0)[None, :])
    ones_up = jnp.triu(jnp.ones((span, span), f32))
    da = dot(ones_up, dcs, highest) + end_term
    g_skip = per_head(jnp.sum(grad_y * x_conv, axis=0)[None, :])[0]
    grad_padded, grad_taps, grad_shift, grad_dt, grad_dt_shift, grad_log = prep_pull(
        (
            dtx * dxd + skip_x * grad_y,
            after(db, dkv_steps[0]),
            dc,
            ddt_direct + decay_rate[None, :] * da,
            jnp.sum(da * dt_value, axis=0),
        )
    )
    rim_back = shifted(grad_padded[: tap_count - 1], "cp", -1)
    grad_conv_in = jnp.concatenate(
        [
            grad_padded[tap_count - 1 : span],
            grad_padded[span:] + rim_back,
        ],
        axis=0,
    ).astype(low_type)
    grad_xs = after(after(grad_conv_in, dkv_steps[1]), s_gu)[:, :x_part]
    grad_bc_dt = jnp.concatenate(
        [
            grad_conv_in[:, x_part:],
            grad_dt.astype(low_type),
            jnp.zeros((span, dt_pad), low_type),
        ],
        axis=1,
    )
    g_early = by_owner(jnp.concatenate([grad_xs, grad_bc_dt], axis=1))
    grad_qkv = jnp.concatenate([dq * score_scale for dq in dqs] + [after(dkv, g_early)], axis=1)
    grad_qkv = (grad_qkv * cosines - half_turn(grad_qkv) * sines).astype(low_type)
    g_late = by_owner(jnp.concatenate([grad_z, grad_qkv], axis=1))
    r_late, late_steps, late_sents = fold_cp(g_late, low_last())
    r_early, _, early_sents = fold_cp(g_early, low_first())
    grad_misc = jnp.concatenate([grad_qkv, grad_bc_dt], axis=1)

    grad_misc = after(after(grad_misc, early_sents[0]), late_sents[0])
    grad_normed1 = dot_t(grad_z, w_z) + dot_t(grad_misc, w_misc) + dot_t(grad_xs, w_xs)
    grad_normed1 = fold(grad_normed1.reshape(n_hd, tok_count, d_model), "hd", 1, 0)
    grad_normed1 = after(grad_normed1, late_steps[0])
    _, norm1_pull = jax.vjp(rms_norm, x_in, norm1)
    grad_x_part, g_norm1 = norm1_pull(grad_normed1)
    grad_tokens_out = (grad_mid + grad_x_part).astype(low_type)

    reduced_in = jnp.concatenate([r_late, r_early], axis=1).astype(low_type)
    own_rows = reduced_in.shape[0] // n_hd
    halves = reduced_in.reshape(n_hd, own_rows, reduced_in.shape[1])
    got = swap(jnp.where(hd_high, halves[0], halves[1]), "hd", 1)
    mine = jnp.where(hd_high, halves[1], halves[0])
    group0 = jnp.where(hd_high, got, mine).astype(f32)
    group1 = jnp.where(hd_high, mine, got).astype(f32)

    def both(begin, width):
        return [group0[:, begin : begin + width], group1[:, begin : begin + width]]

    xs_at = x_part + qkv_cols
    bc0, bc1 = both(xs_at + x_part, bc_width)
    s_in = jnp.concatenate(
        both(0, x_part)
        + both(xs_at, x_part)
        + [bc0 + bc1]
        + both(x_part, q_part)
        + both(x_part + q_part, k_part)
        + both(x_part + q_part + k_part, k_part),
        axis=1,
    )
    s_dt = jnp.concatenate(both(xs_at + x_part + bc_width, heads), axis=1)

    def placed(values, width):
        full = jnp.zeros(values.shape[:-1] + (width,), f32)
        return lax.dynamic_update_slice_in_dim(
            full, values, hd_index * values.shape[-1], values.ndim - 1
        )

    g_conv_w = jnp.concatenate([placed(grad_taps[:, :x_part], d_ssm), grad_taps[:, x_part:]], axis=1)
    g_conv_b = jnp.concatenate([placed(grad_shift[:x_part], d_ssm), grad_shift[x_part:]], axis=0)
    small = [
        g_norm1,
        g_norm2,
        placed(g_gain, d_ssm),
        g_conv_w,
        g_conv_b,
        placed(grad_dt_shift, HM),
        placed(grad_log, HM),
        placed(g_skip, HM),
    ]
    flat = jnp.concatenate([s.reshape(-1) for s in small])
    length = flat.shape[0]
    flat = jnp.pad(flat, (0, -length % 1024)).reshape(-1, 128)
    flat = flat + swap(flat, "dp", 1)
    flat = flat + swap(flat, "hd", 1)
    for bit in low_first():
        flat = flat + swap(flat, "cp", bit)
    flat = flat.reshape(-1)
    sums = []
    begin = 0
    for s in small:
        sums.append(flat[begin : begin + s.size].reshape(s.shape))
        begin += s.size
    return (
        result_low[None],
        grad_tokens_out[None],
        s_in,
        s_dt,
        s_mo,
        s_ao,
        s_gu,
        s_down,
        *sums,
    )


def solution(mesh):
    weight = P(("dp", "cp"), None)
    grad = P(("dp", "cp", "hd"), None)
    seq = P("dp", ("cp", "hd"), None)
    in_specs = (seq, P("dp", None), seq) + (weight,) * 6 + (P(),) * 8
    out_specs = (seq, seq) + (grad,) * 6 + (P(),) * 8
    return jax.shard_map(
        per_device, mesh=mesh, in_specs=in_specs, out_specs=out_specs, check_vma=False
    )
```
